512 devices in a mesh: cam: 8 (over x, y_hi), slab: 64 (over y_lo, z, core).
Axes of the slice: x: 4, y: 8 (y_hi: 2, y_lo: 4; y = y_hi * 4 + y_lo), z: 8, core: 2. Of those that a mesh axis runs over, the one named last changes fastest.
Arguments:
- frames_in: bfloat16 [8, 16384, 1152], P('cam', 'slab'), may hold values from -6 to 6
- cam_embed: float32 [8, 1152], replicated, may hold values from -6 to 6
- norm_gain: float32 [1152], replicated, may hold values from 0.1 to 1.9
- q_gain: float32 [1152], replicated, may hold values from 0.1 to 1.9
- k_gain: float32 [1152], replicated, may hold values from 0.1 to 1.9
- w_qkv: bfloat16 [1152, 3456], P('slab'), may hold values from -0.1875 to 0.1875
- w_out: bfloat16 [1152, 1152], P('slab'), may hold values from -0.1875 to 0.1875
Outputs:
- frames_out: bfloat16 [8, 16384, 1152], P('cam', 'slab')
The draws below stay inside these ranges and needn't reach their ends.
All inputs are finite; a program needn't handle non-finite values.
Results may differ from the reference program's by a relative error of at most 0.0033.
Values may be sent and summed in bfloat16 or wider, within the bound.
No kernel may reach another device: no remote copies, remote signals or barrier semaphores. Data moves between devices by JAX's collectives and lax.ppermute only.
A program may use at most 128 MiB of HBM per device.

```python
import jax
import jax.numpy as jnp
from jax import lax

D = 1152
HEADS = 16
HD = 72
SH = 8
XH = 4
TOK_DEV = 256
CAMS = 8
SEQ = 16384


def levels(stream_key, extent, shards, least, high):
    def one(dim, blocks):
        steps = jax.random.uniform(jax.random.fold_in(jax.random.fold_in(stream_key, 6), dim), (blocks,), jnp.float32, least / len(shards), high / len(shards))
        return jnp.repeat(jnp.exp(steps), extent[dim] // blocks).reshape((-1,) + (1,) * (len(extent) - dim - 1))

    level = one(*shards[0])
    for cut in shards[1:]:
        level = level * one(*cut)
    return level


def normal_values(own_key, extent, scale, limit, cuts=(), dtype=jnp.bfloat16):
    level = levels(own_key, extent, cuts, -0.22, 0.18) if cuts else 1.0
    drawn = jax.random.normal(own_key, extent, jnp.float32) * scale * level
    return jnp.minimum(jnp.maximum(drawn, -limit), limit).astype(dtype)


def setup_inputs(seed: int = 0) -> dict:
    seeds = jax.random.split(jax.random.key(seed), 8)
    frames_in = normal_values(seeds[0], (CAMS, SEQ, D), 1.0, 6.0, ((0, 8), (1, 64)))
    cam_embed = normal_values(seeds[1], (CAMS, D), 1.0, 6.0, (), jnp.float32)
    norm_gain = jnp.clip(1.0 + 0.18 * jax.random.normal(seeds[2], (D,), jnp.float32), 0.1, 1.9)
    q_gain = jnp.clip(1.0 + 0.18 * jax.random.normal(seeds[3], (D,), jnp.float32), 0.1, 1.9)
    k_gain = jnp.clip(1.0 + 0.18 * jax.random.normal(seeds[4], (D,), jnp.float32), 0.1, 1.9)
    w_qkv = normal_values(seeds[5], (D, 3 * D), D ** -0.5, 0.1875, ((0, 64),))
    w_out = normal_values(seeds[6], (D, D), D ** -0.5, 0.1875, ((0, 64),))
    return {"frames_in": frames_in, "cam_embed": cam_embed, "norm_gain": norm_gain, "q_gain": q_gain, "k_gain": k_gain, "w_qkv": w_qkv, "w_out": w_out}


def layer_norm(hidden, gain):
    mean = lax.optimization_barrier(jnp.mean(hidden, -1, keepdims=True))
    centred = hidden - mean
    variance = lax.optimization_barrier(jnp.mean(centred * centred, -1, keepdims=True))
    return centred * lax.rsqrt(variance + 1e-06) * gain

def head_norm(part, gain):
    shaped = part.reshape(part.shape[0], HEADS, HD)
    mean_sq = lax.optimization_barrier(jnp.mean(shaped * shaped, -1, keepdims=True))
    return (shaped * lax.rsqrt(mean_sq + 1e-06)).reshape(part.shape) * gain

def softmax_rows(scores):
    expd = jnp.exp(scores)
    return (expd / lax.optimization_barrier(jnp.sum(expd, -1, keepdims=True))).astype(jnp.bfloat16)

def reference(frames_in, cam_embed, norm_gain, q_gain, k_gain, w_qkv, w_out):
    n_sp = SH * HD
    n_cr = XH * HD
    f_tok = 2 * TOK_DEV
    n_fr = SEQ // f_tok
    scale = 1.0 / HD ** 0.5

    def project(items):
        tokens, emb = items
        hidden = tokens.astype(jnp.float32) + emb[None, :]
        normed = layer_norm(hidden, norm_gain).astype(jnp.bfloat16)
        projected = jnp.dot(normed, w_qkv, preferred_element_type=jnp.float32)
        query = head_norm(projected[:, :D], q_gain).astype(jnp.bfloat16)
        keys = head_norm(projected[:, D:2 * D], k_gain).astype(jnp.bfloat16)
        values = projected[:, 2 * D:].astype(jnp.bfloat16)
        return (hidden, query, keys, values)
    hidden, query, keys, values = lax.map(project, (frames_in, cam_embed))
    cross_k = keys[:, :, n_sp:n_sp + n_cr]
    cross_v = values[:, :, n_sp:n_sp + n_cr]
    left_k = jnp.roll(cross_k, 1, axis=0)
    left_v = jnp.roll(cross_v, 1, axis=0)
    right_k = jnp.roll(cross_k, -1, axis=0)
    right_v = jnp.roll(cross_v, -1, axis=0)

    def mix(items):
        hid, que, key, val, lk, lv, rk, rv = items
        q4 = que.reshape(n_fr, f_tok, HEADS, HD).astype(jnp.float32)
        k4 = key.reshape(n_fr, f_tok, HEADS, HD).astype(jnp.float32)
        v4 = val.reshape(n_fr, f_tok, HEADS, HD).astype(jnp.float32)
        sw = softmax_rows(jnp.einsum('frnd,fknd->fnrk', q4[:, :, :SH], k4[:, :, :SH]) * scale)
        space = jnp.einsum('fnrk,fknd->frnd', sw.astype(jnp.float32), v4[:, :, :SH])
        ck = jnp.concatenate([lk.reshape(n_fr, f_tok, XH, HD), rk.reshape(n_fr, f_tok, XH, HD)], 1).astype(jnp.float32)
        cv = jnp.concatenate([lv.reshape(n_fr, f_tok, XH, HD), rv.reshape(n_fr, f_tok, XH, HD)], 1).astype(jnp.float32)
        cw = softmax_rows(jnp.einsum('frnd,fknd->fnrk', q4[:, :, SH:SH + XH], ck) * scale)
        cross = jnp.einsum('fnrk,fknd->frnd', cw.astype(jnp.float32), cv)
        tq = q4[:, :, SH + XH:]
        tk = k4[:, :, SH + XH:]
        tv = v4[:, :, SH + XH:]
        tw = softmax_rows(jnp.einsum('fpnd,gpnd->pnfg', tq, tk) * scale)
        temporal = jnp.einsum('pnfg,gpnd->fpnd', tw.astype(jnp.float32), tv)
        mixed = jnp.concatenate([space.astype(jnp.bfloat16), cross.astype(jnp.bfloat16), temporal.astype(jnp.bfloat16)], 2)
        mixed = mixed.reshape(SEQ, D)
        return (hid + jnp.dot(mixed, w_out, preferred_element_type=jnp.float32)).astype(jnp.bfloat16)
    return lax.map(mix, (hidden, query, keys, values, left_k, left_v, right_k, right_v))
```

```python
import jax
import jax.numpy as jnp
from jax import lax
from jax.experimental import pallas as pl
from jax.experimental.pallas import tpu as pltpu
from jax.sharding import Mesh
from jax.sharding import PartitionSpec as P

HEADS = 16
HD = 72
D = HEADS * HD
PAIR = 2 * HD
GROUP = 3 * PAIR
HALF = 256
CAM = ("x", "yh")
CHIP = ("yl", "z")
SLAB = ("yl", "z", "core")
EVERY = ("x", "yh", "yl", "z", "core")
SCALE = 1.4426950408889634 / HD**0.5
F32 = jnp.float32
BF16 = jnp.bfloat16
VMEM_LIMIT = 50 * 1024 * 1024


def route(move):
    pairs = []
    for x in range(4):
        for y in range(8):
            for z in range(8):
                for core in range(2):
                    a, b, c = move(x, y, z, core)
                    source = ((x * 8 + y) * 8 + z) * 2 + core
                    pairs.append((source, ((a % 4 * 8 + b % 8) * 8 + c % 8) * 2 + core))
    return pairs


def towards(core):
    return 1 if core else -1


ROUTES = (
    route(lambda x, y, z, core: (x + towards(core), y, z)),
    route(lambda x, y, z, core: (x, y + towards(core), z)),
    route(lambda x, y, z, core: (x, y, z + towards(core))),
)


def shift_cam(block, distance):
    return lax.ppermute(block, CAM, [(i, (i + distance) % 8) for i in range(8)])


def swap_core(block):
    return lax.ppermute(block, "core", [(0, 1), (1, 0)])


def mm(a, b):
    return jnp.dot(a, b, preferred_element_type=F32)


def split_mm(a, b):
    high = a.astype(BF16)
    low = (a - high.astype(F32)).astype(BF16)
    return mm(high, b) + mm(low, b)


def normalise(tokens, embed, gain):
    hidden = tokens.astype(F32) + embed
    centred = hidden - jnp.mean(hidden, -1, keepdims=True)
    variance = jnp.mean(centred * centred, -1, keepdims=True)
    return (centred * lax.rsqrt(variance + 1e-06) * gain).astype(BF16)


def head_parts(normed, weight, gains):
    projected = mm(normed, weight)
    lane = lax.broadcasted_iota(jnp.int32, (GROUP, 128), 0) // HD
    head = lax.broadcasted_iota(jnp.int32, (GROUP, 128), 1)
    member = ((lane == head) & (head < 4)).astype(BF16)
    lane_t = lax.broadcasted_iota(jnp.int32, (128, GROUP), 1) // HD
    head_t = lax.broadcasted_iota(jnp.int32, (128, GROUP), 0)
    member_t = ((lane_t == head_t) & (head_t < 4)).astype(BF16)
    mean_sq = split_mm(projected * projected, member) * (1.0 / HD)
    factor = split_mm(lax.rsqrt(mean_sq + 1e-06), member_t)
    column = lax.broadcasted_iota(jnp.int32, projected.shape, 1)
    factor = jnp.where(column < 2 * PAIR, factor, 1.0)
    scaled = (projected * factor * gains).astype(BF16)
    return scaled[:, :PAIR], scaled[:, PAIR : 2 * PAIR], scaled[:, 2 * PAIR :]


def attend(query, pairs_kv, mask=None):
    rows = query.shape[0]
    column = lax.broadcasted_iota(jnp.int32, (rows, PAIR), 1)
    result = None
    for head in range(2):
        own = (column >= head * HD) & (column < (head + 1) * HD)
        picked = jnp.where(own, query, jnp.zeros_like(query))
        total = None
        for keys, values in pairs_kv:
            scores = lax.dot_general(picked, keys, (((1,), (1,)), ((), ())), preferred_element_type=F32)
            expd = jnp.exp2(scores * SCALE)
            if mask is not None:
                expd = jnp.where(mask, expd, 0.0)
            wide = jnp.concatenate([values, jnp.ones((values.shape[0], 256 - PAIR), BF16)], 1)
            part = mm(expd.astype(BF16), wide)
            total = part if total is None else total + part
        head_out = total[:, :PAIR] / total[:, PAIR : PAIR + 1]
        result = head_out if head == 0 else jnp.where(own, head_out, result)
    return result


def start_fetch(order, blocks, group, slot, sem):
    for j, block in enumerate(blocks):
        @pl.when(order[group] == j)
        def _(block=block):
            pltpu.make_async_copy(block, slot, sem).start()


def wait_fetch(blocks, slot, sem):
    pltpu.make_async_copy(blocks[0], slot, sem).wait()


def cross_project_kernel(order, own, other, embed, gain, gains, b0, b1, b2, b3, query, kv, normed, weight, sem):
    blocks = (b0, b1, b2, b3)
    start_fetch(order, blocks, 2, weight, sem)
    normed[:HALF] = normalise(own[...], embed[...], gain[...])
    normed[HALF:] = normalise(other[...], embed[...], gain[...])
    wait_fetch(blocks, weight, sem)
    q, k, v = head_parts(normed[...], weight[...], gains[2:3])
    query[...] = q
    kv[...] = jnp.concatenate([k, v], 1)


def space_kernel(order, normed, gains, b0, b1, b2, b3, out, weight, sem):
    blocks = (b0, b1, b2, b3)
    for group in range(2):
        start_fetch(order, blocks, group, weight.at[group], sem.at[group])
    outs = []
    for group in range(2):
        wait_fetch(blocks, weight.at[group], sem.at[group])
        q, k, v = head_parts(normed[...], weight[group], gains[group : group + 1])
        outs.append(attend(q, [(k, v)]).astype(BF16))
    out[...] = jnp.concatenate(outs, 1)


def time_kernel(order, own, other, embed, gain, gains, b0, b1, b2, b3, out, weight, sem):
    blocks = (b0, b1, b2, b3)
    start_fetch(order, blocks, 3, weight, sem)
    parts = [normalise(ref[...], embed[...], gain[...]) for ref in (own, other)]
    wait_fetch(blocks, weight, sem)
    row = lax.broadcasted_iota(jnp.int32, (HALF, HALF), 0) % 8
    col = lax.broadcasted_iota(jnp.int32, (HALF, HALF), 1) % 8
    core = order[4]
    for i, part in enumerate(parts):
        q, k, v = head_parts(part, weight[...], gains[3:4])
        result = attend(q, [(k, v)], row == col)
        place = core if i == 0 else 1 - core
        out[place] = result.astype(BF16)


def cross_kernel(query, left, right, out):
    sides = [(ref[:, :PAIR], ref[:, PAIR:]) for ref in (left, right)]
    out[...] = attend(query[...], sides).astype(BF16)


def out_kernel(order, tokens, embed, own_sc, other_sc, timed, w_out, out):
    core = order[4]
    total = tokens[...].astype(F32) + embed[...]
    for who, ref in ((core, own_sc), (1 - core, other_sc)):
        total += mm(ref[:, : 2 * PAIR], w_out[pl.ds(pl.multiple_of(who * 2 * PAIR, 16), 2 * PAIR)])
        start = pl.multiple_of(8 * HD + who * PAIR, 16)
        total += mm(ref[:, 2 * PAIR :], w_out[pl.ds(start, PAIR)])
    for who in range(2):
        start = 12 * HD + who * PAIR
        total += mm(timed[who], w_out[start : start + PAIR])
    out[...] = total.astype(BF16)


def call(kernel, out_shapes, args, scratch=(), flops=0, anys=0):
    smem = pl.BlockSpec(memory_space=pltpu.SMEM)
    vmem = pl.BlockSpec(memory_space=pltpu.VMEM)
    hbm = pl.BlockSpec(memory_space=pl.ANY)
    specs = []
    for i, arg in enumerate(args):
        if arg.dtype == jnp.int32:
            specs.append(smem)
        else:
            specs.append(hbm if i >= len(args) - anys else vmem)
    moved = sum(a.size * a.dtype.itemsize for a in args)
    single = not isinstance(out_shapes, tuple)
    return pl.pallas_call(
        kernel,
        out_shape=out_shapes,
        in_specs=specs,
        out_specs=vmem if single else (vmem,) * len(out_shapes),
        scratch_shapes=list(scratch),
        compiler_params=pltpu.CompilerParams(vmem_limit_bytes=VMEM_LIMIT),
        cost_estimate=pl.CostEstimate(flops=flops, bytes_accessed=moved, transcendentals=0),
    )(*args)


def by_group(array, rows):
    shaped = array.reshape(rows, -1, HEADS, HD)
    kinds = shaped.shape[1]

    def arranged(low, high, groups):
        part = shaped[:, :, low:high].reshape(rows, kinds, 2, groups, 2, HD)
        return part.transpose(2, 3, 0, 1, 4, 5).reshape(2, groups, rows, kinds * PAIR)

    return jnp.concatenate([arranged(0, 8, 2), arranged(8, 12, 1), arranged(12, 16, 1)], 1)


def local(frames_in, cam_embed, norm_gain, q_gain, k_gain, w_qkv, w_out):
    tokens = frames_in[0]
    core = lax.axis_index("core")
    x, yl, z = lax.axis_index("x"), lax.axis_index("yl"), lax.axis_index("z")
    colour = (x + 2 * yl + 3 * z) % 4
    groups = jnp.arange(4, dtype=jnp.int32)
    order = jnp.where(core == 0, groups - colour, colour - groups) % 4
    order = jnp.concatenate([order, core[None]]).astype(jnp.int32)
    embed = lax.dynamic_slice_in_dim(cam_embed, lax.axis_index(CAM), 1, 0)
    gain = norm_gain[None]
    gains = jnp.concatenate([q_gain, k_gain, jnp.ones_like(q_gain)])[None]
    gains = lax.dynamic_index_in_dim(by_group(gains, 1), core, 0, False).reshape(4, GROUP)

    w_out_all = lax.all_gather(w_out, SLAB, axis=0, tiled=True)

    mine = by_group(w_qkv, 18)
    received = swap_core(lax.dynamic_index_in_dim(mine, 1 - core, 0, False))
    kept = lax.dynamic_index_in_dim(mine, core, 0, False)
    first = jnp.where(core == 0, kept, received)
    second = jnp.where(core == 0, received, kept)
    pair = jnp.concatenate([first, second], 1)
    rolled = lax.dynamic_slice_in_dim(jnp.concatenate([pair, pair[:3]], 0), x, 4, 0)
    pieces = jnp.stack([rolled[(2 * (i // 8) + 3 * (i % 8)) % 4] for i in range(32)])
    time_own = lax.all_to_all(tokens.reshape(32, 8, D), CHIP, 0, 0, tiled=True).reshape(HALF, D)
    b0 = lax.all_to_all(pieces, CHIP, 0, 0, tiled=True).reshape(D, GROUP)
    other = swap_core(tokens)
    time_other = swap_core(time_own)
    blocks = (b0,) + tuple(lax.ppermute(b0, EVERY, r) for r in ROUTES)

    one = [pltpu.VMEM((D, GROUP), BF16), pltpu.SemaphoreType.DMA]
    two = [pltpu.VMEM((2, D, GROUP), BF16), pltpu.SemaphoreType.DMA((2,))]
    rows = 2 * HALF
    query, kv, normed = call(
        cross_project_kernel,
        (
            jax.ShapeDtypeStruct((rows, PAIR), BF16),
            jax.ShapeDtypeStruct((rows, 2 * PAIR), BF16),
            jax.ShapeDtypeStruct((rows, D), BF16),
        ),
        (order, tokens, other, embed, gain, gains) + blocks,
        one,
        2 * rows * D * GROUP,
        4,
    )
    left, right = shift_cam(kv, 1), shift_cam(kv, -1)
    timed = call(
        time_kernel,
        jax.ShapeDtypeStruct((2, HALF, PAIR), BF16),
        (order, time_own, time_other, embed, gain, gains) + blocks,
        one,
        2 * rows * D * GROUP,
        4,
    )
    timed = timed.reshape(2, 32, 8, PAIR).transpose(1, 0, 2, 3).reshape(64, 8, PAIR)
    timed = lax.all_to_all(timed, SLAB, 0, 0, tiled=True)
    timed = timed.reshape(32, 2, 8, PAIR).transpose(1, 0, 2, 3).reshape(2, HALF, PAIR)
    space = call(
        space_kernel,
        jax.ShapeDtypeStruct((rows, 2 * PAIR), BF16),
        (order, normed, gains) + blocks,
        two,
        4 * rows * D * GROUP,
        4,
    )
    cross = call(cross_kernel, jax.ShapeDtypeStruct((rows, PAIR), BF16), (query, left, right), (), 8 * rows * rows * 256)
    mixed = jnp.concatenate([space, cross], 1)
    arrived = swap_core(mixed[HALF:])
    return call(
        out_kernel,
        jax.ShapeDtypeStruct((HALF, D), BF16),
        (order, tokens, embed, mixed[:HALF], arrived, timed, w_out_all),
        (),
        2 * HALF * D * D,
    )[None]


def solution(mesh):
    fine = Mesh(mesh.devices.reshape(4, 2, 4, 8, 2), EVERY)
    placed = (P(CAM, SLAB, None), P(), P(), P(), P(), P(SLAB, None), P(SLAB, None))
    return jax.shard_map(local, mesh=fine, in_specs=placed, out_specs=P(CAM, SLAB, None), check_vma=False)
```

```python
import jax
import jax.numpy as jnp
from jax import lax
from jax.experimental import pallas as pl
from jax.experimental.pallas import tpu as pltpu
from jax.sharding import Mesh
from jax.sharding import PartitionSpec as P

HEADS = 16
HD = 72
D = HEADS * HD
PAIR = 2 * HD
TRIPLE = 3 * HD
HALF = 256
ROWS = 2 * HALF
FIRST = TRIPLE
SECOND = PAIR + TRIPLE
CAM = ("x", "yh")
CHIP = ("yl", "z")
SLAB = ("yl", "z", "core")
EVERY = ("x", "yh", "yl", "z", "core")
SCALE = 1.4426950408889634 / HD**0.5
F32 = jnp.float32
BF16 = jnp.bfloat16
VMEM_LIMIT = 50 * 1024 * 1024


def route(move):
    pairs = []
    for x in range(4):
        for y in range(8):
            for z in range(8):
                for core in range(2):
                    a, b, c = move(x, y, z, core)
                    source = ((x * 8 + y) * 8 + z) * 2 + core
                    pairs.append((source, ((a % 4 * 8 + b % 8) * 8 + c % 8) * 2 + core))
    return pairs


def towards(core):
    return 1 if core else -1


ROUTES = (
    route(lambda x, y, z, core: (x + towards(core), y, z)),
    route(lambda x, y, z, core: (x, y + towards(core), z)),
    route(lambda x, y, z, core: (x, y, z + towards(core))),
)

ACROSS = route(lambda x, y, z, core: (x, y + 4, z))
ALONG = route(lambda x, y, z, core: (x + (1 if y < 4 else -1), y, z))


def swap_core(block):
    return lax.ppermute(block, "core", [(0, 1), (1, 0)])


def mm(a, b):
    return jnp.dot(a, b, preferred_element_type=F32)


def mm_t(a, b):
    return lax.dot_general(a, b, (((1,), (1,)), ((), ())), preferred_element_type=F32)


def after(value, *others):
    return lax.optimization_barrier((value,) + others)[0]


def arrange_kernel(order, w_qkv, w_out, out):
    core = order[4]

    def columns(kind, head, count):
        start = kind * D + head * HD
        return w_qkv[:, start : start + count * HD]

    for who in range(2):
        place = (who + core) % 2
        for group in range(4):
            head = (8, 12)[group // 2] + 2 * who
            if group % 2 == 0:
                first = [columns(0, head, 2), columns(1, head, 1)]
            else:
                first = [columns(1, head + 1, 1), columns(2, head, 2)]
            start = (who * 4 + group) * PAIR
            one = 4 * who + group
            second = [w_out[:, start : start + PAIR]] + [columns(kind, one, 1) for kind in range(3)]
            out[place, group] = jnp.concatenate(first + second, 1)


def pack_kernel(order, pair, out):
    x = order[5]
    for i in range(32):
        out[i] = pair[(x + 2 * (i // 8) + 3 * (i % 8)) % 4]


def norm_kernel(own, other, embed, gain, out):
    for i, ref in enumerate((own, other)):
        hidden = ref[...].astype(F32) + embed[...]
        centred = hidden - jnp.mean(hidden, -1, keepdims=True)
        variance = jnp.mean(centred * centred, -1, keepdims=True)
        out[i * HALF : (i + 1) * HALF] = (centred * lax.rsqrt(variance + 1e-06) * gain[...]).astype(BF16)


def start_fetch(order, blocks, group, slot, sem):
    for j, block in enumerate(blocks):
        @pl.when(order[group] == j)
        def _(block=block):
            pltpu.make_async_copy(block, slot, sem).start()


def wait_fetch(blocks, slot, sem):
    pltpu.make_async_copy(blocks[0], slot, sem).wait()


def head_norm(part, gain):
    shaped = part.reshape(part.shape[0] // HD, HD, part.shape[1])
    mean_sq = jnp.mean(shaped * shaped, 1, keepdims=True)
    return (shaped * lax.rsqrt(mean_sq + 1e-06)).reshape(part.shape) * gain


def attend(q_t, sides, mask=None):
    total = None
    for k_t, v_t in sides:
        scores = mm(k_t.T.astype(BF16), q_t.astype(BF16))
        expd = jnp.exp2(scores * SCALE)
        if mask is not None:
            expd = jnp.where(mask, expd, 0.0)
        wide = jnp.concatenate([v_t, jnp.ones((8, v_t.shape[1]), F32)], 0).astype(BF16)
        part = mm(wide, expd.astype(BF16))
        total = part if total is None else total + part
    return total[:HD] / total[HD : HD + 1]


def project_pair(normed, weight, gains):
    projected = jnp.concatenate([mm_t(weight[i], normed[...]) for i in range(2)], 0)
    return head_norm(projected[: 2 * PAIR], gains), projected[2 * PAIR :]


def cross_project_kernel(order, normed, gains, b0, b1, b2, b3, q_t, kv_t, weight, sem):
    blocks = (b0, b1, b2, b3)
    for group in range(2):
        start_fetch(order, blocks, group, weight.at[group], sem.at[group])
    for group in range(2):
        wait_fetch(blocks, weight.at[group], sem.at[group])
    qk, v = project_pair(normed, weight, gains[0])
    q_t[...] = qk[:PAIR].astype(BF16)
    kv_t[...] = jnp.concatenate([qk[PAIR:], v], 0).astype(BF16)


def time_kernel(order, normed, gains, b0, b1, b2, b3, out, weight, sem):
    blocks = (b0, b1, b2, b3)
    for group in range(2):
        start_fetch(order, blocks, 2 + group, weight.at[group], sem.at[group])
    for group in range(2):
        wait_fetch(blocks, weight.at[group], sem.at[group])
    qk, v = project_pair(normed, weight, gains[1])
    row = lax.broadcasted_iota(jnp.int32, (HALF, HALF), 0) % 8
    col = lax.broadcasted_iota(jnp.int32, (HALF, HALF), 1) % 8
    core = order[4]
    for i in range(2):
        part = slice(i * HALF, (i + 1) * HALF)
        heads = []
        for head in range(2):
            at = head * HD
            side = (qk[PAIR + at : PAIR + at + HD, part], v[at : at + HD, part])
            heads.append(attend(qk[at : at + HD, part], [side], row == col))
        place = core if i == 0 else 1 - core
        out[place] = jnp.concatenate(heads, 0).T.astype(BF16)


def space_kernel(order, normed, gains, b0, b1, b2, b3, out, w_out, weight, sem):
    blocks = (b0, b1, b2, b3)
    for group in range(4):
        start_fetch(order, blocks, group, weight.at[group], sem.at[group])
    for group in range(4):
        wait_fetch(blocks, weight.at[group], sem.at[group])
        w_out[group * PAIR : (group + 1) * PAIR] = weight[group, :PAIR]
    heads = []
    for group in range(4):
        projected = mm_t(weight[group, PAIR:], normed[...])
        qk = head_norm(projected[:PAIR], gains[group])
        heads.append(attend(qk[:HD], [(qk[HD:], projected[PAIR:])]))
    out[...] = jnp.concatenate(heads, 0).astype(BF16)


def cross_kernel(q_t, kv_a, kv_b, out):
    query = q_t[...].astype(F32)
    both = [ref[...].astype(F32) for ref in (kv_a, kv_b)]
    heads = []
    for head in range(2):
        at = head * HD
        sides = [(kv[at : at + HD], kv[PAIR + at : PAIR + at + HD]) for kv in both]
        heads.append(attend(query[at : at + HD], sides))
    out[...] = jnp.concatenate(heads, 0).astype(BF16)


def out_kernel(order, tokens, embed, own, arrived, timed, w_own, w_other, out):
    swap = order[4] == 1
    mine, theirs = own[...].astype(F32), arrived[...].astype(F32)
    first = jnp.where(swap, theirs, mine)
    second = jnp.where(swap, mine, theirs)
    split = 2 * PAIR
    mixed_t = jnp.concatenate([first[:split], second[:split], first[split:], second[split:]], 0)
    mixed = jnp.concatenate([mixed_t.T.astype(BF16), timed[0], timed[1]], 1)
    one, two = mm_t(mixed, w_own[...]), mm_t(mixed, w_other[...])
    update = jnp.concatenate([jnp.where(swap, two, one), jnp.where(swap, one, two)], 1)
    out[...] = (tokens[...].astype(F32) + embed[...] + update).astype(BF16)


def call(kernel, out_shapes, args, scratch=(), flops=0, anys=0):
    smem = pl.BlockSpec(memory_space=pltpu.SMEM)
    vmem = pl.BlockSpec(memory_space=pltpu.VMEM)
    hbm = pl.BlockSpec(memory_space=pl.ANY)
    specs = []
    for i, arg in enumerate(args):
        if arg.dtype == jnp.int32:
            specs.append(smem)
        else:
            specs.append(hbm if i >= len(args) - anys else vmem)
    moved = sum(a.size * a.dtype.itemsize for a in args)
    single = not isinstance(out_shapes, tuple)
    return pl.pallas_call(
        kernel,
        out_shape=out_shapes,
        in_specs=specs,
        out_specs=vmem if single else (vmem,) * len(out_shapes),
        scratch_shapes=list(scratch),
        compiler_params=pltpu.CompilerParams(vmem_limit_bytes=VMEM_LIMIT),
        cost_estimate=pl.CostEstimate(flops=flops, bytes_accessed=1, transcendentals=0),
    )(*args)


def shape(*dims):
    return jax.ShapeDtypeStruct(dims, BF16)


def local(frames_in, cam_embed, norm_gain, q_gain, k_gain, w_qkv, w_out):
    tokens = frames_in[0]
    core = lax.axis_index("core")
    x, yl, z = lax.axis_index("x"), lax.axis_index("yl"), lax.axis_index("z")
    colour = (x + 2 * yl + 3 * z) % 4
    groups = jnp.arange(4, dtype=jnp.int32)
    order = jnp.where(core == 0, groups - colour, colour - groups) % 4
    order = jnp.concatenate([order, core[None], x[None]]).astype(jnp.int32)
    embed = lax.dynamic_slice_in_dim(cam_embed, lax.axis_index(CAM), 1, 0)
    gain = norm_gain[None]
    both = jnp.stack([q_gain.reshape(HEADS, HD), k_gain.reshape(HEADS, HD)], 1)

    def gains_of(head, count):
        return lax.dynamic_slice_in_dim(both, head, count, 0)

    pair_gains = jnp.stack([gains_of(8 + 2 * core, 2), gains_of(12 + 2 * core, 2)])
    pair_gains = pair_gains.transpose(0, 2, 1, 3).reshape(2, 2 * PAIR, 1)
    space_gains = gains_of(4 * core, 4).reshape(4, PAIR, 1)

    time_own = lax.all_to_all(tokens.reshape(32, 8, D), CHIP, 0, 0, tiled=True).reshape(HALF, D)
    halves = call(arrange_kernel, shape(2, 4, 18, FIRST + SECOND), (order, w_qkv, w_out))
    received = swap_core(halves[1])
    first = jnp.where(core == 0, halves[0], received)
    second = jnp.where(core == 0, received, halves[0])
    pair = jnp.concatenate([first, second], 1)
    other = swap_core(tokens)
    normed = call(norm_kernel, shape(ROWS, D), (tokens, other, embed, gain), (), 8 * 10**9)

    def gather(part):
        pieces = call(pack_kernel, shape(32, 36, part.shape[2]), (order, part))
        return lax.all_to_all(pieces, CHIP, 0, 0, tiled=True).reshape(D, part.shape[2]).T

    def spread(block):
        return (block,) + tuple(lax.ppermute(block, EVERY, r) for r in ROUTES)

    time_other = swap_core(time_own)
    time_normed = call(norm_kernel, shape(ROWS, D), (time_own, time_other, embed, gain), (), 8 * 10**9)
    block = gather(after(pair[:, :, :FIRST], time_own))
    late = gather(after(pair[:, :, FIRST:], block, normed, time_normed))
    blocks = spread(after(block, normed, time_normed))

    two = [pltpu.VMEM((2, FIRST, D), BF16), pltpu.SemaphoreType.DMA((2,))]
    four = [pltpu.VMEM((4, SECOND, D), BF16), pltpu.SemaphoreType.DMA((4,))]
    q_t, kv_t = call(
        cross_project_kernel,
        (shape(PAIR, ROWS), shape(2 * PAIR, ROWS)),
        (order, normed, pair_gains) + blocks,
        two,
        0,
        4,
    )
    kv_a = lax.ppermute(kv_t, EVERY, ACROSS)
    kv_b = lax.ppermute(kv_a, EVERY, ALONG)
    timed = call(
        time_kernel, shape(2, HALF, PAIR), (order, after(time_normed, kv_t), pair_gains) + blocks, two, 0, 4
    )
    more = spread(after(late, timed, kv_a))
    timed = timed.reshape(2, 32, 8, PAIR).transpose(1, 0, 2, 3).reshape(64, 8, PAIR)
    timed = lax.all_to_all(timed, SLAB, 0, 0, tiled=True)
    timed = timed.reshape(32, 2, 8, PAIR).transpose(1, 0, 2, 3).reshape(2, HALF, PAIR)
    space, w_own = call(
        space_kernel,
        (shape(2 * PAIR, ROWS), shape(4 * PAIR, D)),
        (order, after(normed, kv_b, timed), space_gains) + more,
        four,
        0,
        4,
    )
    w_other = swap_core(w_own)
    cross = call(cross_kernel, shape(PAIR, ROWS), (q_t, kv_a, kv_b), )
    mixed = jnp.concatenate([space, cross], 0)
    arrived = swap_core(mixed[:, HALF:])
    return call(
        out_kernel, shape(HALF, D), (order, tokens, embed, mixed[:, :HALF], arrived, timed, w_own, w_other)
    )[None]


def solution(mesh):
    fine = Mesh(mesh.devices.reshape(4, 2, 4, 8, 2), EVERY)
    placed = (P(CAM, SLAB, None), P(), P(), P(), P(), P(SLAB, None), P(SLAB, None))
    return jax.shard_map(local, mesh=fine, in_specs=placed, out_specs=P(CAM, SLAB, None), check_vma=False)
```

```python
import jax
import jax.numpy as jnp
from jax import lax
from jax.experimental import pallas as pl
from jax.experimental.pallas import tpu as pltpu
from jax.sharding import Mesh
from jax.sharding import PartitionSpec as P

HEADS = 16
HD = 72
D = HEADS * HD
PAIR = 2 * HD
TRIPLE = 3 * HD
HALF = 256
ROWS = 2 * HALF
FIRST = TRIPLE
SECOND = PAIR + TRIPLE
CAM = ("x", "yh")
CHIP = ("yl", "z")
SLAB = ("yl", "z", "core")
EVERY = ("x", "yh", "yl", "z", "core")
SCALE = 1.4426950408889634 / HD**0.5
F32 = jnp.float32
BF16 = jnp.bfloat16
VMEM_LIMIT = 50 * 1024 * 1024


def route(move):
    pairs = []
    for x in range(4):
        for y in range(8):
            for z in range(8):
                for core in range(2):
                    a, b, c = move(x, y, z, core)
                    source = ((x * 8 + y) * 8 + z) * 2 + core
                    pairs.append((source, ((a % 4 * 8 + b % 8) * 8 + c % 8) * 2 + core))
    return pairs


def towards(core):
    return 1 if core else -1


ROUTES = (
    route(lambda x, y, z, core: (x + towards(core), y, z)),
    route(lambda x, y, z, core: (x, y + towards(core), z)),
    route(lambda x, y, z, core: (x, y, z + towards(core))),
)

ACROSS = route(lambda x, y, z, core: (x, y + 4, z))
ALONG = route(lambda x, y, z, core: (x + (1 if y < 4 else -1), y, z))


def swap_core(block):
    return lax.ppermute(block, "core", [(0, 1), (1, 0)])


def mm(a, b):
    return jnp.dot(a, b, preferred_element_type=F32)


def mm_t(a, b):
    return lax.dot_general(a, b, (((1,), (1,)), ((), ())), preferred_element_type=F32)


def after(value, *others):
    return lax.optimization_barrier((value,) + others)[0]


def pack_kernel(order, w_qkv, w_out, tokens, out, pieces):
    def columns(kind, head, count):
        start = kind * D + head * HD
        return w_qkv[:, start : start + count * HD].astype(F32)

    for who in range(2):
        for group in range(4):
            start = (who * 4 + group) * PAIR
            parts = [w_out[:, start : start + PAIR].astype(F32)]
            parts += [columns(kind, 4 * who + group, 1) for kind in range(3)]
            head = (8, 12)[group // 2] + 2 * who
            if group % 2 == 0:
                parts += [columns(0, head, 2), columns(1, head, 1)]
            else:
                parts += [columns(1, head + 1, 1), columns(2, head, 2)]
            wide = jnp.concatenate(parts, 1)
            place = who * 4 + group
            for tile in range(4):
                pieces[place, tile * 18 : tile * 18 + 18] = wide[:, tile * 128 : tile * 128 + 128]
            pieces[place, 72:81] = jnp.concatenate([wide[:9, 512:], wide[9:, 512:]], 1)
            pieces[place, 81:84] = jnp.zeros((3, 128), F32)
    x = order[5]
    for dest in range(64):
        colour = (x + 2 * (dest // 16) + 3 * (dest // 2 % 8)) % 4
        block = tokens[dest // 2 * 8 : dest // 2 * 8 + 8].astype(F32)
        block = block[dest % 2 * 4 : dest % 2 * 4 + 4]
        rows = [block[:, tile * 128 : tile * 128 + 128] for tile in range(9)]
        out[dest] = jnp.concatenate([pieces[dest % 2 * 4 + colour]] + rows, 0).astype(BF16)


def unpack_kernel(got, block, tokens, wide):
    for source in range(64):
        rows = got[source].astype(F32)
        at = source * 18
        for tile in range(4):
            wide[tile, at : at + 18] = rows[tile * 18 : tile * 18 + 18]
        wide[4, at : at + 9, :64] = rows[72:81, :64]
        wide[4, at + 9 : at + 18, :64] = rows[72:81, 64:]
        if source % 2 == 1:
            pair = [got[source - 1].astype(F32), rows]
            tiles = []
            for tile in range(9):
                start = 84 + tile * 4
                tiles.append(jnp.concatenate([one[start : start + 4] for one in pair], 0))
            tokens[source * 4 - 4 : source * 4 + 4] = jnp.concatenate(tiles, 1).astype(BF16)
    for tile in range(4):
        block[tile * 128 : tile * 128 + 128] = wide[tile].T.astype(BF16)
    block[512:] = wide[4].T[:64].astype(BF16)


def norm_kernel(own, other, embed, gain, out):
    for i, ref in enumerate((own, other)):
        hidden = ref[...].astype(F32) + embed[...]
        centred = hidden - jnp.mean(hidden, -1, keepdims=True)
        variance = jnp.mean(centred * centred, -1, keepdims=True)
        out[i * HALF : (i + 1) * HALF] = (centred * lax.rsqrt(variance + 1e-06) * gain[...]).astype(BF16)


def start_fetch(order, blocks, group, slot, sem):
    for j, block in enumerate(blocks):
        @pl.when(order[group] == j)
        def _(block=block):
            pltpu.make_async_copy(block, slot, sem).start()


def wait_fetch(blocks, slot, sem):
    pltpu.make_async_copy(blocks[0], slot, sem).wait()


def head_norm(part, gain):
    shaped = part.reshape(part.shape[0] // HD, HD, part.shape[1])
    mean_sq = jnp.mean(shaped * shaped, 1, keepdims=True)
    return (shaped * lax.rsqrt(mean_sq + 1e-06)).reshape(part.shape) * gain


def attend(q_t, sides, mask=None):
    total = None
    for k_t, v_t in sides:
        scores = mm(k_t.T.astype(BF16), q_t.astype(BF16))
        expd = jnp.exp2(scores * SCALE)
        if mask is not None:
            expd = jnp.where(mask, expd, 0.0)
        wide = jnp.concatenate([v_t, jnp.ones((8, v_t.shape[1]), F32)], 0).astype(BF16)
        part = mm(wide, expd.astype(BF16))
        total = part if total is None else total + part
    return total[:HD] / total[HD : HD + 1]


def project_pair(normed, weight, gains):
    projected = jnp.concatenate([mm_t(weight[i, SECOND:], normed[...]) for i in range(2)], 0)
    return head_norm(projected[: 2 * PAIR], gains), projected[2 * PAIR :]


def fetch_all(order, blocks, groups, weight, sem):
    for slot, group in enumerate(groups):
        start_fetch(order, blocks, group, weight.at[slot], sem.at[slot])
    for slot in range(len(groups)):
        wait_fetch(blocks, weight.at[slot], sem.at[slot])


def cross_project_kernel(order, normed, gains, b0, b1, b2, b3, q_t, kv_t, weight, sem):
    fetch_all(order, (b0, b1, b2, b3), (0, 1), weight, sem)
    qk, v = project_pair(normed, weight, gains[0])
    q_t[...] = qk[:PAIR].astype(BF16)
    kv_t[...] = jnp.concatenate([qk[PAIR:], v], 0).astype(BF16)


def time_kernel(order, normed, gains, b0, b1, b2, b3, out, weight, sem):
    fetch_all(order, (b0, b1, b2, b3), (2, 3), weight, sem)
    qk, v = project_pair(normed, weight, gains[1])
    row = lax.broadcasted_iota(jnp.int32, (HALF, HALF), 0) % 8
    col = lax.broadcasted_iota(jnp.int32, (HALF, HALF), 1) % 8
    sets = []
    for i in range(2):
        part = slice(i * HALF, (i + 1) * HALF)
        heads = []
        for head in range(2):
            at = head * HD
            side = (qk[PAIR + at : PAIR + at + HD, part], v[at : at + HD, part])
            heads.append(attend(qk[at : at + HD, part], [side], row == col))
        sets.append(jnp.concatenate(heads, 0).T.reshape(64, 4, PAIR))
    swap = order[4] == 1
    one = jnp.where(swap, sets[1], sets[0])
    two = jnp.where(swap, sets[0], sets[1])
    out[...] = jnp.concatenate([one, two], 1).astype(BF16)


def collect_kernel(order, b0, b1, b2, b3, out, sem):
    blocks = [block.at[pl.ds(0, PAIR)] for block in (b0, b1, b2, b3)]
    slots = [out.at[pl.ds(group * PAIR, PAIR)] for group in range(4)]
    for group in range(4):
        start_fetch(order, blocks, group, slots[group], sem.at[group])
    for group in range(4):
        wait_fetch(blocks, slots[group], sem.at[group])


def space_kernel(order, normed, gains, b0, b1, b2, b3, out, weight, sem):
    fetch_all(order, (b0, b1, b2, b3), range(4), weight, sem)
    heads = []
    for group in range(4):
        projected = mm_t(weight[group, PAIR:SECOND], normed[...])
        qk = head_norm(projected[:PAIR], gains[group])
        heads.append(attend(qk[:HD], [(qk[HD:], projected[PAIR:])]))
    out[...] = jnp.concatenate(heads, 0).astype(BF16)


def cross_kernel(q_t, kv_a, kv_b, out):
    query = q_t[...].astype(F32)
    both = [ref[...].astype(F32) for ref in (kv_a, kv_b)]
    heads = []
    for head in range(2):
        at = head * HD
        sides = [(kv[at : at + HD], kv[PAIR + at : PAIR + at + HD]) for kv in both]
        heads.append(attend(query[at : at + HD], sides))
    out[...] = jnp.concatenate(heads, 0).astype(BF16)


def out_kernel(order, tokens, embed, own, arrived, timed, w_own, w_other, out):
    swap = order[4] == 1
    mine, theirs = own[...].astype(F32), arrived[...].astype(F32)
    first = jnp.where(swap, theirs, mine)
    second = jnp.where(swap, mine, theirs)
    split = 2 * PAIR
    mixed_t = jnp.concatenate([first[:split], second[:split], first[split:], second[split:]], 0)
    late = timed[...].astype(F32).reshape(32, 2, 8, PAIR)
    late = [late[:, who].reshape(HALF, PAIR).astype(BF16) for who in range(2)]
    mixed = jnp.concatenate([mixed_t.T.astype(BF16)] + late, 1)
    one, two = mm_t(mixed, w_own[...]), mm_t(mixed, w_other[...])
    update = jnp.concatenate([jnp.where(swap, two, one), jnp.where(swap, one, two)], 1)
    out[...] = (tokens[...].astype(F32) + embed[...] + update).astype(BF16)


def call(kernel, out_shapes, args, scratch=(), flops=0, anys=0):
    smem = pl.BlockSpec(memory_space=pltpu.SMEM)
    vmem = pl.BlockSpec(memory_space=pltpu.VMEM)
    hbm = pl.BlockSpec(memory_space=pl.ANY)
    specs = []
    for i, arg in enumerate(args):
        if arg.dtype == jnp.int32:
            specs.append(smem)
        else:
            specs.append(hbm if i >= len(args) - anys else vmem)
    moved = sum(a.size * a.dtype.itemsize for a in args)
    single = not isinstance(out_shapes, tuple)
    return pl.pallas_call(
        kernel,
        out_shape=out_shapes,
        in_specs=specs,
        out_specs=vmem if single else (vmem,) * len(out_shapes),
        scratch_shapes=list(scratch),
        compiler_params=pltpu.CompilerParams(vmem_limit_bytes=VMEM_LIMIT),
        cost_estimate=pl.CostEstimate(flops=flops, bytes_accessed=1, transcendentals=0),
    )(*args)


def shape(*dims):
    return jax.ShapeDtypeStruct(dims, BF16)


def local(frames_in, cam_embed, norm_gain, q_gain, k_gain, w_qkv, w_out):
    tokens = frames_in[0]
    core = lax.axis_index("core")
    x, yl, z = lax.axis_index("x"), lax.axis_index("yl"), lax.axis_index("z")
    colour = (x + 2 * yl + 3 * z) % 4
    groups = jnp.arange(4, dtype=jnp.int32)
    order = jnp.where(core == 0, groups - colour, colour - groups) % 4
    order = jnp.concatenate([order, core[None], x[None]]).astype(jnp.int32)
    embed = lax.dynamic_slice_in_dim(cam_embed, lax.axis_index(CAM), 1, 0)
    gain = norm_gain[None]
    both = jnp.stack([q_gain.reshape(HEADS, HD), k_gain.reshape(HEADS, HD)], 1)

    def gains_of(head, count):
        return lax.dynamic_slice_in_dim(both, head, count, 0)

    pair_gains = jnp.stack([gains_of(8 + 2 * core, 2), gains_of(12 + 2 * core, 2)])
    pair_gains = pair_gains.transpose(0, 2, 1, 3).reshape(2, 2 * PAIR, 1)
    space_gains = gains_of(4 * core, 4).reshape(4, PAIR, 1)

    pieces = call(
        pack_kernel, shape(64, 120, 128), (order, w_qkv, w_out, tokens), [pltpu.VMEM((8, 84, 128), F32)]
    )
    got = lax.all_to_all(pieces, SLAB, 0, 0, tiled=True)
    other = swap_core(tokens)
    normed = call(norm_kernel, shape(ROWS, D), (tokens, other, embed, gain), (), 8 * 10**9)
    block, time_own = call(
        unpack_kernel, (shape(SECOND + FIRST, D), shape(HALF, D)), (after(got, normed),), [pltpu.VMEM((5, D, 128), F32)]
    )
    blocks = (block,) + tuple(lax.ppermute(block, EVERY, r) for r in ROUTES)
    time_other = swap_core(time_own)
    time_normed = call(norm_kernel, shape(ROWS, D), (time_own, time_other, embed, gain), (), 8 * 10**9)

    two = [pltpu.VMEM((2, SECOND + FIRST, D), BF16), pltpu.SemaphoreType.DMA((2,))]
    four = [pltpu.VMEM((4, SECOND + FIRST, D), BF16), pltpu.SemaphoreType.DMA((4,))]
    q_t, kv_t = call(
        cross_project_kernel,
        (shape(PAIR, ROWS), shape(2 * PAIR, ROWS)),
        (order, after(normed, time_normed), pair_gains) + blocks,
        two,
        0,
        4,
    )
    kv_a = lax.ppermute(kv_t, EVERY, ACROSS)
    kv_b = lax.ppermute(kv_a, EVERY, ALONG)
    timed = call(time_kernel, shape(64, 8, PAIR), (order, after(time_normed, kv_t), pair_gains) + blocks, two, 0, 4)
    returned = lax.all_to_all(timed, SLAB, 0, 0, tiled=True)
    space = call(
        space_kernel, shape(2 * PAIR, ROWS), (order, after(normed, kv_a, timed), space_gains) + blocks, four, 16 * 10**9, 4
    )
    w_own = call(collect_kernel, shape(4 * PAIR, D), (order,) + blocks, [pltpu.SemaphoreType.DMA((4,))], 0, 4)
    w_other = swap_core(w_own)
    cross = call(cross_kernel, shape(PAIR, ROWS), (q_t, kv_a, kv_b), )
    mixed = jnp.concatenate([space, cross], 0)
    arrived = swap_core(mixed[:, HALF:])
    return call(
        out_kernel, shape(HALF, D), (order, tokens, embed, mixed[:, :HALF], arrived, returned, w_own, w_other)
    )[None]


def solution(mesh):
    fine = Mesh(mesh.devices.reshape(4, 2, 4, 8, 2), EVERY)
    placed = (P(CAM, SLAB, None), P(), P(), P(), P(), P(SLAB, None), P(SLAB, None))
    return jax.shard_map(local, mesh=fine, in_specs=placed, out_specs=P(CAM, SLAB, None), check_vma=False)
```

```python
import jax
import jax.numpy as jnp
from jax import lax
from jax.experimental import pallas as pl
from jax.experimental.pallas import tpu as pltpu
from jax.sharding import Mesh
from jax.sharding import PartitionSpec as P

HEADS = 16
HD = 72
D = HEADS * HD
PAIR = 2 * HD
TRIPLE = 3 * HD
HALF = 256
ROWS = 2 * HALF
FIRST = TRIPLE
SECOND = PAIR + TRIPLE
PIECE = 96
CAM = ("x", "yh")
CHIP = ("yl", "z")
SLAB = ("yl", "z", "core")
EVERY = ("x", "yh", "yl", "z", "core")
SCALE = 1.4426950408889634 / HD**0.5
F32 = jnp.float32
BF16 = jnp.bfloat16
VMEM_LIMIT = 50 * 1024 * 1024


def route(move):
    pairs = []
    for x in range(4):
        for y in range(8):
            for z in range(8):
                for core in range(2):
                    a, b, c = move(x, y, z, core)
                    source = ((x * 8 + y) * 8 + z) * 2 + core
                    pairs.append((source, ((a % 4 * 8 + b % 8) * 8 + c % 8) * 2 + core))
    return pairs


def towards(core):
    return 1 if core else -1


ROUTES = (
    route(lambda x, y, z, core: (x + towards(core), y, z)),
    route(lambda x, y, z, core: (x, y + towards(core), z)),
    route(lambda x, y, z, core: (x, y, z + towards(core))),
)

ACROSS = route(lambda x, y, z, core: (x, y + 4, z))
ALONG = route(lambda x, y, z, core: (x + (1 if y < 4 else -1), y, z))


def swap_core(block):
    return lax.ppermute(block, "core", [(0, 1), (1, 0)])


def mm(a, b):
    return jnp.dot(a, b, preferred_element_type=F32)


def mm_t(a, b):
    return lax.dot_general(a, b, (((1,), (1,)), ((), ())), preferred_element_type=F32)


def after(value, *others):
    return lax.optimization_barrier((value,) + others)[0]


def pack_kernel(order, w_qkv_hbm, w_out_hbm, out, w_qkv, w_out, wide, pieces, in_sem, out_sem):
    loads = [
        pltpu.make_async_copy(w_qkv_hbm, w_qkv, in_sem.at[0]),
        pltpu.make_async_copy(w_out_hbm, w_out, in_sem.at[1]),
    ]
    for load in loads:
        load.start()
    for load in loads:
        load.wait()

    def columns(kind, head, count):
        start = kind * D + head * HD
        return w_qkv[:, start : start + count * HD].astype(F32)

    for who in range(2):
        for group in range(4):
            start = (who * 4 + group) * PAIR
            parts = [w_out[:, start : start + PAIR].astype(F32)]
            parts += [columns(kind, 4 * who + group, 1) for kind in range(3)]
            head = (8, 12)[group // 2] + 2 * who
            if group % 2 == 0:
                parts += [columns(0, head, 2), columns(1, head, 1)]
            else:
                parts += [columns(1, head + 1, 1), columns(2, head, 2)]
            whole = jnp.concatenate(parts, 1)
            place = who * 4 + group
            for tile in range(4):
                wide[tile * 18 : tile * 18 + 18] = whole[:, tile * 128 : tile * 128 + 128]
            wide[72:81] = jnp.concatenate([whole[:9, 512:], whole[9:, 512:]], 1)
            wide[81:] = jnp.zeros((PIECE - 81, 128), F32)
            pieces[place] = wide[...].astype(BF16)
    x = order[5]
    stores = []
    for dest in range(64):
        colour = (x + 2 * (dest // 16) + 3 * (dest // 2 % 8)) % 4
        stores.append(pltpu.make_async_copy(pieces.at[dest % 2 * 4 + colour], out.at[dest], out_sem))
        stores[-1].start()
    for store in stores:
        store.wait()


def unpack_kernel(got, block, wide):
    for source in range(64):
        rows = got[source].astype(F32)
        at = source * 18
        for tile in range(4):
            wide[tile, at : at + 18] = rows[tile * 18 : tile * 18 + 18]
        wide[4, at : at + 9, :64] = rows[72:81, :64]
        wide[4, at + 9 : at + 18, :64] = rows[72:81, 64:]
    for tile in range(4):
        block[tile * 128 : tile * 128 + 128] = wide[tile].T.astype(BF16)
    block[512:] = wide[4].T[:64].astype(BF16)


def norm_kernel(own, other, embed, gain, out):
    for i, ref in enumerate((own, other)):
        hidden = ref[...].astype(F32) + embed[...]
        centred = hidden - jnp.mean(hidden, -1, keepdims=True)
        variance = jnp.mean(centred * centred, -1, keepdims=True)
        out[i * HALF : (i + 1) * HALF] = (centred * lax.rsqrt(variance + 1e-06) * gain[...]).astype(BF16)


def start_fetch(order, blocks, group, slot, sem):
    for j, block in enumerate(blocks):
        @pl.when(order[group] == j)
        def _(block=block):
            pltpu.make_async_copy(block, slot, sem).start()


def wait_fetch(blocks, slot, sem):
    pltpu.make_async_copy(blocks[0], slot, sem).wait()


def head_norm(part, gain):
    shaped = part.reshape(part.shape[0] // HD, HD, part.shape[1])
    mean_sq = jnp.mean(shaped * shaped, 1, keepdims=True)
    return (shaped * lax.rsqrt(mean_sq + 1e-06)).reshape(part.shape) * gain


def attend(q_t, sides, mask=None):
    total = None
    for k_t, v_t in sides:
        scores = mm(k_t.T.astype(BF16), q_t.astype(BF16))
        expd = jnp.exp2(scores * SCALE)
        if mask is not None:
            expd = jnp.where(mask, expd, 0.0)
        wide = jnp.concatenate([v_t, jnp.ones((8, v_t.shape[1]), F32)], 0).astype(BF16)
        part = mm(wide, expd.astype(BF16))
        total = part if total is None else total + part
    return total[:HD] / total[HD : HD + 1]


def project_pair(normed, weight, gains):
    projected = jnp.concatenate([mm_t(weight[i, SECOND:], normed[...]) for i in range(2)], 0)
    return head_norm(projected[: 2 * PAIR], gains), projected[2 * PAIR :]


def fetch_all(order, blocks, groups, weight, sem):
    for slot, group in enumerate(groups):
        start_fetch(order, blocks, group, weight.at[slot], sem.at[slot])
    for slot in range(len(groups)):
        wait_fetch(blocks, weight.at[slot], sem.at[slot])


def cross_project_kernel(order, normed, gains, b0, b1, b2, b3, q_t, kv_t, w_out, weight, sem):
    blocks = (b0, b1, b2, b3)
    parts = [block.at[pl.ds(0, PAIR)] for block in blocks]
    for group in range(2):
        start_fetch(order, blocks, group, weight.at[group], sem.at[group])
    for group in range(4):
        start_fetch(order, parts, group, w_out.at[pl.ds(group * PAIR, PAIR)], sem.at[2 + group])
    for group in range(2):
        wait_fetch(blocks, weight.at[group], sem.at[group])
    qk, v = project_pair(normed, weight, gains[0])
    q_t[...] = qk[:PAIR].astype(BF16)
    kv_t[...] = jnp.concatenate([qk[PAIR:], v], 0).astype(BF16)
    for group in range(4):
        wait_fetch(parts, w_out.at[pl.ds(group * PAIR, PAIR)], sem.at[2 + group])


def time_kernel(order, normed, gains, b0, b1, b2, b3, out, weight, sem):
    fetch_all(order, (b0, b1, b2, b3), (2, 3), weight, sem)
    qk, v = project_pair(normed, weight, gains[1])
    row = lax.broadcasted_iota(jnp.int32, (HALF, HALF), 0) % 8
    col = lax.broadcasted_iota(jnp.int32, (HALF, HALF), 1) % 8
    sets = []
    for i in range(2):
        part = slice(i * HALF, (i + 1) * HALF)
        heads = []
        for head in range(2):
            at = head * HD
            side = (qk[PAIR + at : PAIR + at + HD, part], v[at : at + HD, part])
            heads.append(attend(qk[at : at + HD, part], [side], row == col))
        sets.append(jnp.concatenate(heads, 0).T.reshape(32, 8, PAIR))
    swap = order[4] == 1
    one = jnp.where(swap, sets[1], sets[0])
    two = jnp.where(swap, sets[0], sets[1])
    out[...] = jnp.concatenate([one, two], 1).astype(BF16)


def space_kernel(order, normed, gains, b0, b1, b2, b3, out, weight, sem):
    fetch_all(order, (b0, b1, b2, b3), range(4), weight, sem)
    heads = []
    for group in range(4):
        projected = mm_t(weight[group, PAIR:SECOND], normed[...])
        qk = head_norm(projected[:PAIR], gains[group])
        heads.append(attend(qk[:HD], [(qk[HD:], projected[PAIR:])]))
    out[...] = jnp.concatenate(heads, 0).astype(BF16)


def cross_kernel(order, q_t, kv_a, kv_b, space, timed, keep, give):
    query = q_t[...].astype(F32)
    both = [ref[...].astype(F32) for ref in (kv_a, kv_b)]
    heads = [space[...].astype(F32)]
    for head in range(2):
        at = head * HD
        sides = [(kv[at : at + HD], kv[PAIR + at : PAIR + at + HD]) for kv in both]
        heads.append(attend(query[at : at + HD], sides))
    mixed = jnp.concatenate(heads, 0).T
    late = timed[...].astype(F32)
    late = [late[:, i * 8 : i * 8 + 8].reshape(HALF, PAIR) for i in range(2)]
    swap = order[4] == 1
    keep[...] = jnp.concatenate([mixed[:HALF], jnp.where(swap, late[1], late[0])], 1).astype(BF16)
    give[...] = jnp.concatenate([mixed[HALF:], jnp.where(swap, late[0], late[1])], 1).astype(BF16)


def out_kernel(order, tokens, embed, own, arrived, w_own, w_other, out):
    swap = order[4] == 1
    mine, theirs = own[...].astype(F32), arrived[...].astype(F32)
    first = jnp.where(swap, theirs, mine)
    second = jnp.where(swap, mine, theirs)
    parts = []
    for start, end in ((0, 2 * PAIR), (2 * PAIR, 3 * PAIR), (3 * PAIR, 4 * PAIR)):
        parts += [first[:, start:end], second[:, start:end]]
    mixed = jnp.concatenate(parts, 1).astype(BF16)
    one, two = mm_t(mixed, w_own[...]), mm_t(mixed, w_other[...])
    update = jnp.concatenate([jnp.where(swap, two, one), jnp.where(swap, one, two)], 1)
    out[...] = (tokens[...].astype(F32) + embed[...] + update).astype(BF16)


def call(kernel, out_shapes, args, scratch=(), flops=0, anys=0, out_any=False):
    smem = pl.BlockSpec(memory_space=pltpu.SMEM)
    vmem = pl.BlockSpec(memory_space=pltpu.VMEM)
    hbm = pl.BlockSpec(memory_space=pl.ANY)
    specs = []
    for i, arg in enumerate(args):
        if arg.dtype == jnp.int32:
            specs.append(smem)
        else:
            specs.append(hbm if i >= len(args) - anys else vmem)
    moved = sum(a.size * a.dtype.itemsize for a in args)
    single = not isinstance(out_shapes, tuple)
    return pl.pallas_call(
        kernel,
        out_shape=out_shapes,
        in_specs=specs,
        out_specs=hbm if out_any else vmem if single else (vmem,) * len(out_shapes),
        scratch_shapes=list(scratch),
        compiler_params=pltpu.CompilerParams(vmem_limit_bytes=VMEM_LIMIT),
        cost_estimate=pl.CostEstimate(flops=flops, bytes_accessed=1, transcendentals=0),
    )(*args)


def shape(*dims):
    return jax.ShapeDtypeStruct(dims, BF16)


def local(frames_in, cam_embed, norm_gain, q_gain, k_gain, w_qkv, w_out):
    tokens = frames_in[0]
    core = lax.axis_index("core")
    x, yl, z = lax.axis_index("x"), lax.axis_index("yl"), lax.axis_index("z")
    colour = (x + 2 * yl + 3 * z) % 4
    groups = jnp.arange(4, dtype=jnp.int32)
    order = jnp.where(core == 0, groups - colour, colour - groups) % 4
    order = jnp.concatenate([order, core[None], x[None]]).astype(jnp.int32)
    embed = lax.dynamic_slice_in_dim(cam_embed, lax.axis_index(CAM), 1, 0)
    gain = norm_gain[None]
    both = jnp.stack([q_gain.reshape(HEADS, HD), k_gain.reshape(HEADS, HD)], 1)

    def gains_of(head, count):
        return lax.dynamic_slice_in_dim(both, head, count, 0)

    pair_gains = jnp.stack([gains_of(8 + 2 * core, 2), gains_of(12 + 2 * core, 2)])
    pair_gains = pair_gains.transpose(0, 2, 1, 3).reshape(2, 2 * PAIR, 1)
    space_gains = gains_of(4 * core, 4).reshape(4, PAIR, 1)

    pieces = call(
        pack_kernel,
        shape(64, PIECE, 128),
        (order, w_qkv, w_out),
        [
            pltpu.VMEM((18, 3 * D), BF16),
            pltpu.VMEM((18, D), BF16),
            pltpu.VMEM((PIECE, 128), F32),
            pltpu.VMEM((8, PIECE, 128), BF16),
            pltpu.SemaphoreType.DMA((2,)),
            pltpu.SemaphoreType.DMA,
        ],
        0,
        2,
        True,
    )
    got = lax.all_to_all(pieces, SLAB, 0, 0, tiled=True)
    other = swap_core(tokens)
    normed = call(norm_kernel, shape(ROWS, D), (tokens, other, embed, gain), (), 8 * 10**9)
    block = call(
        unpack_kernel, shape(SECOND + FIRST, D), (after(got, normed, pair_gains, space_gains),), [pltpu.VMEM((5, D, 128), F32)]
    )
    blocks = (block,) + tuple(lax.ppermute(block, EVERY, r) for r in ROUTES)
    time_own = lax.all_to_all(after(tokens, block).reshape(32, 8, D), CHIP, 0, 0, tiled=True).reshape(HALF, D)

    two = pltpu.VMEM((2, SECOND + FIRST, D), BF16)
    four = [pltpu.VMEM((4, SECOND + FIRST, D), BF16), pltpu.SemaphoreType.DMA((4,))]
    q_t, kv_t, w_own = call(
        cross_project_kernel,
        (shape(PAIR, ROWS), shape(2 * PAIR, ROWS), shape(4 * PAIR, D)),
        (order, normed, pair_gains) + blocks,
        [two, pltpu.SemaphoreType.DMA((6,))],
        0,
        4,
    )
    kv_a = lax.ppermute(kv_t, EVERY, ACROSS)
    kv_b = lax.ppermute(kv_a, EVERY, ALONG)
    w_other = swap_core(w_own)
    space = call(
        space_kernel, shape(2 * PAIR, ROWS), (order, after(normed, kv_t), space_gains) + blocks, four, 16 * 10**9, 4
    )
    time_own = after(time_own, kv_t)
    time_other = swap_core(time_own)
    time_normed = call(norm_kernel, shape(ROWS, D), (time_own, time_other, embed, gain), (), 8 * 10**9)
    timed = call(
        time_kernel,
        shape(32, 16, PAIR),
        (order, after(time_normed, space), pair_gains) + blocks,
        [two, pltpu.SemaphoreType.DMA((2,))],
        0,
        4,
    )
    returned = lax.all_to_all(timed, CHIP, 0, 0, tiled=True)
    keep, give = call(
        cross_kernel, (shape(HALF, 4 * PAIR), shape(HALF, 4 * PAIR)), (order, q_t, kv_a, kv_b, space, returned)
    )
    arrived = swap_core(give)
    return call(
        out_kernel, shape(HALF, D), (order, tokens, embed, keep, arrived, w_own, w_other)
    )[None]


def solution(mesh):
    fine = Mesh(mesh.devices.reshape(4, 2, 4, 8, 2), EVERY)
    placed = (P(CAM, SLAB, None), P(), P(), P(), P(), P(SLAB, None), P(SLAB, None))
    return jax.shard_map(local, mesh=fine, in_specs=placed, out_specs=P(CAM, SLAB, None), check_vma=False)
```

```python
import jax
import jax.numpy as jnp
from jax import lax
from jax.experimental import pallas as pl
from jax.experimental.pallas import tpu as pltpu
from jax.sharding import Mesh
from jax.sharding import PartitionSpec as P

HEADS = 16
HD = 72
D = HEADS * HD
PAIR = 2 * HD
TRIPLE = 3 * HD
HALF = 256
ROWS = 2 * HALF
FIRST = TRIPLE
SECOND = PAIR + TRIPLE
PIECE = 96
CAM = ("x", "yh")
CHIP = ("yl", "z")
SLAB = ("yl", "z", "core")
EVERY = ("x", "yh", "yl", "z", "core")
SCALE = 1.4426950408889634 / HD**0.5
F32 = jnp.float32
BF16 = jnp.bfloat16
VMEM_LIMIT = 18 * 1024 * 1024


def route(move):
    pairs = []
    for x in range(4):
        for y in range(8):
            for z in range(8):
                for core in range(2):
                    a, b, c = move(x, y, z, core)
                    source = ((x * 8 + y) * 8 + z) * 2 + core
                    pairs.append((source, ((a % 4 * 8 + b % 8) * 8 + c % 8) * 2 + core))
    return pairs


def towards(core):
    return 1 if core else -1


ROUTES = (
    route(lambda x, y, z, core: (x + towards(core), y, z)),
    route(lambda x, y, z, core: (x, y + towards(core), z)),
    route(lambda x, y, z, core: (x, y, z + towards(core))),
)

ACROSS = route(lambda x, y, z, core: (x, y + 4, z))
ALONG = route(lambda x, y, z, core: (x + (1 if y < 4 else -1), y, z))


def swap_core(block):
    return lax.ppermute(block, "core", [(0, 1), (1, 0)])


def mm(a, b):
    return jnp.dot(a, b, preferred_element_type=F32)


def mm_t(a, b):
    return lax.dot_general(a, b, (((1,), (1,)), ((), ())), preferred_element_type=F32)


def after(value, *others):
    return lax.optimization_barrier((value,) + others)[0]


def pack_kernel(order, w_qkv_hbm, w_out_hbm, out, w_qkv, w_out, wide, pieces, in_sem, out_sem):
    loads = [
        pltpu.make_async_copy(w_qkv_hbm, w_qkv, in_sem.at[0]),
        pltpu.make_async_copy(w_out_hbm, w_out, in_sem.at[1]),
    ]
    for load in loads:
        load.start()
    for load in loads:
        load.wait()

    def columns(kind, head, count):
        start = kind * D + head * HD
        return w_qkv[:, start : start + count * HD].astype(F32)

    for who in range(2):
        for group in range(4):
            start = (who * 4 + group) * PAIR
            parts = [w_out[:, start : start + PAIR].astype(F32)]
            parts += [columns(kind, 4 * who + group, 1) for kind in range(3)]
            head = (8, 12)[group // 2] + 2 * who
            if group % 2 == 0:
                parts += [columns(0, head, 2), columns(1, head, 1)]
            else:
                parts += [columns(1, head + 1, 1), columns(2, head, 2)]
            whole = jnp.concatenate(parts, 1)
            place = who * 4 + group
            for tile in range(4):
                wide[tile * 18 : tile * 18 + 18] = whole[:, tile * 128 : tile * 128 + 128]
            wide[72:81] = jnp.concatenate([whole[:9, 512:], whole[9:, 512:]], 1)
            wide[81:] = jnp.zeros((PIECE - 81, 128), F32)
            pieces[place] = wide[...].astype(BF16)
    x = order[5]
    stores = []
    for dest in range(64):
        colour = (x + 2 * (dest // 16) + 3 * (dest // 2 % 8)) % 4
        stores.append(pltpu.make_async_copy(pieces.at[dest % 2 * 4 + colour], out.at[dest], out_sem))
        stores[-1].start()
    for store in stores:
        store.wait()


def unpack_kernel(got, block, wide):
    for source in range(64):
        rows = got[source].astype(F32)
        at = source * 18
        for tile in range(4):
            wide[tile, at : at + 18] = rows[tile * 18 : tile * 18 + 18]
        wide[4, at : at + 9, :64] = rows[72:81, :64]
        wide[4, at + 9 : at + 18, :64] = rows[72:81, 64:]
    for tile in range(4):
        block[tile * 128 : tile * 128 + 128] = wide[tile].T.astype(BF16)
    block[512:] = wide[4].T[:64].astype(BF16)


def normalise(ref, embed, gain):
    hidden = ref[...].astype(F32) + embed[...]
    centred = hidden - jnp.mean(hidden, -1, keepdims=True)
    variance = jnp.mean(centred * centred, -1, keepdims=True)
    return (centred * lax.rsqrt(variance + 1e-06) * gain[...]).astype(BF16)


def norm_kernel(own, other, embed, gain, out, rows, sem):
    copies = []
    for i, ref in enumerate((own, other)):
        part = pl.ds(i * HALF, HALF)
        rows[part] = normalise(ref, embed, gain)
        copies.append(pltpu.make_async_copy(rows.at[part], out.at[part], sem.at[i]))
        copies[-1].start()
    for copy in copies:
        copy.wait()


def start_fetch(order, blocks, group, slot, sem):
    for j, block in enumerate(blocks):
        @pl.when(order[group] == j)
        def _(block=block):
            pltpu.make_async_copy(block, slot, sem).start()


def wait_fetch(blocks, slot, sem):
    pltpu.make_async_copy(blocks[0], slot, sem).wait()


def head_norm(part, gain):
    shaped = part.reshape(part.shape[0] // HD, HD, part.shape[1])
    mean_sq = jnp.mean(shaped * shaped, 1, keepdims=True)
    return (shaped * lax.rsqrt(mean_sq + 1e-06)).reshape(part.shape) * gain


def attend(q_t, sides, mask=None):
    total = None
    for k_t, v_t in sides:
        scores = mm(k_t.T.astype(BF16), q_t.astype(BF16))
        expd = jnp.exp2(scores * SCALE)
        if mask is not None:
            expd = jnp.where(mask, expd, 0.0)
        wide = jnp.concatenate([v_t, jnp.ones((8, v_t.shape[1]), F32)], 0).astype(BF16)
        part = mm(wide, expd.astype(BF16))
        total = part if total is None else total + part
    return total[:HD] / total[HD : HD + 1]


def project_pair(normed, weight, gains):
    projected = jnp.concatenate([mm_t(weight[i, SECOND:], normed[...]) for i in range(2)], 0)
    return head_norm(projected[: 2 * PAIR], gains), projected[2 * PAIR :]


def cross_project_kernel(order, gains, normed_hbm, b0, b1, b2, b3, q_out, kv_out, w_out, normed, q_t, kv_t, weight, sem):
    blocks = (b0, b1, b2, b3)
    load = pltpu.make_async_copy(normed_hbm, normed, sem.at[6])
    load.start()
    for group in range(2):
        start_fetch(order, blocks, group, weight.at[group], sem.at[group])
    parts = [block.at[pl.ds(0, PAIR)] for block in blocks]
    for group in range(4):
        start_fetch(order, parts, group, w_out.at[pl.ds(group * PAIR, PAIR)], sem.at[2 + group])
    load.wait()
    for group in range(2):
        wait_fetch(blocks, weight.at[group], sem.at[group])
    qk, v = project_pair(normed, weight, gains[...].T[:, :1])
    kv_t[...] = jnp.concatenate([qk[PAIR:], v], 0).astype(BF16)
    kv_store = pltpu.make_async_copy(kv_t, kv_out, sem.at[7])
    kv_store.start()
    q_t[...] = qk[:PAIR].astype(BF16)
    q_store = pltpu.make_async_copy(q_t, q_out, sem.at[8])
    q_store.start()
    for group in range(4):
        wait_fetch(parts, w_out.at[pl.ds(group * PAIR, PAIR)], sem.at[2 + group])
    kv_store.wait()
    q_store.wait()


def time_kernel(order, gains, own, other, embed, gain, b0, b1, b2, b3, out, normed, result, weight, sem):
    blocks = (b0, b1, b2, b3)
    for slot in range(2):
        start_fetch(order, blocks, 2 + slot, weight.at[slot], sem.at[slot])
    normed[:HALF] = normalise(own, embed, gain)
    normed[HALF:] = normalise(other, embed, gain)
    for slot in range(2):
        wait_fetch(blocks, weight.at[slot], sem.at[slot])
    qk, v = project_pair(normed, weight, gains[...].T[:, 1:2])
    row = lax.broadcasted_iota(jnp.int32, (HALF, HALF), 0) % 8
    col = lax.broadcasted_iota(jnp.int32, (HALF, HALF), 1) % 8
    sets = []
    for i in range(2):
        part = slice(i * HALF, (i + 1) * HALF)
        heads = []
        for head in range(2):
            at = head * HD
            side = (qk[PAIR + at : PAIR + at + HD, part], v[at : at + HD, part])
            heads.append(attend(qk[at : at + HD, part], [side], row == col))
        sets.append(jnp.concatenate(heads, 0).T.reshape(32, 8, PAIR))
    swap = order[4] == 1
    one = jnp.where(swap, sets[1], sets[0])
    two = jnp.where(swap, sets[0], sets[1])
    result[...] = jnp.concatenate([one, two], 1).astype(BF16)
    store = pltpu.make_async_copy(result, out, sem.at[2])
    store.start()
    store.wait()


def space_kernel(order, gains, normed_hbm, b0, b1, b2, b3, out, normed, result, weight, sem):
    blocks = (b0, b1, b2, b3)
    load = pltpu.make_async_copy(normed_hbm, normed, sem.at[4])
    load.start()
    for group in range(4):
        start_fetch(order, blocks, group, weight.at[group], sem.at[group])
    load.wait()
    heads = []
    columns = gains[...].T[:PAIR]
    for group in range(4):
        wait_fetch(blocks, weight.at[group], sem.at[group])
        projected = mm_t(weight[group, PAIR:SECOND], normed[...])
        qk = head_norm(projected[:PAIR], columns[:, 2 + group : 3 + group])
        heads.append(attend(qk[:HD], [(qk[HD:], projected[PAIR:])]))
    result[...] = jnp.concatenate(heads, 0).astype(BF16)
    store = pltpu.make_async_copy(result, out, sem.at[5])
    store.start()
    store.wait()


def cross_kernel(order, q_t, kv_a, kv_b, space, timed, keep, give):
    query = q_t[...].astype(F32)
    both = [ref[...].astype(F32) for ref in (kv_a, kv_b)]
    heads = [space[...].astype(F32)]
    for head in range(2):
        at = head * HD
        sides = [(kv[at : at + HD], kv[PAIR + at : PAIR + at + HD]) for kv in both]
        heads.append(attend(query[at : at + HD], sides))
    mixed = jnp.concatenate(heads, 0).T
    late = timed[...].astype(F32)
    late = [late[:, i * 8 : i * 8 + 8].reshape(HALF, PAIR) for i in range(2)]
    swap = order[4] == 1
    keep[...] = jnp.concatenate([mixed[:HALF], jnp.where(swap, late[1], late[0])], 1).astype(BF16)
    give[...] = jnp.concatenate([mixed[HALF:], jnp.where(swap, late[0], late[1])], 1).astype(BF16)


def out_kernel(order, tokens, embed, own, arrived, w_own, w_other, out, weight, sem):
    loads = [pltpu.make_async_copy(ref, weight.at[i], sem.at[i]) for i, ref in enumerate((w_own, w_other))]
    for load in loads:
        load.start()
    swap = order[4] == 1
    mine, theirs = own[...].astype(F32), arrived[...].astype(F32)
    first = jnp.where(swap, theirs, mine)
    second = jnp.where(swap, mine, theirs)
    parts = []
    for start, end in ((0, 2 * PAIR), (2 * PAIR, 3 * PAIR), (3 * PAIR, 4 * PAIR)):
        parts += [first[:, start:end], second[:, start:end]]
    mixed = jnp.concatenate(parts, 1).astype(BF16)
    for load in loads:
        load.wait()
    one, two = mm_t(mixed, weight[0]), mm_t(mixed, weight[1])
    update = jnp.concatenate([jnp.where(swap, two, one), jnp.where(swap, one, two)], 1)
    out[...] = (tokens[...].astype(F32) + embed[...] + update).astype(BF16)


def call(kernel, out_shapes, args, scratch=(), flops=0, anys=0, out_any=False, room=VMEM_LIMIT):
    smem = pl.BlockSpec(memory_space=pltpu.SMEM)
    vmem = pl.BlockSpec(memory_space=pltpu.VMEM)
    hbm = pl.BlockSpec(memory_space=pltpu.HBM)
    specs = []
    for i, arg in enumerate(args):
        if arg.dtype == jnp.int32:
            specs.append(smem)
        else:
            specs.append(hbm if i >= len(args) - anys else vmem)
    moved = sum(a.size * a.dtype.itemsize for a in args)
    single = not isinstance(out_shapes, tuple)
    place = hbm if out_any else vmem
    return pl.pallas_call(
        kernel,
        out_shape=out_shapes,
        in_specs=specs,
        out_specs=place if single else (place,) * len(out_shapes),
        scratch_shapes=list(scratch),
        compiler_params=pltpu.CompilerParams(vmem_limit_bytes=room),
        cost_estimate=pl.CostEstimate(flops=flops, bytes_accessed=1, transcendentals=0),
    )(*args)


def shape(*dims):
    return jax.ShapeDtypeStruct(dims, BF16)


def far(*dims):
    return pltpu.HBM(dims, BF16)


def stay(array):
    return pltpu.with_memory_space_constraint(array, pltpu.HBM)


def local(frames_in, cam_embed, norm_gain, q_gain, k_gain, w_qkv, w_out):
    tokens = frames_in[0]
    core = lax.axis_index("core")
    x, yl, z = lax.axis_index("x"), lax.axis_index("yl"), lax.axis_index("z")
    colour = (x + 2 * yl + 3 * z) % 4
    groups = jnp.arange(4, dtype=jnp.int32)
    order = jnp.where(core == 0, groups - colour, colour - groups) % 4
    order = jnp.concatenate([order, core[None], x[None]]).astype(jnp.int32)
    embed = lax.dynamic_slice_in_dim(cam_embed, lax.axis_index(CAM), 1, 0)
    gain = norm_gain[None]
    both = jnp.stack([q_gain.reshape(HEADS, HD), k_gain.reshape(HEADS, HD)], 1)

    def gains_of(head, count):
        return lax.dynamic_slice_in_dim(both, head, count, 0)

    pair_gains = jnp.stack([gains_of(8 + 2 * core, 2), gains_of(12 + 2 * core, 2)])
    pair_gains = pair_gains.transpose(0, 2, 1, 3).reshape(2, 2 * PAIR)
    space_gains = gains_of(4 * core, 4).reshape(4, PAIR)
    gains = jnp.concatenate([pair_gains, jnp.pad(space_gains, ((0, 2), (0, PAIR)))], 0)

    pieces = call(
        pack_kernel,
        far(64, PIECE, 128),
        (order, w_qkv, w_out),
        [
            pltpu.VMEM((18, 3 * D), BF16),
            pltpu.VMEM((18, D), BF16),
            pltpu.VMEM((PIECE, 128), F32),
            pltpu.VMEM((8, PIECE, 128), BF16),
            pltpu.SemaphoreType.DMA((2,)),
            pltpu.SemaphoreType.DMA,
        ],
        0,
        2,
        True,
        60 * 1024 * 1024,
    )
    got = lax.all_to_all(pieces, SLAB, 0, 0, tiled=True)
    other = swap_core(tokens)
    normed = call(
        norm_kernel,
        far(ROWS, D),
        (tokens, other, embed, gain),
        [pltpu.VMEM((ROWS, D), BF16), pltpu.SemaphoreType.DMA((2,))],
        8 * 10**9,
        0,
        True,
    )
    block = call(
        unpack_kernel, shape(SECOND + FIRST, D), (after(got, normed, gains),), [pltpu.VMEM((5, D, 128), F32)]
    )
    blocks = (block,) + tuple(lax.ppermute(block, EVERY, r) for r in ROUTES)
    time_own = lax.all_to_all(after(tokens, block).reshape(32, 8, D), CHIP, 0, 0, tiled=True).reshape(HALF, D)

    frame = pltpu.VMEM((ROWS, D), BF16)
    two, four = (pltpu.VMEM((n, SECOND + FIRST, D), BF16) for n in (2, 4))
    q_t, kv_t, w_own = call(
        cross_project_kernel,
        (far(PAIR, ROWS), far(2 * PAIR, ROWS), far(4 * PAIR, D)),
        (order, gains, stay(normed)) + blocks,
        [
            frame,
            pltpu.VMEM((PAIR, ROWS), BF16),
            pltpu.VMEM((2 * PAIR, ROWS), BF16),
            two,
            pltpu.SemaphoreType.DMA((9,)),
        ],
        0,
        5,
        True,
    )
    kv_a = lax.ppermute(kv_t, EVERY, ACROSS)
    w_other = swap_core(w_own)
    time_own = after(time_own, kv_t)
    time_other = swap_core(time_own)
    timed = call(
        time_kernel,
        far(32, 16, PAIR),
        (order, gains, time_own, time_other, embed, gain) + blocks,
        [frame, pltpu.VMEM((32, 16, PAIR), BF16), two, pltpu.SemaphoreType.DMA((3,))],
        0,
        4,
        True,
    )
    kv_b = lax.ppermute(after(kv_a, timed), EVERY, ALONG)
    space = call(
        space_kernel,
        far(2 * PAIR, ROWS),
        (order, gains, stay(after(normed, timed))) + blocks,
        [frame, pltpu.VMEM((2 * PAIR, ROWS), BF16), four, pltpu.SemaphoreType.DMA((6,))],
        16 * 10**9,
        5,
        True,
    )
    returned = lax.all_to_all(timed, CHIP, 0, 0, tiled=True)
    keep, give = call(
        cross_kernel, (shape(HALF, 4 * PAIR), shape(HALF, 4 * PAIR)), (order, q_t, kv_a, kv_b, space, returned)
    )
    arrived = swap_core(give)
    return call(
        out_kernel,
        shape(HALF, D),
        (order, tokens, embed, keep, arrived, w_own, w_other),
        [pltpu.VMEM((2, 4 * PAIR, D), BF16), pltpu.SemaphoreType.DMA((2,))],
        0,
        2,
    )[None]


def solution(mesh):
    fine = Mesh(mesh.devices.reshape(4, 2, 4, 8, 2), EVERY)
    placed = (P(CAM, SLAB, None), P(), P(), P(), P(), P(SLAB, None), P(SLAB, None))
    return jax.shard_map(local, mesh=fine, in_specs=placed, out_specs=P(CAM, SLAB, None), check_vma=False)
```

```python
import jax
import jax.numpy as jnp
from jax import lax
from jax.experimental import pallas as pl
from jax.experimental.pallas import tpu as pltpu
from jax.sharding import Mesh
from jax.sharding import PartitionSpec as P

HEADS = 16
HD = 72
D = HEADS * HD
PAIR = 2 * HD
QUAD = 4 * HD
HALF = 256
ROWS = 2 * HALF
PIECE = 88
REST = (1, 5, 6, 7, 2, 3)
CAM = ("x", "yh")
CHIP = ("yl", "z")
SLAB = ("yl", "z", "core")
EVERY = ("x", "yh", "yl", "z", "core")
SCALE = 1.4426950408889634 / HD**0.5
F32 = jnp.float32
BF16 = jnp.bfloat16
VMEM_LIMIT = 18 * 1024 * 1024


def route(move):
    pairs = []
    for x in range(4):
        for y in range(8):
            for z in range(8):
                for core in range(2):
                    a, b, c = move(x, y, z, core)
                    source = ((x * 8 + y) * 8 + z) * 2 + core
                    pairs.append((source, ((a % 4 * 8 + b % 8) * 8 + c % 8) * 2 + core))
    return pairs


def towards(core):
    return 1 if core else -1


OFFSETS = ((0, 1, 0), (1, 0, 0), (0, 0, 1), (0, 1, 1), (0, 0, -1), (-1, 0, 0), (0, -1, 0))


def bring(offset):
    a, b, c = offset
    return route(lambda x, y, z, core: (x + a * towards(core), y + b * towards(core), z + c * towards(core)))


ROUTES = tuple(bring(offset) for offset in OFFSETS)
ACROSS = route(lambda x, y, z, core: (x, y + 4, z))
ALONG = route(lambda x, y, z, core: (x + (1 if y < 4 else -1), y, z))


def swap_core(block):
    return lax.ppermute(block, "core", [(0, 1), (1, 0)])


def mm(a, b):
    return jnp.dot(a, b, preferred_element_type=F32)


def mm_t(a, b):
    return lax.dot_general(a, b, (((1,), (1,)), ((), ())), preferred_element_type=F32)


def after(value, *others):
    return lax.optimization_barrier((value,) + others)[0]


def pack_kernel(order, tokens, w_qkv_hbm, w_out_hbm, out, w_qkv, w_out, pieces, sem):
    loads = [
        pltpu.make_async_copy(w_qkv_hbm, w_qkv, sem.at[0]),
        pltpu.make_async_copy(w_out_hbm, w_out, sem.at[1]),
    ]
    for load in loads:
        load.start()
    for load in loads:
        load.wait()

    def columns(kind, head):
        start = kind * D + head * HD
        return w_qkv[:, start : start + HD].astype(F32)

    for who in range(2):
        a, b, c = 8 + 2 * who, 12 + 2 * who, 4 * who
        content = (
            ((0, a), (0, a + 1)),
            ((0, b), (0, b + 1)),
            ((2, c + 2), (0, c + 3)),
            ((1, c + 3), (2, c + 3)),
            ((1, a), (1, a + 1), (2, a), (2, a + 1)),
            ((1, b), (1, b + 1), (2, b), (2, b + 1)),
            ((0, c), (1, c), (2, c), (0, c + 1)),
            ((1, c + 1), (2, c + 1), (0, c + 2), (1, c + 2)),
        )
        for colour in range(8):
            parts = [columns(*one) for one in content[colour]]
            if colour < 4:
                start = (who * 4 + colour) * PAIR
                parts = [w_out[:, start : start + PAIR].astype(F32)] + parts
            whole = jnp.concatenate(parts, 1)
            place = who * 8 + colour
            pieces[place, :18] = whole[:, :128]
            pieces[place, 18:36] = whole[:, 128:256]
            tail = jnp.concatenate([whole[:9, 256:], whole[9:, 256:], jnp.zeros((9, 64), F32)], 1)
            pieces[place, 36:45] = tail
            pieces[place, 45:] = jnp.zeros((3, 128), F32)
    base = order[9]
    for dest in range(64):
        colour = (base + dest // 16 + 3 * (dest // 2 % 8)) % 8
        block = tokens[dest // 2 * 8 : dest // 2 * 8 + 8].astype(F32)
        block = block[dest % 2 * 4 : dest % 2 * 4 + 4]
        rows = [block[:, tile * 128 : tile * 128 + 128] for tile in range(9)]
        rows = [pieces[dest % 2 * 8 + colour]] + rows + [jnp.zeros((PIECE - 84, 128), F32)]
        out[dest] = jnp.concatenate(rows, 0).astype(BF16)


def unpack_kernel(got, block_out, tokens_out, block, tokens, wide, sem):
    for source in range(64):
        rows = got[source].astype(F32)
        at = source * 18
        wide[0, at : at + 18] = rows[:18]
        wide[1, at : at + 18] = rows[18:36]
        wide[2, at : at + 9, :32] = rows[36:45, :32]
        wide[2, at + 9 : at + 18, :32] = rows[36:45, 32:64]
        if source % 2 == 1:
            pair = [got[source - 1].astype(F32), rows]
            tiles = []
            for tile in range(9):
                start = 48 + tile * 4
                tiles.append(jnp.concatenate([one[start : start + 4] for one in pair], 0))
            tokens[source * 4 - 4 : source * 4 + 4] = jnp.concatenate(tiles, 1).astype(BF16)
    block[:128] = wide[0].T.astype(BF16)
    block[128:256] = wide[1].T.astype(BF16)
    block[256:] = wide[2].T[:32].astype(BF16)
    stores = [
        pltpu.make_async_copy(block, block_out, sem.at[0]),
        pltpu.make_async_copy(tokens, tokens_out, sem.at[1]),
    ]
    for store in stores:
        store.start()
    for store in stores:
        store.wait()


def normalise(ref, embed, gain):
    hidden = ref[...].astype(F32) + embed[...]
    centred = hidden - jnp.mean(hidden, -1, keepdims=True)
    variance = jnp.mean(centred * centred, -1, keepdims=True)
    return (centred * lax.rsqrt(variance + 1e-06) * gain[...]).astype(BF16)


def norm_kernel(own, other, embed, gain, out, rows, sem):
    copies = []
    for i, ref in enumerate((own, other)):
        part = pl.ds(i * HALF, HALF)
        rows[part] = normalise(ref, embed, gain)
        copies.append(pltpu.make_async_copy(rows.at[part], out.at[part], sem.at[i]))
        copies[-1].start()
    for copy in copies:
        copy.wait()


def start_fetch(order, blocks, group, slot, sem):
    for j, block in enumerate(blocks):
        @pl.when(order[group] == j)
        def _(block=block):
            pltpu.make_async_copy(block, slot, sem).start()


def wait_fetch(blocks, slot, sem):
    pltpu.make_async_copy(blocks[0], slot, sem).wait()


def head_norm(part, gain):
    shaped = part.reshape(part.shape[0] // HD, HD, part.shape[1])
    mean_sq = jnp.mean(shaped * shaped, 1, keepdims=True)
    return (shaped * lax.rsqrt(mean_sq + 1e-06)).reshape(part.shape) * gain


def attend(q_t, sides, mask=None):
    total = None
    for k_t, v_t in sides:
        scores = mm(k_t.T.astype(BF16), q_t.astype(BF16))
        expd = jnp.exp2(scores * SCALE)
        if mask is not None:
            expd = jnp.where(mask, expd, 0.0)
        wide = jnp.concatenate([v_t, jnp.ones((8, v_t.shape[1]), F32)], 0).astype(BF16)
        part = mm(wide, expd.astype(BF16))
        total = part if total is None else total + part
    return total[:HD] / total[HD : HD + 1]


def project_pair(normed, w_q, w_kv, gain):
    q = head_norm(mm_t(w_q, normed[...]), gain[:PAIR])
    kv = mm_t(w_kv, normed[...])
    return q, head_norm(kv[:PAIR], gain[PAIR:]), kv[PAIR:]


def cross_project_kernel(order, gains, normed_hbm, *refs):
    blocks, (q_out, kv_out, w_out, rest, normed, q_t, kv_t, weight, sem) = refs[:8], refs[8:]
    load = pltpu.make_async_copy(normed_hbm, normed, sem.at[8])
    load.start()
    first = (0, 4)
    for colour in first + REST:
        start_fetch(order, blocks, colour, weight.at[colour], sem.at[colour])
    stores = []

    def store(source, target):
        stores.append(pltpu.make_async_copy(source, target, sem.at[9 + len(stores)]))
        stores[-1].start()

    def arrived(colour):
        wait_fetch(blocks, weight.at[colour], sem.at[colour])
        if colour < 4:
            store(weight.at[colour, pl.ds(0, PAIR)], w_out.at[pl.ds(colour * PAIR, PAIR)])

    load.wait()
    for colour in first:
        arrived(colour)
    q, k, v = project_pair(normed, weight[0, PAIR:], weight[4], gains[...].T[:, :1])
    kv_t[...] = jnp.concatenate([k, v], 0).astype(BF16)
    store(kv_t, kv_out)
    q_t[...] = q.astype(BF16)
    store(q_t, q_out)
    for place, colour in enumerate(REST):
        arrived(colour)
        store(weight.at[colour], rest.at[place])
    for copy in stores:
        copy.wait()


def time_kernel(order, gains, own, other, embed, gain, rest, out, normed, result, weight, sem):
    load = pltpu.make_async_copy(rest.at[pl.ds(0, 2)], weight, sem.at[0])
    load.start()
    normed[:HALF] = normalise(own, embed, gain)
    normed[HALF:] = normalise(other, embed, gain)
    load.wait()
    q, k, v = project_pair(normed, weight[0, PAIR:], weight[1], gains[...].T[:, 1:2])
    row = lax.broadcasted_iota(jnp.int32, (HALF, HALF), 0) % 8
    col = lax.broadcasted_iota(jnp.int32, (HALF, HALF), 1) % 8
    sets = []
    for i in range(2):
        part = slice(i * HALF, (i + 1) * HALF)
        heads = []
        for head in range(2):
            at = head * HD
            side = (k[at : at + HD, part], v[at : at + HD, part])
            heads.append(attend(q[at : at + HD, part], [side], row == col))
        sets.append(jnp.concatenate(heads, 0).T.reshape(64, 4, PAIR))
    swap = order[8] == 1
    one = jnp.where(swap, sets[1], sets[0])
    two = jnp.where(swap, sets[0], sets[1])
    result[...] = jnp.concatenate([one, two], 1).reshape(32, 16, PAIR).astype(BF16)
    store = pltpu.make_async_copy(result, out, sem.at[1])
    store.start()
    store.wait()


def space_kernel(order, gains, normed_hbm, rest, out, normed, result, weight, sem):
    loads = [pltpu.make_async_copy(rest.at[2 + slot], weight.at[slot], sem.at[slot]) for slot in range(4)]
    loads.append(pltpu.make_async_copy(normed_hbm, normed, sem.at[4]))
    for load in loads:
        load.start()
    columns = gains[...].T[:PAIR]
    loads[4].wait()
    rows = []
    for slot in range(4):
        loads[slot].wait()
        projected = mm_t(weight[slot, (PAIR if slot > 1 else 0) :], normed[...])
        rows += [projected[at : at + HD] for at in range(0, projected.shape[0], HD)]
    heads = []
    for head in range(4):
        q, k, v = rows[3 * head : 3 * head + 3]
        gain = columns[:, 2 + head : 3 + head]
        q, k = head_norm(q, gain[:HD]), head_norm(k, gain[HD:])
        heads.append(attend(q, [(k, v)]))
    result[...] = jnp.concatenate(heads, 0).astype(BF16)
    store = pltpu.make_async_copy(result, out, sem.at[5])
    store.start()
    store.wait()


def cross_kernel(order, q_t, kv_a, kv_b, timed, space_hbm, keep, give, space, sem):
    load = pltpu.make_async_copy(space_hbm, space, sem)
    load.start()
    query = q_t[...].astype(F32)
    both = [ref[...].astype(F32) for ref in (kv_a, kv_b)]
    heads = []
    for head in range(2):
        at = head * HD
        sides = [(kv[at : at + HD], kv[PAIR + at : PAIR + at + HD]) for kv in both]
        heads.append(attend(query[at : at + HD], sides))
    load.wait()
    mixed = jnp.concatenate([space[...].astype(F32)] + heads, 0).T
    late = timed[...].astype(F32)
    late = [late[:, i * 8 : i * 8 + 8].reshape(HALF, PAIR) for i in range(2)]
    swap = order[8] == 1
    keep[...] = jnp.concatenate([mixed[:HALF], jnp.where(swap, late[1], late[0])], 1).astype(BF16)
    give[...] = jnp.concatenate([mixed[HALF:], jnp.where(swap, late[0], late[1])], 1).astype(BF16)


def out_kernel(order, tokens, embed, own, arrived, w_own, w_other, out):
    swap = order[8] == 1
    mine, theirs = own[...].astype(F32), arrived[...].astype(F32)
    first = jnp.where(swap, theirs, mine)
    second = jnp.where(swap, mine, theirs)
    parts = []
    for start, end in ((0, 2 * PAIR), (2 * PAIR, 3 * PAIR), (3 * PAIR, 4 * PAIR)):
        parts += [first[:, start:end], second[:, start:end]]
    mixed = jnp.concatenate(parts, 1).astype(BF16)
    one, two = mm_t(mixed, w_own[...]), mm_t(mixed, w_other[...])
    update = jnp.concatenate([jnp.where(swap, two, one), jnp.where(swap, one, two)], 1)
    out[...] = (tokens[...].astype(F32) + embed[...] + update).astype(BF16)


def call(kernel, out_shapes, args, scratch=(), flops=0, anys=0, out_any=False, room=VMEM_LIMIT):
    smem = pl.BlockSpec(memory_space=pltpu.SMEM)
    vmem = pl.BlockSpec(memory_space=pltpu.VMEM)
    hbm = pl.BlockSpec(memory_space=pltpu.HBM)
    specs = []
    for i, arg in enumerate(args):
        if arg.dtype == jnp.int32:
            specs.append(smem)
        else:
            specs.append(hbm if i >= len(args) - anys else vmem)
    moved = sum(a.size * a.dtype.itemsize for a in args)
    single = not isinstance(out_shapes, tuple)
    place = hbm if out_any else vmem
    return pl.pallas_call(
        kernel,
        out_shape=out_shapes,
        in_specs=specs,
        out_specs=place if single else (place,) * len(out_shapes),
        scratch_shapes=list(scratch),
        compiler_params=pltpu.CompilerParams(vmem_limit_bytes=room),
        cost_estimate=pl.CostEstimate(flops=flops, bytes_accessed=1, transcendentals=0),
    )(*args)


def shape(*dims):
    return jax.ShapeDtypeStruct(dims, BF16)


def far(*dims):
    return pltpu.HBM(dims, BF16)


def stay(array):
    return pltpu.with_memory_space_constraint(array, pltpu.HBM)


def local(frames_in, cam_embed, norm_gain, q_gain, k_gain, w_qkv, w_out):
    tokens = frames_in[0]
    core = lax.axis_index("core")
    base = 2 * lax.axis_index("x") + 4 * lax.axis_index("yh")
    colour = base + lax.axis_index("yl") + 3 * lax.axis_index("z")
    colours = jnp.arange(8, dtype=jnp.int32)
    order = jnp.where(core == 0, colours + 8 * 8 - colour, colour + 8 - colours) % 8
    order = jnp.concatenate([order, core[None], base[None]]).astype(jnp.int32)
    embed = lax.dynamic_slice_in_dim(cam_embed, lax.axis_index(CAM), 1, 0)
    gain = norm_gain[None]
    both = jnp.stack([q_gain.reshape(HEADS, HD), k_gain.reshape(HEADS, HD)], 1)

    def gains_of(head, count):
        return lax.dynamic_slice_in_dim(both, head, count, 0)

    pair_gains = jnp.stack([gains_of(8 + 2 * core, 2), gains_of(12 + 2 * core, 2)])
    pair_gains = pair_gains.transpose(0, 2, 1, 3).reshape(2, 2 * PAIR)
    space_gains = gains_of(4 * core, 4).reshape(4, PAIR)
    gains = jnp.concatenate([pair_gains, jnp.pad(space_gains, ((0, 2), (0, PAIR)))], 0)

    pieces = call(
        pack_kernel,
        shape(64, PIECE, 128),
        (order, tokens, w_qkv, w_out),
        [
            pltpu.VMEM((18, 3 * D), BF16),
            pltpu.VMEM((18, D), BF16),
            pltpu.VMEM((16, 48, 128), F32),
            pltpu.SemaphoreType.DMA((2,)),
        ],
        0,
        2,
        False,
        58 * 1024 * 1024,
    )
    got = lax.all_to_all(pieces, SLAB, 0, 0, tiled=True)
    other = swap_core(tokens)
    normed = call(
        norm_kernel,
        far(ROWS, D),
        (tokens, other, embed, gain),
        [pltpu.VMEM((ROWS, D), BF16), pltpu.SemaphoreType.DMA((2,))],
        8 * 10**9,
        0,
        True,
    )
    block, time_own = call(
        unpack_kernel,
        (far(QUAD, D), far(HALF, D)),
        (after(got, normed, gains),),
        [
            pltpu.VMEM((QUAD, D), BF16),
            pltpu.VMEM((HALF, D), BF16),
            pltpu.VMEM((3, D, 128), F32),
            pltpu.SemaphoreType.DMA((2,)),
        ],
        0,
        0,
        True,
    )
    blocks = (block,) + tuple(lax.ppermute(block, EVERY, r) for r in ROUTES)
    time_other = swap_core(time_own)

    frame = pltpu.VMEM((ROWS, D), BF16)
    two, four, eight = (pltpu.VMEM((n, QUAD, D), BF16) for n in (2, 4, 8))
    q_t, kv_t, w_own, rest = call(
        cross_project_kernel,
        (far(PAIR, ROWS), far(2 * PAIR, ROWS), far(4 * PAIR, D), far(len(REST), QUAD, D)),
        (order, gains, stay(normed)) + blocks,
        [
            frame,
            pltpu.VMEM((PAIR, ROWS), BF16),
            pltpu.VMEM((2 * PAIR, ROWS), BF16),
            eight,
            pltpu.SemaphoreType.DMA((21,)),
        ],
        0,
        9,
        True,
    )
    rest = stay(rest)
    kv_a = lax.ppermute(kv_t, EVERY, ACROSS)
    w_other = swap_core(w_own)
    timed = call(
        time_kernel,
        far(32, 16, PAIR),
        (order, gains, after(time_own, kv_t), time_other, embed, gain, rest),
        [frame, pltpu.VMEM((32, 16, PAIR), BF16), two, pltpu.SemaphoreType.DMA((2,))],
        0,
        1,
        True,
    )
    kv_b = lax.ppermute(after(kv_a, timed), EVERY, ALONG)
    space = call(
        space_kernel,
        far(2 * PAIR, ROWS),
        (order, gains, stay(after(normed, timed)), rest),
        [frame, pltpu.VMEM((2 * PAIR, ROWS), BF16), four, pltpu.SemaphoreType.DMA((6,))],
        16 * 10**9,
        2,
        True,
    )
    returned = lax.all_to_all(timed, CHIP, 0, 0, tiled=True)
    keep, give = call(
        cross_kernel,
        (shape(HALF, 4 * PAIR), shape(HALF, 4 * PAIR)),
        (order, q_t, kv_a, kv_b, returned, stay(space)),
        [pltpu.VMEM((2 * PAIR, ROWS), BF16), pltpu.SemaphoreType.DMA],
        0,
        1,
    )
    arrived = swap_core(give)
    return call(out_kernel, shape(HALF, D), (order, tokens, embed, keep, arrived, w_own, w_other))[None]


def solution(mesh):
    fine = Mesh(mesh.devices.reshape(4, 2, 4, 8, 2), EVERY)
    placed = (P(CAM, SLAB, None), P(), P(), P(), P(), P(SLAB, None), P(SLAB, None))
    return jax.shard_map(local, mesh=fine, in_specs=placed, out_specs=P(CAM, SLAB, None), check_vma=False)
```

```python
import jax
import jax.numpy as jnp
from jax import lax
from jax.experimental import pallas as pl
from jax.experimental.pallas import tpu as pltpu
from jax.sharding import Mesh
from jax.sharding import PartitionSpec as P

HEADS = 16
HD = 72
D = HEADS * HD
PAIR = 2 * HD
QUAD = 4 * HD
HALF = 256
ROWS = 2 * HALF
PIECE = 88
LATE = (6, 7, 2, 3)
CAM = ("x", "yh")
CHIP = ("yl", "z")
SLAB = ("yl", "z", "core")
EVERY = ("x", "yh", "yl", "z", "core")
SCALE = 1.4426950408889634 / HD**0.5
F32 = jnp.float32
BF16 = jnp.bfloat16
VMEM_LIMIT = 18 * 1024 * 1024


def route(move):
    pairs = []
    for x in range(4):
        for y in range(8):
            for z in range(8):
                for core in range(2):
                    a, b, c = move(x, y, z, core)
                    source = ((x * 8 + y) * 8 + z) * 2 + core
                    pairs.append((source, ((a % 4 * 8 + b % 8) * 8 + c % 8) * 2 + core))
    return pairs


def towards(core):
    return 1 if core else -1


OFFSETS = ((0, 0, 1), (0, 1, 0), (1, 0, 0), (0, 0, -1), (0, -1, 0), (0, 1, 1), (-1, 0, 0))
TURNS = (0,) + tuple((2 * a + b + 3 * c) % 8 for a, b, c in OFFSETS)


def bring(offset):
    a, b, c = offset
    return route(lambda x, y, z, core: (x + a * towards(core), y + b * towards(core), z + c * towards(core)))


ROUTES = tuple(bring(offset) for offset in OFFSETS)
ACROSS = route(lambda x, y, z, core: (x, y + 4, z))
ALONG = route(lambda x, y, z, core: (x + (1 if y < 4 else -1), y, z))


def swap_core(block):
    return lax.ppermute(block, "core", [(0, 1), (1, 0)])


def mm(a, b):
    return jnp.dot(a, b, preferred_element_type=F32)


def mm_t(a, b):
    return lax.dot_general(a, b, (((1,), (1,)), ((), ())), preferred_element_type=F32)


def position():
    return [lax.axis_index(axis) for axis in EVERY]


def after(value, *others):
    return lax.optimization_barrier((value,) + others)[0]


def pack_kernel(tokens, w_qkv_hbm, w_out_hbm, out, w_qkv, w_out, pieces, sem):
    loads = [
        pltpu.make_async_copy(w_qkv_hbm, w_qkv, sem.at[0]),
        pltpu.make_async_copy(w_out_hbm, w_out, sem.at[1]),
    ]
    for load in loads:
        load.start()
    for load in loads:
        load.wait()

    def columns(kind, head):
        start = kind * D + head * HD
        return w_qkv[:, start : start + HD].astype(F32)

    for who in range(2):
        a, b, c = 8 + 2 * who, 12 + 2 * who, 4 * who
        content = (
            ((0, a), (0, a + 1)),
            ((0, b), (0, b + 1)),
            ((2, c + 2), (0, c + 3)),
            ((1, c + 3), (2, c + 3)),
            ((1, a), (1, a + 1), (2, a), (2, a + 1)),
            ((1, b), (1, b + 1), (2, b), (2, b + 1)),
            ((0, c), (1, c), (2, c), (0, c + 1)),
            ((1, c + 1), (2, c + 1), (0, c + 2), (1, c + 2)),
        )
        for colour in range(8):
            parts = [columns(*one) for one in content[colour]]
            if colour < 4:
                start = (who * 4 + colour) * PAIR
                parts = [w_out[:, start : start + PAIR].astype(F32)] + parts
            whole = jnp.concatenate(parts, 1)
            place = who * 8 + colour
            pieces[place, :18] = whole[:, :128]
            pieces[place, 18:36] = whole[:, 128:256]
            tail = jnp.concatenate([whole[:9, 256:], whole[9:, 256:], jnp.zeros((9, 64), F32)], 1)
            pieces[place, 36:45] = tail
            pieces[place, 45:] = jnp.zeros((3, 128), F32)
    x, yh = position()[:2]
    base = 2 * x + 4 * yh
    for dest in range(64):
        colour = (base + dest // 16 + 3 * (dest // 2 % 8)) % 8
        block = tokens[dest // 2 * 8 : dest // 2 * 8 + 8].astype(F32)
        block = block[dest % 2 * 4 : dest % 2 * 4 + 4]
        rows = [block[:, tile * 128 : tile * 128 + 128] for tile in range(9)]
        rows = [pieces[dest % 2 * 8 + colour]] + rows + [jnp.zeros((PIECE - 84, 128), F32)]
        out[dest] = jnp.concatenate(rows, 0).astype(BF16)


def unpack_kernel(got, block, block_out, tokens_out, tokens, wide, sem):
    for source in range(64):
        rows = got[source].astype(F32)
        at = source * 18
        wide[0, at : at + 18] = rows[:18]
        wide[1, at : at + 18] = rows[18:36]
        wide[2, at : at + 9, :32] = rows[36:45, :32]
        wide[2, at + 9 : at + 18, :32] = rows[36:45, 32:64]
        if source % 2 == 1:
            pair = [got[source - 1].astype(F32), rows]
            tiles = []
            for tile in range(9):
                start = 48 + tile * 4
                tiles.append(jnp.concatenate([one[start : start + 4] for one in pair], 0))
            tokens[source * 4 - 4 : source * 4 + 4] = jnp.concatenate(tiles, 1).astype(BF16)
    block[:128] = wide[0].T.astype(BF16)
    block[128:256] = wide[1].T.astype(BF16)
    block[256:] = wide[2].T[:32].astype(BF16)
    stores = [
        pltpu.make_async_copy(block, block_out, sem.at[0]),
        pltpu.make_async_copy(tokens, tokens_out, sem.at[1]),
    ]
    for store in stores:
        store.start()
    for store in stores:
        store.wait()


def own_embed(cam_embed):
    return cam_embed[pl.ds(lax.axis_index("x") * 2 + lax.axis_index("yh"), 1)]


def normalise(ref, embed, gain):
    hidden = ref[...].astype(F32) + embed
    centred = hidden - jnp.mean(hidden, -1, keepdims=True)
    variance = jnp.mean(centred * centred, -1, keepdims=True)
    return (centred * lax.rsqrt(variance + 1e-06) * gain[...]).astype(BF16)


def norm_kernel(own, other, cam_embed, gain, out):
    for i, ref in enumerate((own, other)):
        out[i * HALF : (i + 1) * HALF] = normalise(ref, own_embed(cam_embed), gain)


def start_fetch(blocks, colour, slot, sem):
    x, yh, yl, z, core = position()
    ahead = colour - (2 * x + 4 * yh + yl + 3 * z) + 64
    turn = lax.rem(jnp.where(core == 0, ahead, 128 - ahead), 8)
    for block, own in zip(blocks, TURNS):
        @pl.when(turn == own)
        def _(block=block):
            pltpu.make_async_copy(block, slot, sem).start()


def wait_fetch(blocks, slot, sem):
    pltpu.make_async_copy(blocks[0], slot, sem).wait()


def head_norm(part, gain):
    shaped = part.reshape(part.shape[0] // HD, HD, part.shape[1])
    mean_sq = jnp.mean(shaped * shaped, 1, keepdims=True)
    return (shaped * lax.rsqrt(mean_sq + 1e-06)).reshape(part.shape) * gain


def attend(q_t, sides, mask=None):
    total = None
    for k_t, v_t in sides:
        scores = mm(k_t.T.astype(BF16), q_t.astype(BF16))
        expd = jnp.exp2(scores * SCALE)
        if mask is not None:
            expd = jnp.where(mask, expd, 0.0)
        wide = jnp.concatenate([v_t, jnp.ones((8, v_t.shape[1]), F32)], 0).astype(BF16)
        part = mm(wide, expd.astype(BF16))
        total = part if total is None else total + part
    return total[:HD] / total[HD : HD + 1]


def project_pair(normed, w_q, w_kv, gain):
    q = head_norm(mm_t(w_q, normed[...]), gain[:PAIR])
    kv = mm_t(w_kv, normed[...])
    return q, head_norm(kv[:PAIR], gain[PAIR:]), kv[PAIR:]


def cross_project_kernel(gains, normed, *refs):
    blocks, (q_out, kv_t, w_out, early, late, q_t, weight, sem) = refs[:8], refs[8:]
    slots = {0: weight.at[0], 4: weight.at[1], 1: early.at[0], 5: early.at[1]}
    slots.update({colour: late.at[place] for place, colour in enumerate(LATE)})
    for colour, slot in slots.items():
        start_fetch(blocks, colour, slot, sem.at[colour])
    parts = [block.at[pl.ds(0, PAIR)] for block in blocks]
    thirds = [w_out.at[pl.ds(colour * PAIR, PAIR)] for colour in range(4)]
    for colour in range(4):
        start_fetch(parts, colour, thirds[colour], sem.at[8 + colour])
    for colour in (0, 4):
        wait_fetch(blocks, slots[colour], sem.at[colour])
    q, k, v = project_pair(normed, weight[0, PAIR:], weight[1], gains[...].T[:, :1])
    kv_t[...] = jnp.concatenate([k, v], 0).astype(BF16)
    q_t[...] = q.astype(BF16)
    store = pltpu.make_async_copy(q_t, q_out, sem.at[12])
    store.start()
    for colour in (1, 5) + LATE:
        wait_fetch(blocks, slots[colour], sem.at[colour])
    for colour in range(4):
        wait_fetch(parts, thirds[colour], sem.at[8 + colour])
    store.wait()


def time_kernel(gains, normed, weight, out):
    q, k, v = project_pair(normed, weight[0, PAIR:], weight[1], gains[...].T[:, 1:2])
    row = lax.broadcasted_iota(jnp.int32, (HALF, HALF), 0) % 8
    col = lax.broadcasted_iota(jnp.int32, (HALF, HALF), 1) % 8
    sets = []
    for i in range(2):
        part = slice(i * HALF, (i + 1) * HALF)
        heads = []
        for head in range(2):
            at = head * HD
            side = (k[at : at + HD, part], v[at : at + HD, part])
            heads.append(attend(q[at : at + HD, part], [side], row == col))
        sets.append(jnp.concatenate(heads, 0).T.reshape(64, 4, PAIR))
    swap = lax.axis_index("core") == 1
    one = jnp.where(swap, sets[1], sets[0])
    two = jnp.where(swap, sets[0], sets[1])
    out[...] = jnp.concatenate([one, two], 1).reshape(32, 16, PAIR).astype(BF16)


def space_kernel(gains, normed_hbm, weight_hbm, out, normed, result, weight, sem):
    loads = [pltpu.make_async_copy(weight_hbm.at[slot], weight.at[slot], sem.at[slot]) for slot in range(4)]
    loads.insert(0, pltpu.make_async_copy(normed_hbm, normed, sem.at[4]))
    for load in loads:
        load.start()
    columns = gains[...].T[:PAIR]
    loads[0].wait()
    rows = []
    for slot in range(4):
        loads[1 + slot].wait()
        projected = mm_t(weight[slot, (PAIR if slot > 1 else 0) :], normed[...])
        rows += [projected[at : at + HD] for at in range(0, projected.shape[0], HD)]
    heads = []
    for head in range(4):
        q, k, v = rows[3 * head : 3 * head + 3]
        gain = columns[:, 2 + head : 3 + head]
        q, k = head_norm(q, gain[:HD]), head_norm(k, gain[HD:])
        heads.append(attend(q, [(k, v)]))
    result[...] = jnp.concatenate(heads, 0).astype(BF16)
    store = pltpu.make_async_copy(result, out, sem.at[5])
    store.start()
    store.wait()


def cross_kernel(kv_a, kv_b, timed, space_hbm, q_hbm, keep, give, space, q_t, sem):
    loads = [pltpu.make_async_copy(q_hbm, q_t, sem.at[0]), pltpu.make_async_copy(space_hbm, space, sem.at[1])]
    for load in loads:
        load.start()
    both = [ref[...].astype(F32) for ref in (kv_a, kv_b)]
    loads[0].wait()
    query = q_t[...].astype(F32)
    heads = []
    for head in range(2):
        at = head * HD
        sides = [(kv[at : at + HD], kv[PAIR + at : PAIR + at + HD]) for kv in both]
        heads.append(attend(query[at : at + HD], sides))
    loads[1].wait()
    mixed = jnp.concatenate([space[...].astype(F32)] + heads, 0).T
    late = timed[...].astype(F32)
    late = [late[:, i * 8 : i * 8 + 8].reshape(HALF, PAIR) for i in range(2)]
    swap = lax.axis_index("core") == 1
    keep[...] = jnp.concatenate([mixed[:HALF], jnp.where(swap, late[1], late[0])], 1).astype(BF16)
    give[...] = jnp.concatenate([mixed[HALF:], jnp.where(swap, late[0], late[1])], 1).astype(BF16)


def out_kernel(tokens, own, arrived, w_own, w_other, embed_hbm, out, cam_embed, sem):
    load = pltpu.make_async_copy(embed_hbm, cam_embed, sem)
    load.start()
    swap = lax.axis_index("core") == 1
    mine, theirs = own[...].astype(F32), arrived[...].astype(F32)
    first = jnp.where(swap, theirs, mine)
    second = jnp.where(swap, mine, theirs)
    parts = []
    for start, end in ((0, 2 * PAIR), (2 * PAIR, 3 * PAIR), (3 * PAIR, 4 * PAIR)):
        parts += [first[:, start:end], second[:, start:end]]
    mixed = jnp.concatenate(parts, 1).astype(BF16)
    one, two = mm_t(mixed, w_own[...]), mm_t(mixed, w_other[...])
    update = jnp.concatenate([jnp.where(swap, two, one), jnp.where(swap, one, two)], 1)
    load.wait()
    out[...] = (tokens[...].astype(F32) + own_embed(cam_embed) + update).astype(BF16)


def call(kernel, out_shapes, args, scratch=(), flops=0, anys=0, room=VMEM_LIMIT):
    vmem = pl.BlockSpec(memory_space=pltpu.VMEM)
    hbm = pl.BlockSpec(memory_space=pltpu.HBM)
    specs = []
    for i in range(len(args)):
        specs.append(hbm if i >= len(args) - anys else vmem)

    def place(out):
        return hbm if getattr(out, "memory_space", None) == pltpu.HBM else vmem

    single = not isinstance(out_shapes, tuple)
    return pl.pallas_call(
        kernel,
        out_shape=out_shapes,
        in_specs=specs,
        out_specs=place(out_shapes) if single else tuple(place(out) for out in out_shapes),
        scratch_shapes=list(scratch),
        compiler_params=pltpu.CompilerParams(vmem_limit_bytes=room),
        cost_estimate=pl.CostEstimate(flops=flops, bytes_accessed=1, transcendentals=0),
    )(*args)


def shape(*dims):
    return jax.ShapeDtypeStruct(dims, BF16)


def far(*dims):
    return pltpu.HBM(dims, BF16)


def near(*dims):
    return pltpu.VMEM(dims, BF16)


def keep_near(array):
    return pltpu.with_memory_space_constraint(array, pltpu.VMEM)


def stay(array):
    return pltpu.with_memory_space_constraint(array, pltpu.HBM)


def local(frames_in, cam_embed, norm_gain, q_gain, k_gain, w_qkv, w_out):
    tokens = frames_in[0]
    core = lax.axis_index("core")
    gain = norm_gain[None]
    both = jnp.stack([q_gain.reshape(HEADS, HD), k_gain.reshape(HEADS, HD)], 1)

    def gains_of(head, count):
        return lax.dynamic_slice_in_dim(both, head, count, 0)

    pair_gains = jnp.stack([gains_of(8 + 2 * core, 2), gains_of(12 + 2 * core, 2)])
    pair_gains = pair_gains.transpose(0, 2, 1, 3).reshape(2, 2 * PAIR)
    space_gains = gains_of(4 * core, 4).reshape(4, PAIR)
    gains = jnp.concatenate([pair_gains, jnp.pad(space_gains, ((0, 2), (0, PAIR)))], 0)

    pieces = call(
        pack_kernel,
        shape(64, PIECE, 128),
        (tokens, w_qkv, w_out),
        [
            pltpu.VMEM((18, 3 * D), BF16),
            pltpu.VMEM((18, D), BF16),
            pltpu.VMEM((16, 48, 128), F32),
            pltpu.SemaphoreType.DMA((2,)),
        ],
        0,
        2,
        58 * 1024 * 1024,
    )
    got = lax.all_to_all(pieces, SLAB, 0, 0, tiled=True)
    other = swap_core(tokens)
    normed = keep_near(call(norm_kernel, near(ROWS, D), (tokens, other, cam_embed, gain), (), 8 * 10**9))
    own_block, block, time_own = call(
        unpack_kernel,
        (near(QUAD, D), far(QUAD, D), far(HALF, D)),
        (after(got, normed, gains),),
        [
            pltpu.VMEM((HALF, D), BF16),
            pltpu.VMEM((3, D, 128), F32),
            pltpu.SemaphoreType.DMA((2,)),
        ],
    )
    blocks = (keep_near(own_block),) + tuple(lax.ppermute(block, EVERY, r) for r in ROUTES)
    time_other = swap_core(time_own)
    time_normed = keep_near(call(norm_kernel, near(ROWS, D), (time_own, time_other, cam_embed, gain), (), 8 * 10**9))
    q_t, kv_t, w_own, early, late = call(
        cross_project_kernel,
        (far(PAIR, ROWS), shape(2 * PAIR, ROWS), near(4 * PAIR, D), near(2, QUAD, D), far(4, QUAD, D)),
        (gains, after(normed, time_normed)) + blocks,
        [pltpu.VMEM((PAIR, ROWS), BF16), pltpu.VMEM((2, QUAD, D), BF16), pltpu.SemaphoreType.DMA((13,))],
        0,
        8,
    )
    kv_a = lax.ppermute(kv_t, EVERY, ACROSS)
    w_other = swap_core(w_own)
    timed = call(time_kernel, shape(32, 16, PAIR), (gains, after(time_normed, kv_t), keep_near(early)))
    kv_b = lax.ppermute(after(kv_a, timed), EVERY, ALONG)
    space = call(
        space_kernel,
        far(2 * PAIR, ROWS),
        (gains, stay(after(normed, timed)), stay(late)),
        [
            pltpu.VMEM((ROWS, D), BF16),
            pltpu.VMEM((2 * PAIR, ROWS), BF16),
            pltpu.VMEM((4, QUAD, D), BF16),
            pltpu.SemaphoreType.DMA((6,)),
        ],
        16 * 10**9,
        2,
    )
    returned = lax.all_to_all(timed, CHIP, 0, 0, tiled=True)
    keep, give = call(
        cross_kernel,
        (shape(HALF, 4 * PAIR), shape(HALF, 4 * PAIR)),
        (kv_a, kv_b, returned, stay(space), stay(q_t)),
        [pltpu.VMEM((2 * PAIR, ROWS), BF16), pltpu.VMEM((PAIR, ROWS), BF16), pltpu.SemaphoreType.DMA((2,))],
        0,
        2,
    )
    arrived = swap_core(give)
    return call(
        out_kernel,
        shape(HALF, D),
        (tokens, keep, arrived, w_own, w_other, stay(cam_embed)),
        [pltpu.VMEM((8, D), F32), pltpu.SemaphoreType.DMA],
        0,
        1,
    )[None]


def solution(mesh):
    fine = Mesh(mesh.devices.reshape(4, 2, 4, 8, 2), EVERY)
    placed = (P(CAM, SLAB, None), P(), P(), P(), P(), P(SLAB, None), P(SLAB, None))
    return jax.shard_map(local, mesh=fine, in_specs=placed, out_specs=P(CAM, SLAB, None), check_vma=False)
```

```python
import jax
import jax.numpy as jnp
from jax import lax
from jax.experimental import pallas as pl
from jax.experimental.pallas import tpu as pltpu
from jax.sharding import Mesh
from jax.sharding import PartitionSpec as P

HEADS = 16
HD = 72
D = HEADS * HD
PAIR = 2 * HD
QUAD = 4 * HD
HALF = 256
ROWS = 2 * HALF
PIECE = 80
LATE = (6, 7, 2, 3)
CAM = ("x", "yh")
CHIP = ("yl", "z")
SLAB = ("yl", "z", "core")
EVERY = ("x", "yh", "yl", "z", "core")
SCALE = 1.4426950408889634 / HD**0.5
F32 = jnp.float32
BF16 = jnp.bfloat16
VMEM_LIMIT = 18 * 1024 * 1024


def route(move):
    pairs = []
    for x in range(4):
        for y in range(8):
            for z in range(8):
                for core in range(2):
                    a, b, c = move(x, y, z, core)
                    source = ((x * 8 + y) * 8 + z) * 2 + core
                    pairs.append((source, ((a % 4 * 8 + b % 8) * 8 + c % 8) * 2 + core))
    return pairs


def towards(core):
    return 1 if core else -1


OFFSETS = ((-1, 0, 0), (0, 1, 1), (0, -1, 0), (0, 0, -1), (1, 0, 0), (0, 1, 0), (0, 0, 1))
TURNS = (0,) + tuple((2 * a + b + 3 * c) % 8 for a, b, c in OFFSETS)


def bring(offset):
    a, b, c = offset
    return route(lambda x, y, z, core: (x + a * towards(core), y + b * towards(core), z + c * towards(core)))


ROUTES = tuple(bring(offset) for offset in OFFSETS)
ACROSS = route(lambda x, y, z, core: (x, y + 4, z))
ALONG = route(lambda x, y, z, core: (x + (1 if y < 4 else -1), y, z))


def swap_core(block):
    return lax.ppermute(block, "core", [(0, 1), (1, 0)])


def mm(a, b):
    return jnp.dot(a, b, preferred_element_type=F32)


def mm_t(a, b):
    return lax.dot_general(a, b, (((1,), (1,)), ((), ())), preferred_element_type=F32)


def position():
    return [lax.axis_index(axis) for axis in EVERY]


def after(value, *others):
    return lax.optimization_barrier((value,) + others)[0]


def pack_kernel(tokens, w_qkv_hbm, w_out_hbm, out, w_qkv, w_out, pieces, sem):
    loads = [
        pltpu.make_async_copy(w_qkv_hbm, w_qkv, sem.at[0]),
        pltpu.make_async_copy(w_out_hbm, w_out, sem.at[1]),
    ]
    for load in loads:
        load.start()
    for load in loads:
        load.wait()

    def columns(kind, head):
        start = kind * D + head * HD
        return w_qkv[:, start : start + HD].astype(F32)

    for who in range(2):
        a, b, c = 8 + 2 * who, 12 + 2 * who, 4 * who
        content = (
            ((0, a), (0, a + 1)),
            ((0, b), (0, b + 1)),
            ((2, c + 2), (0, c + 3)),
            ((1, c + 3), (2, c + 3)),
            ((1, a), (1, a + 1), (2, a), (2, a + 1)),
            ((1, b), (1, b + 1), (2, b), (2, b + 1)),
            ((0, c), (1, c), (2, c), (0, c + 1)),
            ((1, c + 1), (2, c + 1), (0, c + 2), (1, c + 2)),
        )
        for colour in range(8):
            parts = [columns(*one) for one in content[colour]]
            if colour < 4:
                start = (who * 4 + colour) * PAIR
                parts = [w_out[:, start : start + PAIR].astype(F32)] + parts
            whole = jnp.concatenate(parts, 1)
            place = who * 8 + colour
            pieces[place, :18] = whole[:, :128]
            pieces[place, 18:36] = whole[:, 128:256]
            tail = whole[:, 256:]
            pieces[place, 36:41] = jnp.concatenate([tail[:5], tail[5:10], tail[9:14], tail[13:18]], 1)
            pieces[place, 41:] = jnp.zeros((3, 128), F32)
    x, yh = position()[:2]
    base = 2 * x + 4 * yh
    for dest in range(64):
        colour = (base + dest // 16 + 3 * (dest // 2 % 8)) % 8
        block = tokens[dest // 2 * 8 : dest // 2 * 8 + 8].astype(F32)
        block = block[dest % 2 * 4 : dest % 2 * 4 + 4]
        rows = [block[:, tile * 128 : tile * 128 + 128] for tile in range(9)]
        rows = [pieces[dest % 2 * 8 + colour]] + rows
        out[dest] = jnp.concatenate(rows, 0).astype(BF16)


def unpack_kernel(got, block, block_out, tokens_out, tokens, wide, sem):
    for source in range(64):
        rows = got[source].astype(F32)
        at = source * 18
        wide[0, at : at + 18] = rows[:18]
        wide[1, at : at + 18] = rows[18:36]
        wide[2, at : at + 5, :32] = rows[36:41, :32]
        wide[2, at + 5 : at + 10, :32] = rows[36:41, 32:64]
        wide[2, at + 10 : at + 14, :32] = rows[37:41, 64:96]
        wide[2, at + 14 : at + 18, :32] = rows[37:41, 96:]
        if source % 2 == 1:
            pair = [got[source - 1].astype(F32), rows]
            tiles = []
            for tile in range(9):
                start = 44 + tile * 4
                tiles.append(jnp.concatenate([one[start : start + 4] for one in pair], 0))
            tokens[source * 4 - 4 : source * 4 + 4] = jnp.concatenate(tiles, 1).astype(BF16)
    block[:128] = wide[0].T.astype(BF16)
    block[128:256] = wide[1].T.astype(BF16)
    block[256:] = wide[2].T[:32].astype(BF16)
    stores = [
        pltpu.make_async_copy(block, block_out, sem.at[0]),
        pltpu.make_async_copy(tokens, tokens_out, sem.at[1]),
    ]
    for store in stores:
        store.start()
    for store in stores:
        store.wait()


def own_embed(cam_embed):
    return cam_embed[pl.ds(lax.axis_index("x") * 2 + lax.axis_index("yh"), 1)]


def normalise(ref, embed, gain):
    hidden = ref[...].astype(F32) + embed
    centred = hidden - jnp.mean(hidden, -1, keepdims=True)
    variance = jnp.mean(centred * centred, -1, keepdims=True)
    return (centred * lax.rsqrt(variance + 1e-06) * gain[...]).astype(BF16)


def norm_kernel(own, other, cam_embed, gain, out):
    for i, ref in enumerate((own, other)):
        out[i * HALF : (i + 1) * HALF] = normalise(ref, own_embed(cam_embed), gain)


def start_fetch(blocks, colour, slot, sem):
    x, yh, yl, z, core = position()
    ahead = colour - (2 * x + 4 * yh + yl + 3 * z) + 64
    turn = lax.rem(jnp.where(core == 0, ahead, 128 - ahead), 8)
    for block, own in zip(blocks, TURNS):
        @pl.when(turn == own)
        def _(block=block):
            pltpu.make_async_copy(block, slot, sem).start()


def wait_fetch(blocks, slot, sem):
    pltpu.make_async_copy(blocks[0], slot, sem).wait()


def head_norm(part, gain):
    shaped = part.reshape(part.shape[0] // HD, HD, part.shape[1])
    mean_sq = jnp.mean(shaped * shaped, 1, keepdims=True)
    return (shaped * lax.rsqrt(mean_sq + 1e-06)).reshape(part.shape) * gain


def attend(q_t, sides, mask=None):
    total = None
    for k_t, v_t in sides:
        scores = mm(k_t.T.astype(BF16), q_t.astype(BF16))
        expd = jnp.exp2(scores * SCALE)
        if mask is not None:
            expd = jnp.where(mask, expd, 0.0)
        wide = jnp.concatenate([v_t, jnp.ones((8, v_t.shape[1]), F32)], 0).astype(BF16)
        part = mm(wide, expd.astype(BF16))
        total = part if total is None else total + part
    return total[:HD] / total[HD : HD + 1]


def project_pair(normed, w_q, w_kv, gain):
    q = head_norm(mm_t(w_q, normed[...]), gain[:PAIR])
    kv = mm_t(w_kv, normed[...])
    return q, head_norm(kv[:PAIR], gain[PAIR:]), kv[PAIR:]


def cross_project_kernel(gains, normed, *refs):
    blocks, (q_out, kv_t, w_out, early, late, q_t, weight, sem) = refs[:8], refs[8:]
    slots = {0: weight.at[0], 4: weight.at[1], 1: early.at[0], 5: early.at[1]}
    slots.update({colour: late.at[place] for place, colour in enumerate(LATE)})
    for colour, slot in slots.items():
        start_fetch(blocks, colour, slot, sem.at[colour])
    parts = [block.at[pl.ds(0, PAIR)] for block in blocks]
    thirds = [w_out.at[pl.ds(colour * PAIR, PAIR)] for colour in range(4)]
    for colour in range(4):
        start_fetch(parts, colour, thirds[colour], sem.at[8 + colour])
    for colour in (0, 4):
        wait_fetch(blocks, slots[colour], sem.at[colour])
    q, k, v = project_pair(normed, weight[0, PAIR:], weight[1], gains[...].T[:, :1])
    kv_t[...] = jnp.concatenate([k, v], 0).astype(BF16)
    q_t[...] = q.astype(BF16)
    store = pltpu.make_async_copy(q_t, q_out, sem.at[12])
    store.start()
    for colour in (1, 5) + LATE:
        wait_fetch(blocks, slots[colour], sem.at[colour])
    for colour in range(4):
        wait_fetch(parts, thirds[colour], sem.at[8 + colour])
    store.wait()


def time_kernel(gains, normed, weight, out):
    q, k, v = project_pair(normed, weight[0, PAIR:], weight[1], gains[...].T[:, 1:2])
    row = lax.broadcasted_iota(jnp.int32, (HALF, HALF), 0) % 8
    col = lax.broadcasted_iota(jnp.int32, (HALF, HALF), 1) % 8
    sets = []
    for i in range(2):
        part = slice(i * HALF, (i + 1) * HALF)
        heads = []
        for head in range(2):
            at = head * HD
            side = (k[at : at + HD, part], v[at : at + HD, part])
            heads.append(attend(q[at : at + HD, part], [side], row == col))
        sets.append(jnp.concatenate(heads, 0).T.reshape(64, 4, PAIR))
    swap = lax.axis_index("core") == 1
    one = jnp.where(swap, sets[1], sets[0])
    two = jnp.where(swap, sets[0], sets[1])
    out[...] = jnp.concatenate([one, two], 1).reshape(32, 16, PAIR).astype(BF16)


def space_kernel(gains, normed_hbm, weight_hbm, out, normed, result, weight, sem):
    loads = [pltpu.make_async_copy(weight_hbm.at[slot], weight.at[slot], sem.at[slot]) for slot in range(4)]
    loads.insert(0, pltpu.make_async_copy(normed_hbm, normed, sem.at[4]))
    for load in loads:
        load.start()
    columns = gains[...].T[:PAIR]
    loads[0].wait()
    rows = []
    for slot in range(4):
        loads[1 + slot].wait()
        projected = mm_t(weight[slot, (PAIR if slot > 1 else 0) :], normed[...])
        rows += [projected[at : at + HD] for at in range(0, projected.shape[0], HD)]
    heads = []
    for head in range(4):
        q, k, v = rows[3 * head : 3 * head + 3]
        gain = columns[:, 2 + head : 3 + head]
        q, k = head_norm(q, gain[:HD]), head_norm(k, gain[HD:])
        heads.append(attend(q, [(k, v)]))
    result[...] = jnp.concatenate(heads, 0).astype(BF16)
    store = pltpu.make_async_copy(result, out, sem.at[5])
    store.start()
    store.wait()


def cross_kernel(kv_a, kv_b, timed, space_hbm, q_hbm, keep, give, space, q_t, sem):
    loads = [pltpu.make_async_copy(q_hbm, q_t, sem.at[0]), pltpu.make_async_copy(space_hbm, space, sem.at[1])]
    for load in loads:
        load.start()
    both = [ref[...].astype(F32) for ref in (kv_a, kv_b)]
    loads[0].wait()
    query = q_t[...].astype(F32)
    heads = []
    for head in range(2):
        at = head * HD
        sides = [(kv[at : at + HD], kv[PAIR + at : PAIR + at + HD]) for kv in both]
        heads.append(attend(query[at : at + HD], sides))
    loads[1].wait()
    mixed = jnp.concatenate([space[...].astype(F32)] + heads, 0).T
    late = timed[...].astype(F32)
    late = [late[:, i * 8 : i * 8 + 8].reshape(HALF, PAIR) for i in range(2)]
    swap = lax.axis_index("core") == 1
    keep[...] = jnp.concatenate([mixed[:HALF], jnp.where(swap, late[1], late[0])], 1).astype(BF16)
    give[...] = jnp.concatenate([mixed[HALF:], jnp.where(swap, late[0], late[1])], 1).astype(BF16)


def out_kernel(tokens, own, arrived, w_own, w_other, embed_hbm, out, cam_embed, sem):
    load = pltpu.make_async_copy(embed_hbm, cam_embed, sem)
    load.start()
    swap = lax.axis_index("core") == 1
    mine, theirs = own[...].astype(F32), arrived[...].astype(F32)
    first = jnp.where(swap, theirs, mine)
    second = jnp.where(swap, mine, theirs)
    parts = []
    for start, end in ((0, 2 * PAIR), (2 * PAIR, 3 * PAIR), (3 * PAIR, 4 * PAIR)):
        parts += [first[:, start:end], second[:, start:end]]
    mixed = jnp.concatenate(parts, 1).astype(BF16)
    one, two = mm_t(mixed, w_own[...]), mm_t(mixed, w_other[...])
    update = jnp.concatenate([jnp.where(swap, two, one), jnp.where(swap, one, two)], 1)
    load.wait()
    out[...] = (tokens[...].astype(F32) + own_embed(cam_embed) + update).astype(BF16)


def call(kernel, out_shapes, args, scratch=(), flops=0, anys=0, room=VMEM_LIMIT):
    vmem = pl.BlockSpec(memory_space=pltpu.VMEM)
    hbm = pl.BlockSpec(memory_space=pltpu.HBM)
    specs = []
    for i in range(len(args)):
        specs.append(hbm if i >= len(args) - anys else vmem)

    def place(out):
        return hbm if getattr(out, "memory_space", None) == pltpu.HBM else vmem

    single = not isinstance(out_shapes, tuple)
    return pl.pallas_call(
        kernel,
        out_shape=out_shapes,
        in_specs=specs,
        out_specs=place(out_shapes) if single else tuple(place(out) for out in out_shapes),
        scratch_shapes=list(scratch),
        compiler_params=pltpu.CompilerParams(vmem_limit_bytes=room),
        cost_estimate=pl.CostEstimate(flops=flops, bytes_accessed=1, transcendentals=0),
    )(*args)


def shape(*dims):
    return jax.ShapeDtypeStruct(dims, BF16)


def far(*dims):
    return pltpu.HBM(dims, BF16)


def near(*dims):
    return pltpu.VMEM(dims, BF16)


def keep_near(array):
    return pltpu.with_memory_space_constraint(array, pltpu.VMEM)


def stay(array):
    return pltpu.with_memory_space_constraint(array, pltpu.HBM)


def local(frames_in, cam_embed, norm_gain, q_gain, k_gain, w_qkv, w_out):
    tokens = frames_in[0]
    core = lax.axis_index("core")
    gain = norm_gain[None]
    both = jnp.stack([q_gain.reshape(HEADS, HD), k_gain.reshape(HEADS, HD)], 1)

    def gains_of(head, count):
        return lax.dynamic_slice_in_dim(both, head, count, 0)

    pair_gains = jnp.stack([gains_of(8 + 2 * core, 2), gains_of(12 + 2 * core, 2)])
    pair_gains = pair_gains.transpose(0, 2, 1, 3).reshape(2, 2 * PAIR)
    space_gains = gains_of(4 * core, 4).reshape(4, PAIR)
    gains = jnp.concatenate([pair_gains, jnp.pad(space_gains, ((0, 2), (0, PAIR)))], 0)

    pieces = call(
        pack_kernel,
        shape(64, PIECE, 128),
        (tokens, w_qkv, w_out),
        [
            pltpu.VMEM((18, 3 * D), BF16),
            pltpu.VMEM((18, D), BF16),
            pltpu.VMEM((16, 44, 128), F32),
            pltpu.SemaphoreType.DMA((2,)),
        ],
        0,
        2,
        58 * 1024 * 1024,
    )
    got = lax.all_to_all(pieces, SLAB, 0, 0, tiled=True)
    other = swap_core(tokens)
    normed = keep_near(call(norm_kernel, near(ROWS, D), (tokens, other, cam_embed, gain), (), 8 * 10**9))
    own_block, block, time_own = call(
        unpack_kernel,
        (near(QUAD, D), far(QUAD, D), far(HALF, D)),
        (after(got, normed, gains),),
        [
            pltpu.VMEM((HALF, D), BF16),
            pltpu.VMEM((3, D, 128), F32),
            pltpu.SemaphoreType.DMA((2,)),
        ],
    )
    blocks = (keep_near(own_block),) + tuple(lax.ppermute(block, EVERY, r) for r in ROUTES)
    time_other = swap_core(time_own)
    time_normed = keep_near(call(norm_kernel, near(ROWS, D), (time_own, time_other, cam_embed, gain), (), 8 * 10**9))
    q_t, kv_t, w_own, early, late = call(
        cross_project_kernel,
        (far(PAIR, ROWS), shape(2 * PAIR, ROWS), near(4 * PAIR, D), near(2, QUAD, D), far(4, QUAD, D)),
        (gains, after(normed, time_normed)) + blocks,
        [pltpu.VMEM((PAIR, ROWS), BF16), pltpu.VMEM((2, QUAD, D), BF16), pltpu.SemaphoreType.DMA((13,))],
        0,
        8,
    )
    kv_a = lax.ppermute(kv_t, EVERY, ACROSS)
    w_other = swap_core(w_own)
    timed = call(time_kernel, shape(32, 16, PAIR), (gains, after(time_normed, kv_t), keep_near(early)))
    kv_b = lax.ppermute(after(kv_a, timed), EVERY, ALONG)
    space = call(
        space_kernel,
        far(2 * PAIR, ROWS),
        (gains, stay(after(normed, timed)), stay(late)),
        [
            pltpu.VMEM((ROWS, D), BF16),
            pltpu.VMEM((2 * PAIR, ROWS), BF16),
            pltpu.VMEM((4, QUAD, D), BF16),
            pltpu.SemaphoreType.DMA((6,)),
        ],
        16 * 10**9,
        2,
    )
    returned = lax.all_to_all(timed, CHIP, 0, 0, tiled=True)
    keep, give = call(
        cross_kernel,
        (shape(HALF, 4 * PAIR), shape(HALF, 4 * PAIR)),
        (kv_a, kv_b, returned, stay(space), stay(q_t)),
        [pltpu.VMEM((2 * PAIR, ROWS), BF16), pltpu.VMEM((PAIR, ROWS), BF16), pltpu.SemaphoreType.DMA((2,))],
        0,
        2,
    )
    arrived = swap_core(give)
    return call(
        out_kernel,
        shape(HALF, D),
        (tokens, keep, arrived, w_own, w_other, stay(cam_embed)),
        [pltpu.VMEM((8, D), F32), pltpu.SemaphoreType.DMA],
        0,
        1,
    )[None]


def solution(mesh):
    fine = Mesh(mesh.devices.reshape(4, 2, 4, 8, 2), EVERY)
    placed = (P(CAM, SLAB, None), P(), P(), P(), P(), P(SLAB, None), P(SLAB, None))
    return jax.shard_map(local, mesh=fine, in_specs=placed, out_specs=P(CAM, SLAB, None), check_vma=False)
```

```python
import jax
import jax.numpy as jnp
from jax import lax
from jax.experimental import pallas as pl
from jax.experimental.pallas import tpu as pltpu
from jax.sharding import Mesh
from jax.sharding import PartitionSpec as P

HEADS = 16
HD = 72
D = HEADS * HD
PAIR = 2 * HD
QUAD = 4 * HD
HALF = 256
ROWS = 2 * HALF
PIECE = 80
LATE = (6, 7, 2, 3)
CAM = ("x", "yh")
CHIP = ("yl", "z")
SLAB = ("yl", "z", "core")
EVERY = ("x", "yh", "yl", "z", "core")
SCALE = 1.4426950408889634 / HD**0.5
F32 = jnp.float32
BF16 = jnp.bfloat16
VMEM_LIMIT = 18 * 1024 * 1024


def route(move):
    pairs = []
    for x in range(4):
        for y in range(8):
            for z in range(8):
                for core in range(2):
                    a, b, c = move(x, y, z, core)
                    source = ((x * 8 + y) * 8 + z) * 2 + core
                    pairs.append((source, ((a % 4 * 8 + b % 8) * 8 + c % 8) * 2 + core))
    return pairs


def towards(core):
    return 1 if core else -1


TURNS = (0, 2, 1, 6, 3, 7, 4, 5)


def bring(offset):
    a, b, c = offset
    return route(lambda x, y, z, core: (x + a * towards(core), y + b * towards(core), z + c * towards(core)))


X_NEXT, X_LAST = bring((1, 0, 0)), bring((-1, 0, 0))
Y_NEXT, Y_LAST = bring((0, 1, 0)), bring((0, -1, 0))
Z_NEXT, Z_LAST = bring((0, 0, 1)), bring((0, 0, -1))
ACROSS = route(lambda x, y, z, core: (x, y + 4, z))
ALONG = route(lambda x, y, z, core: (x + (1 if y < 4 else -1), y, z))


def swap_core(block):
    return lax.ppermute(block, "core", [(0, 1), (1, 0)])


def mm(a, b):
    return jnp.dot(a, b, preferred_element_type=F32)


def mm_t(a, b):
    return lax.dot_general(a, b, (((1,), (1,)), ((), ())), preferred_element_type=F32)


def position():
    return [lax.axis_index(axis) for axis in EVERY]


def after(value, *others):
    return lax.optimization_barrier((value,) + others)[0]


def pack_kernel(tokens, w_qkv_hbm, w_out_hbm, out, w_qkv, w_out, pieces, sem):
    loads = [
        pltpu.make_async_copy(w_qkv_hbm, w_qkv, sem.at[0]),
        pltpu.make_async_copy(w_out_hbm, w_out, sem.at[1]),
    ]
    for load in loads:
        load.start()
    for load in loads:
        load.wait()

    def columns(kind, head):
        start = kind * D + head * HD
        return w_qkv[:, start : start + HD].astype(F32)

    for who in range(2):
        a, b, c = 8 + 2 * who, 12 + 2 * who, 4 * who
        content = (
            ((0, a), (0, a + 1)),
            ((0, b), (0, b + 1)),
            ((2, c + 2), (0, c + 3)),
            ((1, c + 3), (2, c + 3)),
            ((1, a), (1, a + 1), (2, a), (2, a + 1)),
            ((1, b), (1, b + 1), (2, b), (2, b + 1)),
            ((0, c), (1, c), (2, c), (0, c + 1)),
            ((1, c + 1), (2, c + 1), (0, c + 2), (1, c + 2)),
        )
        for colour in range(8):
            parts = [columns(*one) for one in content[colour]]
            if colour < 4:
                start = (who * 4 + colour) * PAIR
                parts = [w_out[:, start : start + PAIR].astype(F32)] + parts
            whole = jnp.concatenate(parts, 1)
            place = who * 8 + colour
            pieces[place, :18] = whole[:, :128]
            pieces[place, 18:36] = whole[:, 128:256]
            tail = whole[:, 256:]
            pieces[place, 36:41] = jnp.concatenate([tail[:5], tail[5:10], tail[9:14], tail[13:18]], 1)
            pieces[place, 41:] = jnp.zeros((3, 128), F32)
    x, yh = position()[:2]
    base = 2 * x + 4 * yh
    for dest in range(64):
        colour = (base + dest // 16 + 3 * (dest // 2 % 8)) % 8
        block = tokens[dest // 2 * 8 : dest // 2 * 8 + 8].astype(F32)
        block = block[dest % 2 * 4 : dest % 2 * 4 + 4]
        rows = [block[:, tile * 128 : tile * 128 + 128] for tile in range(9)]
        rows = [pieces[dest % 2 * 8 + colour]] + rows
        out[dest] = jnp.concatenate(rows, 0).astype(BF16)


def unpack_kernel(got, block, block_out, tokens_out, tokens, wide, sem):
    for source in range(64):
        rows = got[source].astype(F32)
        at = source * 18
        wide[0, at : at + 18] = rows[:18]
        wide[1, at : at + 18] = rows[18:36]
        wide[2, at : at + 5, :32] = rows[36:41, :32]
        wide[2, at + 5 : at + 10, :32] = rows[36:41, 32:64]
        wide[2, at + 10 : at + 14, :32] = rows[37:41, 64:96]
        wide[2, at + 14 : at + 18, :32] = rows[37:41, 96:]
        if source % 2 == 1:
            pair = [got[source - 1].astype(F32), rows]
            tiles = []
            for tile in range(9):
                start = 44 + tile * 4
                tiles.append(jnp.concatenate([one[start : start + 4] for one in pair], 0))
            tokens[source * 4 - 4 : source * 4 + 4] = jnp.concatenate(tiles, 1).astype(BF16)
    block[:128] = wide[0].T.astype(BF16)
    block[128:256] = wide[1].T.astype(BF16)
    block[256:] = wide[2].T[:32].astype(BF16)
    stores = [
        pltpu.make_async_copy(block, block_out, sem.at[0]),
        pltpu.make_async_copy(tokens, tokens_out, sem.at[1]),
    ]
    for store in stores:
        store.start()
    for store in stores:
        store.wait()


def own_embed(cam_embed):
    return cam_embed[pl.ds(lax.axis_index("x") * 2 + lax.axis_index("yh"), 1)]


def normalise(ref, embed, gain):
    hidden = ref[...].astype(F32) + embed
    centred = hidden - jnp.mean(hidden, -1, keepdims=True)
    variance = jnp.mean(centred * centred, -1, keepdims=True)
    return (centred * lax.rsqrt(variance + 1e-06) * gain[...]).astype(BF16)


def norm_kernel(own, other, cam_embed, gain, out):
    for i, ref in enumerate((own, other)):
        out[i * HALF : (i + 1) * HALF] = normalise(ref, own_embed(cam_embed), gain)


def start_fetch(blocks, colour, slot, sem):
    x, yh, yl, z, core = position()
    ahead = colour - (2 * x + 4 * yh + yl + 3 * z) + 64
    turn = lax.rem(jnp.where(core == 0, ahead, 128 - ahead), 8)
    for block, own in zip(blocks, TURNS):
        @pl.when(turn == own)
        def _(block=block):
            pltpu.make_async_copy(block, slot, sem).start()


def wait_fetch(blocks, slot, sem):
    pltpu.make_async_copy(blocks[0], slot, sem).wait()


def head_norm(part, gain):
    shaped = part.reshape(part.shape[0] // HD, HD, part.shape[1])
    mean_sq = jnp.mean(shaped * shaped, 1, keepdims=True)
    return (shaped * lax.rsqrt(mean_sq + 1e-06)).reshape(part.shape) * gain


def attend(q_t, sides, mask=None):
    total = None
    for k_t, v_t in sides:
        scores = mm(k_t.T.astype(BF16), q_t.astype(BF16))
        expd = jnp.exp2(scores * SCALE)
        if mask is not None:
            expd = jnp.where(mask, expd, 0.0)
        wide = jnp.concatenate([v_t, jnp.ones((8, v_t.shape[1]), F32)], 0).astype(BF16)
        part = mm(wide, expd.astype(BF16))
        total = part if total is None else total + part
    return total[:HD] / total[HD : HD + 1]


def project_pair(normed, w_q, w_kv, gain):
    q = head_norm(mm_t(w_q, normed[...]), gain[:PAIR])
    kv = mm_t(w_kv, normed[...])
    return q, head_norm(kv[:PAIR], gain[PAIR:]), kv[PAIR:]


def cross_project_kernel(gains, normed, *refs):
    blocks, (q_out, kv_t, w_out, early, late, q_t, weight, sem) = refs[:8], refs[8:]
    slots = {0: weight.at[0], 4: weight.at[1], 1: early.at[0], 5: early.at[1]}
    slots.update({colour: late.at[place] for place, colour in enumerate(LATE)})
    for colour, slot in slots.items():
        start_fetch(blocks, colour, slot, sem.at[colour])
    parts = [block.at[pl.ds(0, PAIR)] for block in blocks]
    thirds = [w_out.at[pl.ds(colour * PAIR, PAIR)] for colour in range(4)]
    for colour in range(4):
        start_fetch(parts, colour, thirds[colour], sem.at[8 + colour])
    for colour in (0, 4):
        wait_fetch(blocks, slots[colour], sem.at[colour])
    q, k, v = project_pair(normed, weight[0, PAIR:], weight[1], gains[...].T[:, :1])
    kv_t[...] = jnp.concatenate([k, v], 0).astype(BF16)
    q_t[...] = q.astype(BF16)
    store = pltpu.make_async_copy(q_t, q_out, sem.at[12])
    store.start()
    for colour in (1, 5) + LATE:
        wait_fetch(blocks, slots[colour], sem.at[colour])
    for colour in range(4):
        wait_fetch(parts, thirds[colour], sem.at[8 + colour])
    store.wait()


def time_kernel(gains, normed, weight, out):
    q, k, v = project_pair(normed, weight[0, PAIR:], weight[1], gains[...].T[:, 1:2])
    row = lax.broadcasted_iota(jnp.int32, (HALF, HALF), 0) % 8
    col = lax.broadcasted_iota(jnp.int32, (HALF, HALF), 1) % 8
    sets = []
    for i in range(2):
        part = slice(i * HALF, (i + 1) * HALF)
        heads = []
        for head in range(2):
            at = head * HD
            side = (k[at : at + HD, part], v[at : at + HD, part])
            heads.append(attend(q[at : at + HD, part], [side], row == col))
        sets.append(jnp.concatenate(heads, 0).T.reshape(64, 4, PAIR))
    swap = lax.axis_index("core") == 1
    one = jnp.where(swap, sets[1], sets[0])
    two = jnp.where(swap, sets[0], sets[1])
    out[...] = jnp.concatenate([one, two], 1).reshape(32, 16, PAIR).astype(BF16)


def space_kernel(gains, normed_hbm, weight_hbm, out, normed, result, weight, sem):
    loads = [pltpu.make_async_copy(weight_hbm.at[slot], weight.at[slot], sem.at[slot]) for slot in range(4)]
    loads.insert(0, pltpu.make_async_copy(normed_hbm, normed, sem.at[4]))
    for load in loads:
        load.start()
    columns = gains[...].T[:PAIR]
    loads[0].wait()
    rows = []
    for slot in range(4):
        loads[1 + slot].wait()
        projected = mm_t(weight[slot, (PAIR if slot > 1 else 0) :], normed[...])
        rows += [projected[at : at + HD] for at in range(0, projected.shape[0], HD)]
    heads = []
    for head in range(4):
        q, k, v = rows[3 * head : 3 * head + 3]
        gain = columns[:, 2 + head : 3 + head]
        q, k = head_norm(q, gain[:HD]), head_norm(k, gain[HD:])
        heads.append(attend(q, [(k, v)]))
    result[...] = jnp.concatenate(heads, 0).astype(BF16)
    store = pltpu.make_async_copy(result, out, sem.at[5])
    store.start()
    store.wait()


def cross_kernel(kv_a, kv_b, timed, space_hbm, q_hbm, keep, give, space, q_t, sem):
    loads = [pltpu.make_async_copy(q_hbm, q_t, sem.at[0]), pltpu.make_async_copy(space_hbm, space, sem.at[1])]
    for load in loads:
        load.start()
    both = [ref[...].astype(F32) for ref in (kv_a, kv_b)]
    loads[0].wait()
    query = q_t[...].astype(F32)
    heads = []
    for head in range(2):
        at = head * HD
        sides = [(kv[at : at + HD], kv[PAIR + at : PAIR + at + HD]) for kv in both]
        heads.append(attend(query[at : at + HD], sides))
    loads[1].wait()
    mixed = jnp.concatenate([space[...].astype(F32)] + heads, 0).T
    late = timed[...].astype(F32)
    late = [late[:, i * 8 : i * 8 + 8].reshape(HALF, PAIR) for i in range(2)]
    swap = lax.axis_index("core") == 1
    keep[...] = jnp.concatenate([mixed[:HALF], jnp.where(swap, late[1], late[0])], 1).astype(BF16)
    give[...] = jnp.concatenate([mixed[HALF:], jnp.where(swap, late[0], late[1])], 1).astype(BF16)


def out_kernel(tokens, own, arrived, w_own, w_other, embed_hbm, out, cam_embed, sem):
    load = pltpu.make_async_copy(embed_hbm, cam_embed, sem)
    load.start()
    swap = lax.axis_index("core") == 1
    mine, theirs = own[...].astype(F32), arrived[...].astype(F32)
    first = jnp.where(swap, theirs, mine)
    second = jnp.where(swap, mine, theirs)
    parts = []
    for start, end in ((0, 2 * PAIR), (2 * PAIR, 3 * PAIR), (3 * PAIR, 4 * PAIR)):
        parts += [first[:, start:end], second[:, start:end]]
    mixed = jnp.concatenate(parts, 1).astype(BF16)
    one, two = mm_t(mixed, w_own[...]), mm_t(mixed, w_other[...])
    update = jnp.concatenate([jnp.where(swap, two, one), jnp.where(swap, one, two)], 1)
    load.wait()
    out[...] = (tokens[...].astype(F32) + own_embed(cam_embed) + update).astype(BF16)


def call(kernel, out_shapes, args, scratch=(), flops=0, anys=0, room=VMEM_LIMIT):
    vmem = pl.BlockSpec(memory_space=pltpu.VMEM)
    hbm = pl.BlockSpec(memory_space=pltpu.HBM)
    specs = []
    for i in range(len(args)):
        specs.append(hbm if i >= len(args) - anys else vmem)

    def place(out):
        return hbm if getattr(out, "memory_space", None) == pltpu.HBM else vmem

    single = not isinstance(out_shapes, tuple)
    return pl.pallas_call(
        kernel,
        out_shape=out_shapes,
        in_specs=specs,
        out_specs=place(out_shapes) if single else tuple(place(out) for out in out_shapes),
        scratch_shapes=list(scratch),
        compiler_params=pltpu.CompilerParams(vmem_limit_bytes=room),
        cost_estimate=pl.CostEstimate(flops=flops, bytes_accessed=1, transcendentals=0),
    )(*args)


def shape(*dims):
    return jax.ShapeDtypeStruct(dims, BF16)


def far(*dims):
    return pltpu.HBM(dims, BF16)


def near(*dims):
    return pltpu.VMEM(dims, BF16)


def keep_near(array):
    return pltpu.with_memory_space_constraint(array, pltpu.VMEM)


def stay(array):
    return pltpu.with_memory_space_constraint(array, pltpu.HBM)


def local(frames_in, cam_embed, norm_gain, q_gain, k_gain, w_qkv, w_out):
    tokens = frames_in[0]
    core = lax.axis_index("core")
    gain = norm_gain[None]
    both = jnp.stack([q_gain.reshape(HEADS, HD), k_gain.reshape(HEADS, HD)], 1)

    def gains_of(head, count):
        return lax.dynamic_slice_in_dim(both, head, count, 0)

    pair_gains = jnp.stack([gains_of(8 + 2 * core, 2), gains_of(12 + 2 * core, 2)])
    pair_gains = pair_gains.transpose(0, 2, 1, 3).reshape(2, 2 * PAIR)
    space_gains = gains_of(4 * core, 4).reshape(4, PAIR)
    gains = jnp.concatenate([pair_gains, jnp.pad(space_gains, ((0, 2), (0, PAIR)))], 0)

    pieces = call(
        pack_kernel,
        shape(64, PIECE, 128),
        (tokens, w_qkv, w_out),
        [
            pltpu.VMEM((18, 3 * D), BF16),
            pltpu.VMEM((18, D), BF16),
            pltpu.VMEM((16, 44, 128), F32),
            pltpu.SemaphoreType.DMA((2,)),
        ],
        0,
        2,
        58 * 1024 * 1024,
    )
    got = lax.all_to_all(pieces, SLAB, 0, 0, tiled=True)
    other = swap_core(tokens)
    normed = keep_near(call(norm_kernel, near(ROWS, D), (tokens, other, cam_embed, gain), (), 8 * 10**9))
    own_block, block, time_own = call(
        unpack_kernel,
        (near(QUAD, D), far(QUAD, D), far(HALF, D)),
        (after(got, normed, gains),),
        [
            pltpu.VMEM((HALF, D), BF16),
            pltpu.VMEM((3, D, 128), F32),
            pltpu.SemaphoreType.DMA((2,)),
        ],
    )
    blocks = [keep_near(own_block)]
    for way in (X_NEXT, Y_NEXT, X_LAST, Z_NEXT, Y_LAST, None, Z_LAST):
        if way is None:
            blocks.append(lax.ppermute(blocks[1], EVERY, X_NEXT))
        else:
            blocks.append(lax.ppermute(block, EVERY, way))
    blocks = tuple(blocks)
    time_other = swap_core(time_own)
    time_normed = keep_near(call(norm_kernel, near(ROWS, D), (time_own, time_other, cam_embed, gain), (), 8 * 10**9))
    q_t, kv_t, w_own, early, late = call(
        cross_project_kernel,
        (far(PAIR, ROWS), shape(2 * PAIR, ROWS), near(4 * PAIR, D), near(2, QUAD, D), far(4, QUAD, D)),
        (gains, normed) + blocks,
        [pltpu.VMEM((PAIR, ROWS), BF16), pltpu.VMEM((2, QUAD, D), BF16), pltpu.SemaphoreType.DMA((13,))],
        0,
        8,
    )
    kv_a = lax.ppermute(kv_t, EVERY, ACROSS)
    w_other = swap_core(w_own)
    timed = call(time_kernel, shape(32, 16, PAIR), (gains, after(time_normed, kv_t), keep_near(early)))
    kv_b = lax.ppermute(after(kv_a, timed), EVERY, ALONG)
    space = call(
        space_kernel,
        far(2 * PAIR, ROWS),
        (gains, stay(after(normed, timed)), stay(late)),
        [
            pltpu.VMEM((ROWS, D), BF16),
            pltpu.VMEM((2 * PAIR, ROWS), BF16),
            pltpu.VMEM((4, QUAD, D), BF16),
            pltpu.SemaphoreType.DMA((6,)),
        ],
        16 * 10**9,
        2,
    )
    returned = lax.all_to_all(timed, CHIP, 0, 0, tiled=True)
    keep, give = call(
        cross_kernel,
        (shape(HALF, 4 * PAIR), shape(HALF, 4 * PAIR)),
        (kv_a, kv_b, returned, stay(space), stay(q_t)),
        [pltpu.VMEM((2 * PAIR, ROWS), BF16), pltpu.VMEM((PAIR, ROWS), BF16), pltpu.SemaphoreType.DMA((2,))],
        0,
        2,
    )
    arrived = swap_core(give)
    return call(
        out_kernel,
        shape(HALF, D),
        (tokens, keep, arrived, w_own, w_other, stay(cam_embed)),
        [pltpu.VMEM((8, D), F32), pltpu.SemaphoreType.DMA],
        0,
        1,
    )[None]


def solution(mesh):
    fine = Mesh(mesh.devices.reshape(4, 2, 4, 8, 2), EVERY)
    placed = (P(CAM, SLAB, None), P(), P(), P(), P(), P(SLAB, None), P(SLAB, None))
    return jax.shard_map(local, mesh=fine, in_specs=placed, out_specs=P(CAM, SLAB, None), check_vma=False)
```

```python
import jax
import jax.numpy as jnp
from jax import lax
from jax.experimental import pallas as pl
from jax.experimental.pallas import tpu as pltpu
from jax.sharding import Mesh
from jax.sharding import PartitionSpec as P

HEADS = 16
HD = 72
D = HEADS * HD
PAIR = 2 * HD
QUAD = 4 * HD
HALF = 256
ROWS = 2 * HALF
PIECE = 80
LATE = (6, 7, 2, 3)
CAM = ("x", "yh")
CHIP = ("yl", "z")
SLAB = ("yl", "z", "core")
EVERY = ("x", "yh", "yl", "z", "core")
SCALE = 1.4426950408889634 / HD**0.5
F32 = jnp.float32
BF16 = jnp.bfloat16
VMEM_LIMIT = 18 * 1024 * 1024


def route(move):
    pairs = []
    for x in range(4):
        for y in range(8):
            for z in range(8):
                for core in range(2):
                    a, b, c = move(x, y, z, core)
                    source = ((x * 8 + y) * 8 + z) * 2 + core
                    pairs.append((source, ((a % 4 * 8 + b % 8) * 8 + c % 8) * 2 + core))
    return pairs


def towards(core):
    return 1 if core else -1


TURNS = (0, 2, 1, 6, 3, 7, 4, 5)


def bring(offset):
    a, b, c = offset
    return route(lambda x, y, z, core: (x + a * towards(core), y + b * towards(core), z + c * towards(core)))


X_NEXT, X_LAST = bring((1, 0, 0)), bring((-1, 0, 0))
Y_NEXT, Y_LAST = bring((0, 1, 0)), bring((0, -1, 0))
Z_NEXT, Z_LAST = bring((0, 0, 1)), bring((0, 0, -1))
ACROSS = route(lambda x, y, z, core: (x, y + 4, z))
ALONG = route(lambda x, y, z, core: (x + (1 if y < 4 else -1), y, z))


def swap_core(block):
    return lax.ppermute(block, "core", [(0, 1), (1, 0)])


def mm(a, b):
    return jnp.dot(a, b, preferred_element_type=F32)


def mm_t(a, b):
    return lax.dot_general(a, b, (((1,), (1,)), ((), ())), preferred_element_type=F32)


def position():
    return [lax.axis_index(axis) for axis in EVERY]


def after(value, *others):
    return lax.optimization_barrier((value,) + others)[0]


def pack_kernel(w_qkv_hbm, w_out_hbm, tokens_hbm, out, w_qkv, w_out, tokens, pieces, staged, sem):
    loads = [
        pltpu.make_async_copy(w_qkv_hbm, w_qkv, sem.at[0]),
        pltpu.make_async_copy(w_out_hbm, w_out, sem.at[1]),
        pltpu.make_async_copy(tokens_hbm, tokens, sem.at[2]),
    ]
    for load in loads:
        load.start()
    for load in loads[:2]:
        load.wait()

    def columns(kind, head):
        start = kind * D + head * HD
        return w_qkv[:, start : start + HD].astype(F32)

    for who in range(2):
        a, b, c = 8 + 2 * who, 12 + 2 * who, 4 * who
        content = (
            ((0, a), (0, a + 1)),
            ((0, b), (0, b + 1)),
            ((2, c + 2), (0, c + 3)),
            ((1, c + 3), (2, c + 3)),
            ((1, a), (1, a + 1), (2, a), (2, a + 1)),
            ((1, b), (1, b + 1), (2, b), (2, b + 1)),
            ((0, c), (1, c), (2, c), (0, c + 1)),
            ((1, c + 1), (2, c + 1), (0, c + 2), (1, c + 2)),
        )
        for colour in range(8):
            parts = [columns(*one) for one in content[colour]]
            if colour < 4:
                start = (who * 4 + colour) * PAIR
                parts = [w_out[:, start : start + PAIR].astype(F32)] + parts
            whole = jnp.concatenate(parts, 1)
            place = who * 8 + colour
            pieces[place, :18] = whole[:, :128]
            pieces[place, 18:36] = whole[:, 128:256]
            tail = whole[:, 256:]
            pieces[place, 36:41] = jnp.concatenate([tail[:5], tail[5:10], tail[9:14], tail[13:18]], 1)
            pieces[place, 41:] = jnp.zeros((3, 128), F32)
    x, yh = position()[:2]
    base = 2 * x + 4 * yh
    loads[2].wait()
    stores = []
    for dest in range(64):
        colour = (base + dest // 16 + 3 * (dest // 2 % 8)) % 8
        block = tokens[dest // 2 * 8 : dest // 2 * 8 + 8].astype(F32)
        block = block[dest % 2 * 4 : dest % 2 * 4 + 4]
        rows = [block[:, tile * 128 : tile * 128 + 128] for tile in range(9)]
        rows = [pieces[dest % 2 * 8 + colour]] + rows
        staged[dest] = jnp.concatenate(rows, 0).astype(BF16)
        stores.append(pltpu.make_async_copy(staged.at[dest], out.at[dest], sem.at[3]))
        stores[-1].start()
    for store in stores:
        store.wait()


def unpack_kernel(got, block, block_out, tokens_out, tokens, wide, sem):
    for source in range(64):
        rows = got[source].astype(F32)
        at = source * 18
        wide[0, at : at + 18] = rows[:18]
        wide[1, at : at + 18] = rows[18:36]
        wide[2, at : at + 5, :32] = rows[36:41, :32]
        wide[2, at + 5 : at + 10, :32] = rows[36:41, 32:64]
        wide[2, at + 10 : at + 14, :32] = rows[37:41, 64:96]
        wide[2, at + 14 : at + 18, :32] = rows[37:41, 96:]
        if source % 2 == 1:
            pair = [got[source - 1].astype(F32), rows]
            tiles = []
            for tile in range(9):
                start = 44 + tile * 4
                tiles.append(jnp.concatenate([one[start : start + 4] for one in pair], 0))
            tokens[source * 4 - 4 : source * 4 + 4] = jnp.concatenate(tiles, 1).astype(BF16)
    block[:128] = wide[0].T.astype(BF16)
    block[128:256] = wide[1].T.astype(BF16)
    block[256:] = wide[2].T[:32].astype(BF16)
    stores = [
        pltpu.make_async_copy(block, block_out, sem.at[0]),
        pltpu.make_async_copy(tokens, tokens_out, sem.at[1]),
    ]
    for store in stores:
        store.start()
    for store in stores:
        store.wait()


def own_embed(cam_embed):
    return cam_embed[pl.ds(lax.axis_index("x") * 2 + lax.axis_index("yh"), 1)]


def normalise(ref, embed, gain):
    hidden = ref[...].astype(F32) + embed
    centred = hidden - jnp.mean(hidden, -1, keepdims=True)
    variance = jnp.mean(centred * centred, -1, keepdims=True)
    return (centred * lax.rsqrt(variance + 1e-06) * gain[...]).astype(BF16)


def norm_kernel(own, other, cam_embed, gain, out):
    for i, ref in enumerate((own, other)):
        out[i * HALF : (i + 1) * HALF] = normalise(ref, own_embed(cam_embed), gain)


def start_fetch(blocks, colour, slot, sem):
    x, yh, yl, z, core = position()
    ahead = colour - (2 * x + 4 * yh + yl + 3 * z) + 64
    turn = lax.rem(jnp.where(core == 0, ahead, 128 - ahead), 8)
    for block, own in zip(blocks, TURNS):
        @pl.when(turn == own)
        def _(block=block):
            pltpu.make_async_copy(block, slot, sem).start()


def wait_fetch(blocks, slot, sem):
    pltpu.make_async_copy(blocks[0], slot, sem).wait()


def head_norm(part, gain):
    shaped = part.reshape(part.shape[0] // HD, HD, part.shape[1])
    mean_sq = jnp.mean(shaped * shaped, 1, keepdims=True)
    return (shaped * lax.rsqrt(mean_sq + 1e-06)).reshape(part.shape) * gain


def attend(q_t, sides, mask=None):
    total = None
    for k_t, v_t in sides:
        scores = mm(k_t.T.astype(BF16), q_t.astype(BF16))
        expd = jnp.exp2(scores * SCALE)
        if mask is not None:
            expd = jnp.where(mask, expd, 0.0)
        wide = jnp.concatenate([v_t, jnp.ones((8, v_t.shape[1]), F32)], 0).astype(BF16)
        part = mm(wide, expd.astype(BF16))
        total = part if total is None else total + part
    return total[:HD] / total[HD : HD + 1]


def project_pair(normed, w_q, w_kv, gain):
    q = head_norm(mm_t(w_q, normed[...]), gain[:PAIR])
    kv = mm_t(w_kv, normed[...])
    return q, head_norm(kv[:PAIR], gain[PAIR:]), kv[PAIR:]


def cross_project_kernel(gains, normed, *refs):
    blocks, (q_out, kv_t, w_out, early, late, q_t, weight, sem) = refs[:8], refs[8:]
    slots = {0: weight.at[0], 4: weight.at[1], 1: early.at[0], 5: early.at[1]}
    slots.update({colour: late.at[place] for place, colour in enumerate(LATE)})
    for colour, slot in slots.items():
        start_fetch(blocks, colour, slot, sem.at[colour])
    parts = [block.at[pl.ds(0, PAIR)] for block in blocks]
    thirds = [w_out.at[pl.ds(colour * PAIR, PAIR)] for colour in range(4)]
    for colour in range(4):
        start_fetch(parts, colour, thirds[colour], sem.at[8 + colour])
    for colour in (0, 4):
        wait_fetch(blocks, slots[colour], sem.at[colour])
    q, k, v = project_pair(normed, weight[0, PAIR:], weight[1], gains[...].T[:, :1])
    kv_t[...] = jnp.concatenate([k, v], 0).astype(BF16)
    q_t[...] = q.astype(BF16)
    store = pltpu.make_async_copy(q_t, q_out, sem.at[12])
    store.start()
    for colour in (1, 5) + LATE:
        wait_fetch(blocks, slots[colour], sem.at[colour])
    for colour in range(4):
        wait_fetch(parts, thirds[colour], sem.at[8 + colour])
    store.wait()


def time_kernel(gains, normed, weight, late, out, late_out, sem):
    store = pltpu.make_async_copy(late, late_out, sem)
    store.start()
    q, k, v = project_pair(normed, weight[0, PAIR:], weight[1], gains[...].T[:, 1:2])
    row = lax.broadcasted_iota(jnp.int32, (HALF, HALF), 0) % 8
    col = lax.broadcasted_iota(jnp.int32, (HALF, HALF), 1) % 8
    sets = []
    for i in range(2):
        part = slice(i * HALF, (i + 1) * HALF)
        heads = []
        for head in range(2):
            at = head * HD
            side = (k[at : at + HD, part], v[at : at + HD, part])
            heads.append(attend(q[at : at + HD, part], [side], row == col))
        sets.append(jnp.concatenate(heads, 0).T.reshape(64, 4, PAIR))
    swap = lax.axis_index("core") == 1
    one = jnp.where(swap, sets[1], sets[0])
    two = jnp.where(swap, sets[0], sets[1])
    out[...] = jnp.concatenate([one, two], 1).reshape(32, 16, PAIR).astype(BF16)
    store.wait()


def space_kernel(gains, normed_hbm, weight_hbm, out, normed, result, weight, sem):
    loads = [pltpu.make_async_copy(weight_hbm.at[slot], weight.at[slot], sem.at[slot]) for slot in range(4)]
    loads.insert(0, pltpu.make_async_copy(normed_hbm, normed, sem.at[4]))
    for load in loads:
        load.start()
    columns = gains[...].T[:PAIR]
    loads[0].wait()
    rows = []
    for slot in range(4):
        loads[1 + slot].wait()
        projected = mm_t(weight[slot, (PAIR if slot > 1 else 0) :], normed[...])
        rows += [projected[at : at + HD] for at in range(0, projected.shape[0], HD)]
    heads = []
    for head in range(4):
        q, k, v = rows[3 * head : 3 * head + 3]
        gain = columns[:, 2 + head : 3 + head]
        q, k = head_norm(q, gain[:HD]), head_norm(k, gain[HD:])
        heads.append(attend(q, [(k, v)]))
    result[...] = jnp.concatenate(heads, 0).astype(BF16)
    store = pltpu.make_async_copy(result, out, sem.at[5])
    store.start()
    store.wait()


def cross_kernel(kv_a, kv_b, timed, space_hbm, q_hbm, keep, give, space, q_t, sem):
    loads = [pltpu.make_async_copy(q_hbm, q_t, sem.at[0]), pltpu.make_async_copy(space_hbm, space, sem.at[1])]
    for load in loads:
        load.start()
    both = [ref[...].astype(F32) for ref in (kv_a, kv_b)]
    loads[0].wait()
    query = q_t[...].astype(F32)
    heads = []
    for head in range(2):
        at = head * HD
        sides = [(kv[at : at + HD], kv[PAIR + at : PAIR + at + HD]) for kv in both]
        heads.append(attend(query[at : at + HD], sides))
    loads[1].wait()
    mixed = jnp.concatenate([space[...].astype(F32)] + heads, 0).T
    late = timed[...].astype(F32)
    late = [late[:, i * 8 : i * 8 + 8].reshape(HALF, PAIR) for i in range(2)]
    swap = lax.axis_index("core") == 1
    keep[...] = jnp.concatenate([mixed[:HALF], jnp.where(swap, late[1], late[0])], 1).astype(BF16)
    give[...] = jnp.concatenate([mixed[HALF:], jnp.where(swap, late[0], late[1])], 1).astype(BF16)


def out_kernel(tokens, own, arrived, w_own, w_other, embed_hbm, out, cam_embed, sem):
    load = pltpu.make_async_copy(embed_hbm, cam_embed, sem)
    load.start()
    swap = lax.axis_index("core") == 1
    mine, theirs = own[...].astype(F32), arrived[...].astype(F32)
    first = jnp.where(swap, theirs, mine)
    second = jnp.where(swap, mine, theirs)
    parts = []
    for start, end in ((0, 2 * PAIR), (2 * PAIR, 3 * PAIR), (3 * PAIR, 4 * PAIR)):
        parts += [first[:, start:end], second[:, start:end]]
    mixed = jnp.concatenate(parts, 1).astype(BF16)
    one, two = mm_t(mixed, w_own[...]), mm_t(mixed, w_other[...])
    update = jnp.concatenate([jnp.where(swap, two, one), jnp.where(swap, one, two)], 1)
    load.wait()
    out[...] = (tokens[...].astype(F32) + own_embed(cam_embed) + update).astype(BF16)


def call(kernel, out_shapes, args, scratch=(), flops=0, anys=0, room=VMEM_LIMIT):
    vmem = pl.BlockSpec(memory_space=pltpu.VMEM)
    hbm = pl.BlockSpec(memory_space=pltpu.HBM)
    specs = []
    for i in range(len(args)):
        specs.append(hbm if i >= len(args) - anys else vmem)

    def place(out):
        return hbm if getattr(out, "memory_space", None) == pltpu.HBM else vmem

    single = not isinstance(out_shapes, tuple)
    return pl.pallas_call(
        kernel,
        out_shape=out_shapes,
        in_specs=specs,
        out_specs=place(out_shapes) if single else tuple(place(out) for out in out_shapes),
        scratch_shapes=list(scratch),
        compiler_params=pltpu.CompilerParams(vmem_limit_bytes=room),
        cost_estimate=pl.CostEstimate(flops=flops, bytes_accessed=1, transcendentals=0),
    )(*args)


def shape(*dims):
    return jax.ShapeDtypeStruct(dims, BF16)


def far(*dims):
    return pltpu.HBM(dims, BF16)


def near(*dims):
    return pltpu.VMEM(dims, BF16)


def keep_near(array):
    return pltpu.with_memory_space_constraint(array, pltpu.VMEM)


def stay(array):
    return pltpu.with_memory_space_constraint(array, pltpu.HBM)


def local(frames_in, cam_embed, norm_gain, q_gain, k_gain, w_qkv, w_out):
    tokens = frames_in[0]
    core = lax.axis_index("core")
    gain = norm_gain[None]
    both = jnp.stack([q_gain.reshape(HEADS, HD), k_gain.reshape(HEADS, HD)], 1)

    def gains_of(head, count):
        return lax.dynamic_slice_in_dim(both, head, count, 0)

    pair_gains = jnp.stack([gains_of(8 + 2 * core, 2), gains_of(12 + 2 * core, 2)])
    pair_gains = pair_gains.transpose(0, 2, 1, 3).reshape(2, 2 * PAIR)
    space_gains = gains_of(4 * core, 4).reshape(4, PAIR)
    gains = jnp.concatenate([pair_gains, jnp.pad(space_gains, ((0, 2), (0, PAIR)))], 0)

    pieces = call(
        pack_kernel,
        far(64, PIECE, 128),
        (w_qkv, w_out, tokens),
        [
            pltpu.VMEM((18, 3 * D), BF16),
            pltpu.VMEM((18, D), BF16),
            pltpu.VMEM((HALF, D), BF16),
            pltpu.VMEM((16, 44, 128), F32),
            pltpu.VMEM((64, PIECE, 128), BF16),
            pltpu.SemaphoreType.DMA((4,)),
        ],
        0,
        3,
        58 * 1024 * 1024,
    )
    got = lax.all_to_all(pieces, SLAB, 0, 0, tiled=True)
    other = swap_core(tokens)
    normed = keep_near(call(norm_kernel, near(ROWS, D), (tokens, other, cam_embed, gain), (), 8 * 10**9))
    own_block, block, time_own = call(
        unpack_kernel,
        (near(QUAD, D), far(QUAD, D), far(HALF, D)),
        (after(got, normed, gains),),
        [
            pltpu.VMEM((HALF, D), BF16),
            pltpu.VMEM((3, D, 128), F32),
            pltpu.SemaphoreType.DMA((2,)),
        ],
    )
    blocks = [keep_near(own_block)]
    for way in (X_NEXT, Y_NEXT, X_LAST, Z_NEXT, Y_LAST, None, Z_LAST):
        if way is None:
            blocks.append(lax.ppermute(blocks[1], EVERY, X_NEXT))
        else:
            blocks.append(lax.ppermute(block, EVERY, way))
    blocks = tuple(blocks)
    time_other = swap_core(time_own)
    time_normed = keep_near(call(norm_kernel, near(ROWS, D), (time_own, time_other, cam_embed, gain), (), 8 * 10**9))
    q_t, kv_t, w_own, early, late = call(
        cross_project_kernel,
        (far(PAIR, ROWS), shape(2 * PAIR, ROWS), near(4 * PAIR, D), near(2, QUAD, D), near(4, QUAD, D)),
        (gains, normed) + blocks,
        [pltpu.VMEM((PAIR, ROWS), BF16), pltpu.VMEM((2, QUAD, D), BF16), pltpu.SemaphoreType.DMA((13,))],
        0,
        8,
    )
    kv_a = lax.ppermute(kv_t, EVERY, ACROSS)
    w_other = keep_near(swap_core(w_own))
    timed, late = call(
        time_kernel,
        (shape(32, 16, PAIR), far(4, QUAD, D)),
        (gains, after(time_normed, kv_t), keep_near(early), keep_near(late)),
        [pltpu.SemaphoreType.DMA],
    )
    kv_b = lax.ppermute(after(kv_a, timed), EVERY, ALONG)
    space = call(
        space_kernel,
        far(2 * PAIR, ROWS),
        (gains, stay(after(normed, timed)), stay(late)),
        [
            pltpu.VMEM((ROWS, D), BF16),
            pltpu.VMEM((2 * PAIR, ROWS), BF16),
            pltpu.VMEM((4, QUAD, D), BF16),
            pltpu.SemaphoreType.DMA((6,)),
        ],
        16 * 10**9,
        2,
    )
    returned = lax.all_to_all(timed, CHIP, 0, 0, tiled=True)
    keep, give = call(
        cross_kernel,
        (shape(HALF, 4 * PAIR), shape(HALF, 4 * PAIR)),
        (kv_a, kv_b, returned, stay(space), stay(q_t)),
        [pltpu.VMEM((2 * PAIR, ROWS), BF16), pltpu.VMEM((PAIR, ROWS), BF16), pltpu.SemaphoreType.DMA((2,))],
        0,
        2,
    )
    arrived = swap_core(give)
    return call(
        out_kernel,
        shape(HALF, D),
        (tokens, keep, arrived, w_own, w_other, stay(cam_embed)),
        [pltpu.VMEM((8, D), F32), pltpu.SemaphoreType.DMA],
        0,
        1,
    )[None]


def solution(mesh):
    fine = Mesh(mesh.devices.reshape(4, 2, 4, 8, 2), EVERY)
    placed = (P(CAM, SLAB, None), P(), P(), P(), P(), P(SLAB, None), P(SLAB, None))
    return jax.shard_map(local, mesh=fine, in_specs=placed, out_specs=P(CAM, SLAB, None), check_vma=False)
```

```python
import jax
import jax.numpy as jnp
from jax import lax
from jax.experimental import pallas as pl
from jax.experimental.pallas import tpu as pltpu
from jax.sharding import Mesh
from jax.sharding import PartitionSpec as P

HEADS = 16
HD = 72
D = HEADS * HD
PAIR = 2 * HD
QUAD = 4 * HD
HALF = 256
ROWS = 2 * HALF
PIECE = 80
LATE = (6, 7, 2, 3)
CAM = ("x", "yh")
CHIP = ("yl", "z")
SLAB = ("yl", "z", "core")
EVERY = ("x", "yh", "yl", "z", "core")
SCALE = 1.4426950408889634 / HD**0.5
F32 = jnp.float32
BF16 = jnp.bfloat16
VMEM_LIMIT = 18 * 1024 * 1024


def route(move):
    pairs = []
    for x in range(4):
        for y in range(8):
            for z in range(8):
                for core in range(2):
                    a, b, c = move(x, y, z, core)
                    source = ((x * 8 + y) * 8 + z) * 2 + core
                    pairs.append((source, ((a % 4 * 8 + b % 8) * 8 + c % 8) * 2 + core))
    return pairs


def towards(core):
    return 1 if core else -1


TURNS = (0, 2, 1, 6, 3, 7, 4, 5)


def bring(offset):
    a, b, c = offset
    return route(lambda x, y, z, core: (x + a * towards(core), y + b * towards(core), z + c * towards(core)))


X_NEXT, X_LAST = bring((1, 0, 0)), bring((-1, 0, 0))
Y_NEXT, Y_LAST = bring((0, 1, 0)), bring((0, -1, 0))
Z_NEXT, Z_LAST = bring((0, 0, 1)), bring((0, 0, -1))
ACROSS = route(lambda x, y, z, core: (x, y + 4, z))
ALONG = route(lambda x, y, z, core: (x + (1 if y < 4 else -1), y, z))


def swap_core(block):
    return lax.ppermute(block, "core", [(0, 1), (1, 0)])


def mm(a, b):
    return jnp.dot(a, b, preferred_element_type=F32)


def mm_t(a, b):
    return lax.dot_general(a, b, (((1,), (1,)), ((), ())), preferred_element_type=F32)


def position():
    return [lax.axis_index(axis) for axis in EVERY]


def after(value, *others):
    return lax.optimization_barrier((value,) + others)[0]


def pack_kernel(w_qkv_hbm, w_out_hbm, tokens_hbm, out, w_qkv, w_out, tokens, pieces, staged, sem):
    loads = [
        pltpu.make_async_copy(w_qkv_hbm, w_qkv, sem.at[0]),
        pltpu.make_async_copy(w_out_hbm, w_out, sem.at[1]),
        pltpu.make_async_copy(tokens_hbm, tokens, sem.at[2]),
    ]
    for load in loads:
        load.start()
    for load in loads[:2]:
        load.wait()

    def columns(kind, head):
        start = kind * D + head * HD
        return w_qkv[:, start : start + HD].astype(F32)

    for who in range(2):
        a, b, c = 8 + 2 * who, 12 + 2 * who, 4 * who
        content = (
            ((0, a), (0, a + 1)),
            ((0, b), (0, b + 1)),
            ((2, c + 2), (0, c + 3)),
            ((1, c + 3), (2, c + 3)),
            ((1, a), (1, a + 1), (2, a), (2, a + 1)),
            ((1, b), (1, b + 1), (2, b), (2, b + 1)),
            ((0, c), (1, c), (2, c), (0, c + 1)),
            ((1, c + 1), (2, c + 1), (0, c + 2), (1, c + 2)),
        )
        for colour in range(8):
            parts = [columns(*one) for one in content[colour]]
            if colour < 4:
                start = (who * 4 + colour) * PAIR
                parts = [w_out[:, start : start + PAIR].astype(F32)] + parts
            whole = jnp.concatenate(parts, 1)
            place = who * 8 + colour
            pieces[place, :18] = whole[:, :128]
            pieces[place, 18:36] = whole[:, 128:256]
            tail = whole[:, 256:]
            pieces[place, 36:41] = jnp.concatenate([tail[:5], tail[5:10], tail[9:14], tail[13:18]], 1)
            pieces[place, 41:] = jnp.zeros((3, 128), F32)
    x, yh = position()[:2]
    base = 2 * x + 4 * yh
    loads[2].wait()
    stores = []
    for dest in range(64):
        colour = (base + dest // 16 + 3 * (dest // 2 % 8)) % 8
        block = tokens[dest // 2 * 8 : dest // 2 * 8 + 8].astype(F32)
        block = block[dest % 2 * 4 : dest % 2 * 4 + 4]
        rows = [block[:, tile * 128 : tile * 128 + 128] for tile in range(9)]
        rows = [pieces[dest % 2 * 8 + colour]] + rows
        staged[dest] = jnp.concatenate(rows, 0).astype(BF16)
        stores.append(pltpu.make_async_copy(staged.at[dest], out.at[dest], sem.at[3]))
        stores[-1].start()
    for store in stores:
        store.wait()


def unpack_kernel(got, own_out, block_out, tokens_out, block, tokens, wide, sem):
    for source in range(64):
        rows = got[source].astype(F32)
        at = source * 18
        wide[0, at : at + 18] = rows[:18]
        wide[1, at : at + 18] = rows[18:36]
        wide[2, at : at + 5, :32] = rows[36:41, :32]
        wide[2, at + 5 : at + 10, :32] = rows[36:41, 32:64]
        wide[2, at + 10 : at + 14, :32] = rows[37:41, 64:96]
        wide[2, at + 14 : at + 18, :32] = rows[37:41, 96:]
        if source % 2 == 1:
            pair = [got[source - 1].astype(F32), rows]
            tiles = []
            for tile in range(9):
                start = 44 + tile * 4
                tiles.append(jnp.concatenate([one[start : start + 4] for one in pair], 0))
            tokens[source * 4 - 4 : source * 4 + 4] = jnp.concatenate(tiles, 1).astype(BF16)
    block[:128] = wide[0].T.astype(BF16)
    block[128:256] = wide[1].T.astype(BF16)
    block[256:] = wide[2].T[:32].astype(BF16)
    stores = [
        pltpu.make_async_copy(block, block_out, sem.at[0]),
        pltpu.make_async_copy(tokens, tokens_out, sem.at[1]),
        pltpu.make_async_copy(block, own_out, sem.at[2]),
    ]
    for store in stores:
        store.start()
    for store in stores:
        store.wait()


def own_embed(cam_embed):
    return cam_embed[pl.ds(lax.axis_index("x") * 2 + lax.axis_index("yh"), 1)]


def normalise(ref, embed, gain):
    hidden = ref[...].astype(F32) + embed
    centred = hidden - jnp.mean(hidden, -1, keepdims=True)
    variance = jnp.mean(centred * centred, -1, keepdims=True)
    return (centred * lax.rsqrt(variance + 1e-06) * gain[...]).astype(BF16)


def norm_kernel(own, other, cam_embed, gain, out):
    for i, ref in enumerate((own, other)):
        out[i * HALF : (i + 1) * HALF] = normalise(ref, own_embed(cam_embed), gain)


def start_fetch(blocks, colour, slot, sem):
    x, yh, yl, z, core = position()
    ahead = colour - (2 * x + 4 * yh + yl + 3 * z) + 64
    turn = lax.rem(jnp.where(core == 0, ahead, 128 - ahead), 8)
    for block, own in zip(blocks, TURNS):
        @pl.when(turn == own)
        def _(block=block):
            pltpu.make_async_copy(block, slot, sem).start()


def wait_fetch(blocks, slot, sem):
    pltpu.make_async_copy(blocks[0], slot, sem).wait()


def head_norm(part, gain):
    shaped = part.reshape(part.shape[0] // HD, HD, part.shape[1])
    mean_sq = jnp.mean(shaped * shaped, 1, keepdims=True)
    return (shaped * lax.rsqrt(mean_sq + 1e-06)).reshape(part.shape) * gain


def attend(q_t, sides, mask=None):
    total = None
    for k_t, v_t in sides:
        scores = mm(k_t.T.astype(BF16), q_t.astype(BF16))
        expd = jnp.exp2(scores * SCALE)
        if mask is not None:
            expd = jnp.where(mask, expd, 0.0)
        wide = jnp.concatenate([v_t, jnp.ones((8, v_t.shape[1]), F32)], 0).astype(BF16)
        part = mm(wide, expd.astype(BF16))
        total = part if total is None else total + part
    return total[:HD] / total[HD : HD + 1]


def project_pair(normed, w_q, w_kv, gain):
    q = head_norm(mm_t(w_q, normed[...]), gain[:PAIR])
    kv = mm_t(w_kv, normed[...])
    return q, head_norm(kv[:PAIR], gain[PAIR:]), kv[PAIR:]


def cross_project_kernel(gains, normed, *refs):
    blocks, (q_out, kv_t, w_out, early, late, q_t, weight, sem) = refs[:8], refs[8:]
    slots = {0: weight.at[0], 4: weight.at[1], 1: early.at[0], 5: early.at[1]}
    slots.update({colour: late.at[place] for place, colour in enumerate(LATE)})
    for colour, slot in slots.items():
        start_fetch(blocks, colour, slot, sem.at[colour])
    parts = [block.at[pl.ds(0, PAIR)] for block in blocks]
    thirds = [w_out.at[pl.ds(colour * PAIR, PAIR)] for colour in range(4)]
    for colour in range(4):
        start_fetch(parts, colour, thirds[colour], sem.at[8 + colour])
    for colour in (0, 4):
        wait_fetch(blocks, slots[colour], sem.at[colour])
    q, k, v = project_pair(normed, weight[0, PAIR:], weight[1], gains[...].T[:, :1])
    kv_t[...] = jnp.concatenate([k, v], 0).astype(BF16)
    q_t[...] = q.astype(BF16)
    store = pltpu.make_async_copy(q_t, q_out, sem.at[12])
    store.start()
    for colour in (1, 5) + LATE:
        wait_fetch(blocks, slots[colour], sem.at[colour])
    for colour in range(4):
        wait_fetch(parts, thirds[colour], sem.at[8 + colour])
    store.wait()


def time_kernel(gains, normed, weight, late, out, late_out, sem):
    store = pltpu.make_async_copy(late, late_out, sem)
    store.start()
    q, k, v = project_pair(normed, weight[0, PAIR:], weight[1], gains[...].T[:, 1:2])
    row = lax.broadcasted_iota(jnp.int32, (HALF, HALF), 0) % 8
    col = lax.broadcasted_iota(jnp.int32, (HALF, HALF), 1) % 8
    sets = []
    for i in range(2):
        part = slice(i * HALF, (i + 1) * HALF)
        heads = []
        for head in range(2):
            at = head * HD
            side = (k[at : at + HD, part], v[at : at + HD, part])
            heads.append(attend(q[at : at + HD, part], [side], row == col))
        sets.append(jnp.concatenate(heads, 0).T.reshape(64, 4, PAIR))
    swap = lax.axis_index("core") == 1
    one = jnp.where(swap, sets[1], sets[0])
    two = jnp.where(swap, sets[0], sets[1])
    out[...] = jnp.concatenate([one, two], 1).reshape(32, 16, PAIR).astype(BF16)
    store.wait()


def space_kernel(gains, normed_hbm, weight_hbm, out, normed, result, weight, sem):
    loads = [pltpu.make_async_copy(weight_hbm.at[slot], weight.at[slot], sem.at[slot]) for slot in range(4)]
    loads.insert(0, pltpu.make_async_copy(normed_hbm, normed, sem.at[4]))
    for load in loads:
        load.start()
    columns = gains[...].T[:PAIR]
    loads[0].wait()
    rows = []
    for slot in range(4):
        loads[1 + slot].wait()
        projected = mm_t(weight[slot, (PAIR if slot > 1 else 0) :], normed[...])
        rows += [projected[at : at + HD] for at in range(0, projected.shape[0], HD)]
    heads = []
    for head in range(4):
        q, k, v = rows[3 * head : 3 * head + 3]
        gain = columns[:, 2 + head : 3 + head]
        q, k = head_norm(q, gain[:HD]), head_norm(k, gain[HD:])
        heads.append(attend(q, [(k, v)]))
    result[...] = jnp.concatenate(heads, 0).astype(BF16)
    store = pltpu.make_async_copy(result, out, sem.at[5])
    store.start()
    store.wait()


def cross_kernel(kv_a, kv_b, timed, space_hbm, q_hbm, w_hbm, keep, give, w_out, space, q_t, sem):
    w_load = pltpu.make_async_copy(w_hbm, w_out, sem.at[2])
    w_load.start()
    loads = [pltpu.make_async_copy(q_hbm, q_t, sem.at[0]), pltpu.make_async_copy(space_hbm, space, sem.at[1])]
    for load in loads:
        load.start()
    both = [ref[...].astype(F32) for ref in (kv_a, kv_b)]
    loads[0].wait()
    query = q_t[...].astype(F32)
    heads = []
    for head in range(2):
        at = head * HD
        sides = [(kv[at : at + HD], kv[PAIR + at : PAIR + at + HD]) for kv in both]
        heads.append(attend(query[at : at + HD], sides))
    loads[1].wait()
    mixed = jnp.concatenate([space[...].astype(F32)] + heads, 0).T
    late = timed[...].astype(F32)
    late = [late[:, i * 8 : i * 8 + 8].reshape(HALF, PAIR) for i in range(2)]
    swap = lax.axis_index("core") == 1
    keep[...] = jnp.concatenate([mixed[:HALF], jnp.where(swap, late[1], late[0])], 1).astype(BF16)
    give[...] = jnp.concatenate([mixed[HALF:], jnp.where(swap, late[0], late[1])], 1).astype(BF16)
    w_load.wait()


def out_kernel(tokens, own, arrived, w_own, w_other, embed_hbm, out, cam_embed, sem):
    load = pltpu.make_async_copy(embed_hbm, cam_embed, sem)
    load.start()
    swap = lax.axis_index("core") == 1
    mine, theirs = own[...].astype(F32), arrived[...].astype(F32)
    first = jnp.where(swap, theirs, mine)
    second = jnp.where(swap, mine, theirs)
    parts = []
    for start, end in ((0, 2 * PAIR), (2 * PAIR, 3 * PAIR), (3 * PAIR, 4 * PAIR)):
        parts += [first[:, start:end], second[:, start:end]]
    mixed = jnp.concatenate(parts, 1).astype(BF16)
    one, two = mm_t(mixed, w_own[...]), mm_t(mixed, w_other[...])
    update = jnp.concatenate([jnp.where(swap, two, one), jnp.where(swap, one, two)], 1)
    load.wait()
    out[...] = (tokens[...].astype(F32) + own_embed(cam_embed) + update).astype(BF16)


def call(kernel, out_shapes, args, scratch=(), flops=0, anys=0, room=VMEM_LIMIT):
    vmem = pl.BlockSpec(memory_space=pltpu.VMEM)
    hbm = pl.BlockSpec(memory_space=pltpu.HBM)
    specs = []
    for i in range(len(args)):
        specs.append(hbm if i >= len(args) - anys else vmem)

    def place(out):
        return pl.BlockSpec(memory_space=pl.ANY) if hasattr(out, "memory_space") else vmem

    single = not isinstance(out_shapes, tuple)
    return pl.pallas_call(
        kernel,
        out_shape=out_shapes,
        in_specs=specs,
        out_specs=place(out_shapes) if single else tuple(place(out) for out in out_shapes),
        scratch_shapes=list(scratch),
        compiler_params=pltpu.CompilerParams(vmem_limit_bytes=room),
        cost_estimate=pl.CostEstimate(flops=flops, bytes_accessed=1, transcendentals=0),
    )(*args)


def shape(*dims):
    return jax.ShapeDtypeStruct(dims, BF16)


def far(*dims):
    return pltpu.HBM(dims, BF16)


def near(*dims):
    return pltpu.VMEM(dims, BF16)


def keep_near(array):
    return pltpu.with_memory_space_constraint(array, pltpu.VMEM)


def stay(array):
    return pltpu.with_memory_space_constraint(array, pltpu.HBM)


def local(frames_in, cam_embed, norm_gain, q_gain, k_gain, w_qkv, w_out):
    tokens = frames_in[0]
    core = lax.axis_index("core")
    gain = norm_gain[None]
    both = jnp.stack([q_gain.reshape(HEADS, HD), k_gain.reshape(HEADS, HD)], 1)

    def gains_of(head, count):
        return lax.dynamic_slice_in_dim(both, head, count, 0)

    pair_gains = jnp.stack([gains_of(8 + 2 * core, 2), gains_of(12 + 2 * core, 2)])
    pair_gains = pair_gains.transpose(0, 2, 1, 3).reshape(2, 2 * PAIR)
    space_gains = gains_of(4 * core, 4).reshape(4, PAIR)
    gains = jnp.concatenate([pair_gains, jnp.pad(space_gains, ((0, 2), (0, PAIR)))], 0)

    pieces = call(
        pack_kernel,
        far(64, PIECE, 128),
        (w_qkv, w_out, tokens),
        [
            pltpu.VMEM((18, 3 * D), BF16),
            pltpu.VMEM((18, D), BF16),
            pltpu.VMEM((HALF, D), BF16),
            pltpu.VMEM((16, 44, 128), F32),
            pltpu.VMEM((64, PIECE, 128), BF16),
            pltpu.SemaphoreType.DMA((4,)),
        ],
        0,
        3,
        58 * 1024 * 1024,
    )
    got = lax.all_to_all(pieces, SLAB, 0, 0, tiled=True)
    other = swap_core(tokens)
    normed = keep_near(call(norm_kernel, shape(ROWS, D), (tokens, other, cam_embed, gain), (), 8 * 10**9))
    own_block, block, time_own = call(
        unpack_kernel,
        (near(QUAD, D), far(QUAD, D), far(HALF, D)),
        (after(got, normed, gains),),
        [
            pltpu.VMEM((QUAD, D), BF16),
            pltpu.VMEM((HALF, D), BF16),
            pltpu.VMEM((3, D, 128), F32),
            pltpu.SemaphoreType.DMA((3,)),
        ],
    )
    blocks = [keep_near(own_block)]
    for way in (X_NEXT, Y_NEXT, X_LAST, Z_NEXT, Y_LAST, None, Z_LAST):
        if way is None:
            blocks.append(lax.ppermute(blocks[1], EVERY, X_NEXT))
        else:
            blocks.append(lax.ppermute(block, EVERY, way))
    blocks = tuple(blocks)
    time_other = swap_core(time_own)
    time_normed = keep_near(call(norm_kernel, shape(ROWS, D), (time_own, time_other, cam_embed, gain), (), 8 * 10**9))
    q_t, kv_t, w_own, early, late = call(
        cross_project_kernel,
        (far(PAIR, ROWS), shape(2 * PAIR, ROWS), near(4 * PAIR, D), near(2, QUAD, D), near(4, QUAD, D)),
        (gains, normed) + blocks,
        [pltpu.VMEM((PAIR, ROWS), BF16), pltpu.VMEM((2, QUAD, D), BF16), pltpu.SemaphoreType.DMA((13,))],
        0,
        8,
    )
    kv_a = lax.ppermute(kv_t, EVERY, ACROSS)
    w_other = swap_core(w_own)
    timed, late = call(
        time_kernel,
        (shape(32, 16, PAIR), far(4, QUAD, D)),
        (gains, after(time_normed, kv_t), keep_near(early), keep_near(late)),
        [pltpu.SemaphoreType.DMA],
        0,
        1,
    )
    kv_b = lax.ppermute(after(kv_a, timed), EVERY, ALONG)
    space = call(
        space_kernel,
        far(2 * PAIR, ROWS),
        (gains, stay(after(normed, timed)), stay(late)),
        [
            pltpu.VMEM((ROWS, D), BF16),
            pltpu.VMEM((2 * PAIR, ROWS), BF16),
            pltpu.VMEM((4, QUAD, D), BF16),
            pltpu.SemaphoreType.DMA((6,)),
        ],
        16 * 10**9,
        2,
    )
    returned = lax.all_to_all(timed, CHIP, 0, 0, tiled=True)
    keep, give, w_other = call(
        cross_kernel,
        (shape(HALF, 4 * PAIR), shape(HALF, 4 * PAIR), near(4 * PAIR, D)),
        (kv_a, kv_b, returned, stay(space), stay(q_t), w_other),
        [pltpu.VMEM((2 * PAIR, ROWS), BF16), pltpu.VMEM((PAIR, ROWS), BF16), pltpu.SemaphoreType.DMA((3,))],
        0,
        3,
    )
    arrived = swap_core(give)
    return call(
        out_kernel,
        shape(HALF, D),
        (tokens, keep, arrived, w_own, keep_near(w_other), stay(cam_embed)),
        [pltpu.VMEM((8, D), F32), pltpu.SemaphoreType.DMA],
        0,
        1,
    )[None]


def solution(mesh):
    fine = Mesh(mesh.devices.reshape(4, 2, 4, 8, 2), EVERY)
    placed = (P(CAM, SLAB, None), P(), P(), P(), P(), P(SLAB, None), P(SLAB, None))
    return jax.shard_map(local, mesh=fine, in_specs=placed, out_specs=P(CAM, SLAB, None), check_vma=False)
```

```python
import jax
import jax.numpy as jnp
from jax import lax
from jax.experimental import pallas as pl
from jax.experimental.pallas import tpu as pltpu
from jax.sharding import Mesh
from jax.sharding import PartitionSpec as P

HEADS = 16
HD = 72
D = HEADS * HD
PAIR = 2 * HD
QUAD = 4 * HD
HALF = 256
ROWS = 2 * HALF
PIECE = 80
LATE = (6, 7, 2, 3)
CAM = ("x", "yh")
CHIP = ("yl", "z")
SLAB = ("yl", "z", "core")
EVERY = ("x", "yh", "yl", "z", "core")
SCALE = 1.4426950408889634 / HD**0.5
F32 = jnp.float32
BF16 = jnp.bfloat16
VMEM_LIMIT = 18 * 1024 * 1024


def route(move):
    pairs = []
    for x in range(4):
        for y in range(8):
            for z in range(8):
                for core in range(2):
                    a, b, c = move(x, y, z, core)
                    source = ((x * 8 + y) * 8 + z) * 2 + core
                    pairs.append((source, ((a % 4 * 8 + b % 8) * 8 + c % 8) * 2 + core))
    return pairs


def towards(core):
    return 1 if core else -1


TURNS = (0, 2, 1, 6, 3, 7, 4, 5)


def bring(offset):
    a, b, c = offset
    return route(lambda x, y, z, core: (x + a * towards(core), y + b * towards(core), z + c * towards(core)))


X_NEXT, X_LAST = bring((1, 0, 0)), bring((-1, 0, 0))
Y_NEXT, Y_LAST = bring((0, 1, 0)), bring((0, -1, 0))
Z_NEXT, Z_LAST = bring((0, 0, 1)), bring((0, 0, -1))
ACROSS = route(lambda x, y, z, core: (x, y + 4, z))
ALONG = route(lambda x, y, z, core: (x + (1 if y < 4 else -1), y, z))


def swap_core(block):
    return lax.ppermute(block, "core", [(0, 1), (1, 0)])


def mm(a, b):
    return jnp.dot(a, b, preferred_element_type=F32)


def mm_t(a, b):
    return lax.dot_general(a, b, (((1,), (1,)), ((), ())), preferred_element_type=F32)


def position():
    return [lax.axis_index(axis) for axis in EVERY]


def after(value, *others):
    return lax.optimization_barrier((value,) + others)[0]


def pack_kernel(w_qkv_hbm, w_out_hbm, tokens_hbm, out, w_qkv, w_out, tokens, pieces, staged, sem):
    loads = [
        pltpu.make_async_copy(w_qkv_hbm, w_qkv, sem.at[0]),
        pltpu.make_async_copy(w_out_hbm, w_out, sem.at[1]),
        pltpu.make_async_copy(tokens_hbm, tokens, sem.at[2]),
    ]
    for load in loads:
        load.start()
    for load in loads[:2]:
        load.wait()

    def columns(kind, head):
        start = kind * D + head * HD
        return w_qkv[:, start : start + HD].astype(F32)

    for who in range(2):
        a, b, c = 8 + 2 * who, 12 + 2 * who, 4 * who
        content = (
            ((0, a), (0, a + 1)),
            ((0, b), (0, b + 1)),
            ((2, c + 2), (0, c + 3)),
            ((1, c + 3), (2, c + 3)),
            ((1, a), (1, a + 1), (2, a), (2, a + 1)),
            ((1, b), (1, b + 1), (2, b), (2, b + 1)),
            ((0, c), (1, c), (2, c), (0, c + 1)),
            ((1, c + 1), (2, c + 1), (0, c + 2), (1, c + 2)),
        )
        for colour in range(8):
            parts = [columns(*one) for one in content[colour]]
            if colour < 4:
                start = (who * 4 + colour) * PAIR
                parts = [w_out[:, start : start + PAIR].astype(F32)] + parts
            whole = jnp.concatenate(parts, 1)
            place = who * 8 + colour
            pieces[place, :18] = whole[:, :128]
            pieces[place, 18:36] = whole[:, 128:256]
            tail = whole[:, 256:]
            pieces[place, 36:41] = jnp.concatenate([tail[:5], tail[5:10], tail[9:14], tail[13:18]], 1)
            pieces[place, 41:] = jnp.zeros((3, 128), F32)
    x, yh = position()[:2]
    base = 2 * x + 4 * yh
    loads[2].wait()
    stores = []
    for dest in range(64):
        colour = (base + dest // 16 + 3 * (dest // 2 % 8)) % 8
        block = tokens[dest // 2 * 8 : dest // 2 * 8 + 8].astype(F32)
        block = block[dest % 2 * 4 : dest % 2 * 4 + 4]
        rows = [block[:, tile * 128 : tile * 128 + 128] for tile in range(9)]
        rows = [pieces[dest % 2 * 8 + colour]] + rows
        staged[dest] = jnp.concatenate(rows, 0).astype(BF16)
        stores.append(pltpu.make_async_copy(staged.at[dest], out.at[dest], sem.at[3]))
        stores[-1].start()
    for store in stores:
        store.wait()


def unpack_kernel(got, own_out, block_out, tokens_out, block, tokens, wide, sem):
    for source in range(64):
        rows = got[source].astype(F32)
        at = source * 18
        wide[0, at : at + 18] = rows[:18]
        wide[1, at : at + 18] = rows[18:36]
        wide[2, at : at + 5, :32] = rows[36:41, :32]
        wide[2, at + 5 : at + 10, :32] = rows[36:41, 32:64]
        wide[2, at + 10 : at + 14, :32] = rows[37:41, 64:96]
        wide[2, at + 14 : at + 18, :32] = rows[37:41, 96:]
        if source % 2 == 1:
            pair = [got[source - 1].astype(F32), rows]
            tiles = []
            for tile in range(9):
                start = 44 + tile * 4
                tiles.append(jnp.concatenate([one[start : start + 4] for one in pair], 0))
            tokens[source * 4 - 4 : source * 4 + 4] = jnp.concatenate(tiles, 1).astype(BF16)
    block[:128] = wide[0].T.astype(BF16)
    block[128:256] = wide[1].T.astype(BF16)
    block[256:] = wide[2].T[:32].astype(BF16)
    stores = [
        pltpu.make_async_copy(block, block_out, sem.at[0]),
        pltpu.make_async_copy(tokens, tokens_out, sem.at[1]),
        pltpu.make_async_copy(block, own_out, sem.at[2]),
    ]
    for store in stores:
        store.start()
    for store in stores:
        store.wait()


def own_embed(cam_embed):
    return cam_embed[pl.ds(lax.axis_index("x") * 2 + lax.axis_index("yh"), 1)]


def normalise(ref, embed, gain):
    hidden = ref[...].astype(F32) + embed
    centred = hidden - jnp.mean(hidden, -1, keepdims=True)
    variance = jnp.mean(centred * centred, -1, keepdims=True)
    return (centred * lax.rsqrt(variance + 1e-06) * gain[...]).astype(BF16)


def norm_kernel(own, other, cam_embed, gain, out):
    for i, ref in enumerate((own, other)):
        out[i * HALF : (i + 1) * HALF] = normalise(ref, own_embed(cam_embed), gain)


def start_fetch(blocks, colour, slot, sem):
    x, yh, yl, z, core = position()
    ahead = colour - (2 * x + 4 * yh + yl + 3 * z) + 64
    turn = lax.rem(jnp.where(core == 0, ahead, 128 - ahead), 8)
    for block, own in zip(blocks, TURNS):
        @pl.when(turn == own)
        def _(block=block):
            pltpu.make_async_copy(block, slot, sem).start()


def wait_fetch(blocks, slot, sem):
    pltpu.make_async_copy(blocks[0], slot, sem).wait()


def head_norm(part, gain):
    shaped = part.reshape(part.shape[0] // HD, HD, part.shape[1])
    mean_sq = jnp.mean(shaped * shaped, 1, keepdims=True)
    return (shaped * lax.rsqrt(mean_sq + 1e-06)).reshape(part.shape) * gain


def attend(q_t, sides, mask=None):
    total = None
    for k_t, v_t in sides:
        scores = mm(k_t.T.astype(BF16), q_t.astype(BF16))
        expd = jnp.exp2(scores * SCALE)
        if mask is not None:
            expd = jnp.where(mask, expd, 0.0)
        wide = jnp.concatenate([v_t, jnp.ones((8, v_t.shape[1]), F32)], 0).astype(BF16)
        part = mm(wide, expd.astype(BF16))
        total = part if total is None else total + part
    return total[:HD] / total[HD : HD + 1]


def project_pair(normed, w_q, w_kv, gain):
    q = head_norm(mm_t(w_q, normed[...]), gain[:PAIR])
    kv = mm_t(w_kv, normed[...])
    return q, head_norm(kv[:PAIR], gain[PAIR:]), kv[PAIR:]


def cross_project_kernel(gains, normed, *refs):
    blocks, (q_out, kv_t, w_out, early, late, q_t, weight, sem) = refs[:8], refs[8:]
    slots = {0: weight.at[0], 4: weight.at[1], 1: early.at[0], 5: early.at[1]}
    slots.update({colour: late.at[place] for place, colour in enumerate(LATE)})
    for colour, slot in slots.items():
        start_fetch(blocks, colour, slot, sem.at[colour])
    parts = [block.at[pl.ds(0, PAIR)] for block in blocks]
    thirds = [w_out.at[pl.ds(colour * PAIR, PAIR)] for colour in range(4)]
    for colour in range(4):
        start_fetch(parts, colour, thirds[colour], sem.at[8 + colour])
    for colour in (0, 4):
        wait_fetch(blocks, slots[colour], sem.at[colour])
    q, k, v = project_pair(normed, weight[0, PAIR:], weight[1], gains[...].T[:, :1])
    kv_t[...] = jnp.concatenate([k, v], 0).astype(BF16)
    q_t[...] = q.astype(BF16)
    store = pltpu.make_async_copy(q_t, q_out, sem.at[12])
    store.start()
    for colour in (1, 5) + LATE:
        wait_fetch(blocks, slots[colour], sem.at[colour])
    for colour in range(4):
        wait_fetch(parts, thirds[colour], sem.at[8 + colour])
    store.wait()


def time_kernel(gains, normed, weight, out):
    q, k, v = project_pair(normed, weight[0, PAIR:], weight[1], gains[...].T[:, 1:2])
    row = lax.broadcasted_iota(jnp.int32, (HALF, HALF), 0) % 8
    col = lax.broadcasted_iota(jnp.int32, (HALF, HALF), 1) % 8
    sets = []
    for i in range(2):
        part = slice(i * HALF, (i + 1) * HALF)
        heads = []
        for head in range(2):
            at = head * HD
            side = (k[at : at + HD, part], v[at : at + HD, part])
            heads.append(attend(q[at : at + HD, part], [side], row == col))
        sets.append(jnp.concatenate(heads, 0).T.reshape(64, 4, PAIR))
    swap = lax.axis_index("core") == 1
    one = jnp.where(swap, sets[1], sets[0])
    two = jnp.where(swap, sets[0], sets[1])
    out[...] = jnp.concatenate([one, two], 1).reshape(32, 16, PAIR).astype(BF16)


def space_kernel(gains, normed_hbm, weight_hbm, out, normed, result, weight, sem):
    loads = [pltpu.make_async_copy(weight_hbm.at[slot], weight.at[slot], sem.at[slot]) for slot in range(4)]
    loads.insert(0, pltpu.make_async_copy(normed_hbm, normed, sem.at[4]))
    for load in loads:
        load.start()
    columns = gains[...].T[:PAIR]
    loads[0].wait()
    rows = []
    for slot in range(4):
        loads[1 + slot].wait()
        projected = mm_t(weight[slot, (PAIR if slot > 1 else 0) :], normed[...])
        rows += [projected[at : at + HD] for at in range(0, projected.shape[0], HD)]
    heads = []
    for head in range(4):
        q, k, v = rows[3 * head : 3 * head + 3]
        gain = columns[:, 2 + head : 3 + head]
        q, k = head_norm(q, gain[:HD]), head_norm(k, gain[HD:])
        heads.append(attend(q, [(k, v)]))
    result[...] = jnp.concatenate(heads, 0).astype(BF16)
    store = pltpu.make_async_copy(result, out, sem.at[5])
    store.start()
    store.wait()


def cross_kernel(kv_a, kv_b, timed, space_hbm, q_hbm, keep, give, space, q_t, sem):
    loads = [pltpu.make_async_copy(q_hbm, q_t, sem.at[0]), pltpu.make_async_copy(space_hbm, space, sem.at[1])]
    for load in loads:
        load.start()
    both = [ref[...].astype(F32) for ref in (kv_a, kv_b)]
    loads[0].wait()
    query = q_t[...].astype(F32)
    heads = []
    for head in range(2):
        at = head * HD
        sides = [(kv[at : at + HD], kv[PAIR + at : PAIR + at + HD]) for kv in both]
        heads.append(attend(query[at : at + HD], sides))
    loads[1].wait()
    mixed = jnp.concatenate([space[...].astype(F32)] + heads, 0).T
    late = timed[...].astype(F32)
    late = [late[:, i * 8 : i * 8 + 8].reshape(HALF, PAIR) for i in range(2)]
    swap = lax.axis_index("core") == 1
    keep[...] = jnp.concatenate([mixed[:HALF], jnp.where(swap, late[1], late[0])], 1).astype(BF16)
    give[...] = jnp.concatenate([mixed[HALF:], jnp.where(swap, late[0], late[1])], 1).astype(BF16)


def out_kernel(tokens, own, arrived, w_own, w_hbm, embed_hbm, out, w_other, cam_embed, sem):
    loads = [
        pltpu.make_async_copy(w_hbm, w_other, sem.at[0]),
        pltpu.make_async_copy(embed_hbm, cam_embed, sem.at[1]),
    ]
    for load in loads:
        load.start()
    swap = lax.axis_index("core") == 1
    mine, theirs = own[...].astype(F32), arrived[...].astype(F32)
    first = jnp.where(swap, theirs, mine)
    second = jnp.where(swap, mine, theirs)
    parts = []
    for start, end in ((0, 2 * PAIR), (2 * PAIR, 3 * PAIR), (3 * PAIR, 4 * PAIR)):
        parts += [first[:, start:end], second[:, start:end]]
    mixed = jnp.concatenate(parts, 1).astype(BF16)
    one = mm_t(mixed, w_own[...])
    for load in loads:
        load.wait()
    two = mm_t(mixed, w_other[...])
    update = jnp.concatenate([jnp.where(swap, two, one), jnp.where(swap, one, two)], 1)
    out[...] = (tokens[...].astype(F32) + own_embed(cam_embed) + update).astype(BF16)


def call(kernel, out_shapes, args, scratch=(), flops=0, anys=0, room=VMEM_LIMIT):
    vmem = pl.BlockSpec(memory_space=pltpu.VMEM)
    hbm = pl.BlockSpec(memory_space=pltpu.HBM)
    specs = []
    for i in range(len(args)):
        specs.append(hbm if i >= len(args) - anys else vmem)

    def place(out):
        return pl.BlockSpec(memory_space=pl.ANY) if hasattr(out, "memory_space") else vmem

    single = not isinstance(out_shapes, tuple)
    return pl.pallas_call(
        kernel,
        out_shape=out_shapes,
        in_specs=specs,
        out_specs=place(out_shapes) if single else tuple(place(out) for out in out_shapes),
        scratch_shapes=list(scratch),
        compiler_params=pltpu.CompilerParams(vmem_limit_bytes=room),
        cost_estimate=pl.CostEstimate(flops=flops, bytes_accessed=1, transcendentals=0),
    )(*args)


def shape(*dims):
    return jax.ShapeDtypeStruct(dims, BF16)


def far(*dims):
    return pltpu.HBM(dims, BF16)


def near(*dims):
    return pltpu.VMEM(dims, BF16)


def keep_near(array):
    return pltpu.with_memory_space_constraint(array, pltpu.VMEM)


def stay(array):
    return pltpu.with_memory_space_constraint(array, pltpu.HBM)


def local(frames_in, cam_embed, norm_gain, q_gain, k_gain, w_qkv, w_out):
    tokens = frames_in[0]
    core = lax.axis_index("core")
    gain = norm_gain[None]
    both = jnp.stack([q_gain.reshape(HEADS, HD), k_gain.reshape(HEADS, HD)], 1)

    def gains_of(head, count):
        return lax.dynamic_slice_in_dim(both, head, count, 0)

    pair_gains = jnp.stack([gains_of(8 + 2 * core, 2), gains_of(12 + 2 * core, 2)])
    pair_gains = pair_gains.transpose(0, 2, 1, 3).reshape(2, 2 * PAIR)
    space_gains = gains_of(4 * core, 4).reshape(4, PAIR)
    gains = jnp.concatenate([pair_gains, jnp.pad(space_gains, ((0, 2), (0, PAIR)))], 0)

    pieces = call(
        pack_kernel,
        far(64, PIECE, 128),
        (w_qkv, w_out, tokens),
        [
            pltpu.VMEM((18, 3 * D), BF16),
            pltpu.VMEM((18, D), BF16),
            pltpu.VMEM((HALF, D), BF16),
            pltpu.VMEM((16, 44, 128), F32),
            pltpu.VMEM((64, PIECE, 128), BF16),
            pltpu.SemaphoreType.DMA((4,)),
        ],
        0,
        3,
        58 * 1024 * 1024,
    )
    got = lax.all_to_all(pieces, SLAB, 0, 0, tiled=True)
    other = swap_core(tokens)
    normed = keep_near(call(norm_kernel, shape(ROWS, D), (tokens, other, cam_embed, gain), (), 8 * 10**9))
    own_block, block, time_own = call(
        unpack_kernel,
        (near(QUAD, D), far(QUAD, D), far(HALF, D)),
        (after(got, normed, gains),),
        [
            pltpu.VMEM((QUAD, D), BF16),
            pltpu.VMEM((HALF, D), BF16),
            pltpu.VMEM((3, D, 128), F32),
            pltpu.SemaphoreType.DMA((3,)),
        ],
    )
    blocks = [keep_near(own_block)]
    for way in (X_NEXT, Y_NEXT, X_LAST, Z_NEXT, Y_LAST, None, Z_LAST):
        if way is None:
            blocks.append(lax.ppermute(blocks[1], EVERY, X_NEXT))
        else:
            blocks.append(lax.ppermute(block, EVERY, way))
    blocks = tuple(blocks)
    time_other = swap_core(time_own)
    time_normed = keep_near(call(norm_kernel, shape(ROWS, D), (time_own, time_other, cam_embed, gain), (), 8 * 10**9))
    q_t, kv_t, w_own, early, late = call(
        cross_project_kernel,
        (far(PAIR, ROWS), shape(2 * PAIR, ROWS), near(4 * PAIR, D), near(2, QUAD, D), far(4, QUAD, D)),
        (gains, normed) + blocks,
        [pltpu.VMEM((PAIR, ROWS), BF16), pltpu.VMEM((2, QUAD, D), BF16), pltpu.SemaphoreType.DMA((13,))],
        0,
        8,
    )
    kv_a = lax.ppermute(kv_t, EVERY, ACROSS)
    timed = call(time_kernel, shape(32, 16, PAIR), (gains, after(time_normed, kv_t), keep_near(early)))
    kv_b = lax.ppermute(after(kv_a, timed), EVERY, ALONG)
    space = call(
        space_kernel,
        far(2 * PAIR, ROWS),
        (gains, stay(after(normed, timed)), stay(late)),
        [
            pltpu.VMEM((ROWS, D), BF16),
            pltpu.VMEM((2 * PAIR, ROWS), BF16),
            pltpu.VMEM((4, QUAD, D), BF16),
            pltpu.SemaphoreType.DMA((6,)),
        ],
        16 * 10**9,
        2,
    )
    returned = lax.all_to_all(timed, CHIP, 0, 0, tiled=True)
    w_other = swap_core(w_own)
    keep, give = call(
        cross_kernel,
        (shape(HALF, 4 * PAIR), shape(HALF, 4 * PAIR)),
        (kv_a, kv_b, returned, stay(space), stay(q_t)),
        [pltpu.VMEM((2 * PAIR, ROWS), BF16), pltpu.VMEM((PAIR, ROWS), BF16), pltpu.SemaphoreType.DMA((2,))],
        0,
        2,
    )
    arrived = swap_core(give)
    return call(
        out_kernel,
        shape(HALF, D),
        (tokens, keep, arrived, w_own, w_other, stay(cam_embed)),
        [pltpu.VMEM((4 * PAIR, D), BF16), pltpu.VMEM((8, D), F32), pltpu.SemaphoreType.DMA((2,))],
        0,
        2,
    )[None]


def solution(mesh):
    fine = Mesh(mesh.devices.reshape(4, 2, 4, 8, 2), EVERY)
    placed = (P(CAM, SLAB, None), P(), P(), P(), P(), P(SLAB, None), P(SLAB, None))
    return jax.shard_map(local, mesh=fine, in_specs=placed, out_specs=P(CAM, SLAB, None), check_vma=False)
```

```python
import jax
import jax.numpy as jnp
from jax import lax
from jax.experimental import pallas as pl
from jax.experimental.pallas import tpu as pltpu
from jax.sharding import Mesh
from jax.sharding import PartitionSpec as P

HEADS = 16
HD = 72
D = HEADS * HD
PAIR = 2 * HD
QUAD = 4 * HD
HALF = 256
ROWS = 2 * HALF
PIECE = 80
LATE = (6, 7, 2, 3)
CAM = ("x", "yh")
CHIP = ("yl", "z")
SLAB = ("yl", "z", "core")
EVERY = ("x", "yh", "yl", "z", "core")
SCALE = 1.4426950408889634 / HD**0.5
F32 = jnp.float32
BF16 = jnp.bfloat16
VMEM_LIMIT = 18 * 1024 * 1024


def route(move):
    pairs = []
    for x in range(4):
        for y in range(8):
            for z in range(8):
                for core in range(2):
                    a, b, c = move(x, y, z, core)
                    source = ((x * 8 + y) * 8 + z) * 2 + core
                    pairs.append((source, ((a % 4 * 8 + b % 8) * 8 + c % 8) * 2 + core))
    return pairs


def towards(core):
    return 1 if core else -1


TURNS = (0, 2, 1, 6, 3, 7, 4, 5)


def bring(offset):
    a, b, c = offset
    return route(lambda x, y, z, core: (x + a * towards(core), y + b * towards(core), z + c * towards(core)))


X_NEXT, X_LAST = bring((1, 0, 0)), bring((-1, 0, 0))
Y_NEXT, Y_LAST = bring((0, 1, 0)), bring((0, -1, 0))
Z_NEXT, Z_LAST = bring((0, 0, 1)), bring((0, 0, -1))
ACROSS = route(lambda x, y, z, core: (x, y + 4, z))
ALONG = route(lambda x, y, z, core: (x + (1 if y < 4 else -1), y, z))


def swap_core(block):
    return lax.ppermute(block, "core", [(0, 1), (1, 0)])


def mm(a, b):
    return jnp.dot(a, b, preferred_element_type=F32)


def mm_t(a, b):
    return lax.dot_general(a, b, (((1,), (1,)), ((), ())), preferred_element_type=F32)


def position():
    return [lax.axis_index(axis) for axis in EVERY]


def after(value, *others):
    return lax.optimization_barrier((value,) + others)[0]


def pack_kernel(w_qkv_hbm, w_out_hbm, tokens_hbm, out, w_qkv, w_out, tokens, pieces, staged, sem):
    loads = [
        pltpu.make_async_copy(w_qkv_hbm, w_qkv, sem.at[0]),
        pltpu.make_async_copy(w_out_hbm, w_out, sem.at[1]),
        pltpu.make_async_copy(tokens_hbm, tokens, sem.at[2]),
    ]
    for load in loads:
        load.start()
    for load in loads[:2]:
        load.wait()

    def columns(kind, head):
        start = kind * D + head * HD
        return w_qkv[:, start : start + HD].astype(F32)

    for who in range(2):
        a, b, c = 8 + 2 * who, 12 + 2 * who, 4 * who
        content = (
            ((0, a), (0, a + 1)),
            ((0, b), (0, b + 1)),
            ((2, c + 2), (0, c + 3)),
            ((1, c + 3), (2, c + 3)),
            ((1, a), (1, a + 1), (2, a), (2, a + 1)),
            ((1, b), (1, b + 1), (2, b), (2, b + 1)),
            ((0, c), (1, c), (2, c), (0, c + 1)),
            ((1, c + 1), (2, c + 1), (0, c + 2), (1, c + 2)),
        )
        for colour in range(8):
            parts = [columns(*one) for one in content[colour]]
            if colour < 4:
                start = (who * 4 + colour) * PAIR
                parts = [w_out[:, start : start + PAIR].astype(F32)] + parts
            whole = jnp.concatenate(parts, 1)
            place = who * 8 + colour
            pieces[place, :18] = whole[:, :128]
            pieces[place, 18:36] = whole[:, 128:256]
            tail = whole[:, 256:]
            pieces[place, 36:41] = jnp.concatenate([tail[:5], tail[5:10], tail[9:14], tail[13:18]], 1)
            pieces[place, 41:] = jnp.zeros((3, 128), F32)
    x, yh = position()[:2]
    base = 2 * x + 4 * yh
    loads[2].wait()
    stores = []
    for dest in range(64):
        colour = (base + dest // 16 + 3 * (dest // 2 % 8)) % 8
        block = tokens[dest // 2 * 8 : dest // 2 * 8 + 8].astype(F32)
        block = block[dest % 2 * 4 : dest % 2 * 4 + 4]
        rows = [block[:, tile * 128 : tile * 128 + 128] for tile in range(9)]
        rows = [pieces[dest % 2 * 8 + colour]] + rows
        staged[dest] = jnp.concatenate(rows, 0).astype(BF16)
        stores.append(pltpu.make_async_copy(staged.at[dest], out.at[dest], sem.at[3]))
        stores[-1].start()
    for store in stores:
        store.wait()


def unpack_kernel(got, own_out, block_out, tokens_out, block, tokens, wide, sem):
    for source in range(64):
        rows = got[source].astype(F32)
        at = source * 18
        wide[0, at : at + 18] = rows[:18]
        wide[1, at : at + 18] = rows[18:36]
        wide[2, at : at + 5, :32] = rows[36:41, :32]
        wide[2, at + 5 : at + 10, :32] = rows[36:41, 32:64]
        wide[2, at + 10 : at + 14, :32] = rows[37:41, 64:96]
        wide[2, at + 14 : at + 18, :32] = rows[37:41, 96:]
    block[:128] = wide[0].T.astype(BF16)
    block[128:256] = wide[1].T.astype(BF16)
    block[256:] = wide[2].T[:32].astype(BF16)
    stores = [
        pltpu.make_async_copy(block, block_out, sem.at[0]),
        pltpu.make_async_copy(block, own_out, sem.at[1]),
        pltpu.make_async_copy(tokens, tokens_out, sem.at[2]),
    ]
    for store in stores[:2]:
        store.start()
    for source in range(0, 64, 2):
        pair = [got[source + i].astype(F32) for i in range(2)]
        tiles = []
        for tile in range(9):
            start = 44 + tile * 4
            tiles.append(jnp.concatenate([one[start : start + 4] for one in pair], 0))
        tokens[source * 4 : source * 4 + 8] = jnp.concatenate(tiles, 1).astype(BF16)
    stores[2].start()
    for store in stores:
        store.wait()


def own_embed(cam_embed):
    return cam_embed[pl.ds(lax.axis_index("x") * 2 + lax.axis_index("yh"), 1)]


def normalise(ref, embed, gain):
    hidden = ref[...].astype(F32) + embed
    centred = hidden - jnp.mean(hidden, -1, keepdims=True)
    variance = jnp.mean(centred * centred, -1, keepdims=True)
    return (centred * lax.rsqrt(variance + 1e-06) * gain[...]).astype(BF16)


def norm_kernel(own, other, cam_embed, gain, out):
    for i, ref in enumerate((own, other)):
        out[i * HALF : (i + 1) * HALF] = normalise(ref, own_embed(cam_embed), gain)


def start_fetch(blocks, colour, slot, sem):
    x, yh, yl, z, core = position()
    ahead = colour - (2 * x + 4 * yh + yl + 3 * z) + 64
    turn = lax.rem(jnp.where(core == 0, ahead, 128 - ahead), 8)
    for block, own in zip(blocks, TURNS):
        @pl.when(turn == own)
        def _(block=block):
            pltpu.make_async_copy(block, slot, sem).start()


def wait_fetch(blocks, slot, sem):
    pltpu.make_async_copy(blocks[0], slot, sem).wait()


def head_norm(part, gain):
    shaped = part.reshape(part.shape[0] // HD, HD, part.shape[1])
    mean_sq = jnp.mean(shaped * shaped, 1, keepdims=True)
    return (shaped * lax.rsqrt(mean_sq + 1e-06)).reshape(part.shape) * gain


def attend(q_t, sides, mask=None):
    total = None
    for k_t, v_t in sides:
        scores = mm(k_t.T.astype(BF16), q_t.astype(BF16))
        expd = jnp.exp2(scores * SCALE)
        if mask is not None:
            expd = jnp.where(mask, expd, 0.0)
        wide = jnp.concatenate([v_t, jnp.ones((8, v_t.shape[1]), F32)], 0).astype(BF16)
        part = mm(wide, expd.astype(BF16))
        total = part if total is None else total + part
    return total[:HD] / total[HD : HD + 1]


def project_pair(normed, w_q, w_kv, gain):
    q = head_norm(mm_t(w_q, normed[...]), gain[:PAIR])
    kv = mm_t(w_kv, normed[...])
    return q, head_norm(kv[:PAIR], gain[PAIR:]), kv[PAIR:]


def cross_project_kernel(gains, normed, *refs):
    blocks, (q_out, kv_t, w_out, early, late, q_t, weight, sem) = refs[:8], refs[8:]
    slots = {0: weight.at[0], 4: weight.at[1], 1: early.at[0], 5: early.at[1]}
    slots.update({colour: late.at[place] for place, colour in enumerate(LATE)})
    for colour in (0, 4):
        start_fetch(blocks, colour, slots[colour], sem.at[colour])
    for colour in (0, 4):
        wait_fetch(blocks, slots[colour], sem.at[colour])
    for colour in (1, 5) + LATE:
        start_fetch(blocks, colour, slots[colour], sem.at[colour])
    parts = [block.at[pl.ds(0, PAIR)] for block in blocks]
    thirds = [w_out.at[pl.ds(colour * PAIR, PAIR)] for colour in range(4)]
    for colour in range(4):
        start_fetch(parts, colour, thirds[colour], sem.at[8 + colour])
    q, k, v = project_pair(normed, weight[0, PAIR:], weight[1], gains[...].T[:, :1])
    kv_t[...] = jnp.concatenate([k, v], 0).astype(BF16)
    q_t[...] = q.astype(BF16)
    store = pltpu.make_async_copy(q_t, q_out, sem.at[12])
    store.start()
    for colour in (1, 5) + LATE:
        wait_fetch(blocks, slots[colour], sem.at[colour])
    for colour in range(4):
        wait_fetch(parts, thirds[colour], sem.at[8 + colour])
    store.wait()


def time_kernel(gains, normed, weight, out):
    q, k, v = project_pair(normed, weight[0, PAIR:], weight[1], gains[...].T[:, 1:2])
    row = lax.broadcasted_iota(jnp.int32, (HALF, HALF), 0) % 8
    col = lax.broadcasted_iota(jnp.int32, (HALF, HALF), 1) % 8
    sets = []
    for i in range(2):
        part = slice(i * HALF, (i + 1) * HALF)
        heads = []
        for head in range(2):
            at = head * HD
            side = (k[at : at + HD, part], v[at : at + HD, part])
            heads.append(attend(q[at : at + HD, part], [side], row == col))
        sets.append(jnp.concatenate(heads, 0).T.reshape(64, 4, PAIR))
    swap = lax.axis_index("core") == 1
    one = jnp.where(swap, sets[1], sets[0])
    two = jnp.where(swap, sets[0], sets[1])
    out[...] = jnp.concatenate([one, two], 1).reshape(32, 16, PAIR).astype(BF16)


def space_kernel(gains, normed_hbm, weight_hbm, out, normed, result, weight, sem):
    loads = [pltpu.make_async_copy(weight_hbm.at[slot], weight.at[slot], sem.at[slot]) for slot in range(4)]
    loads.insert(0, pltpu.make_async_copy(normed_hbm, normed, sem.at[4]))
    for load in loads:
        load.start()
    columns = gains[...].T[:PAIR]
    loads[0].wait()
    rows = []
    for slot in range(4):
        loads[1 + slot].wait()
        projected = mm_t(weight[slot, (PAIR if slot > 1 else 0) :], normed[...])
        rows += [projected[at : at + HD] for at in range(0, projected.shape[0], HD)]
    heads = []
    for head in range(4):
        q, k, v = rows[3 * head : 3 * head + 3]
        gain = columns[:, 2 + head : 3 + head]
        q, k = head_norm(q, gain[:HD]), head_norm(k, gain[HD:])
        heads.append(attend(q, [(k, v)]))
    result[...] = jnp.concatenate(heads, 0).astype(BF16)
    store = pltpu.make_async_copy(result, out, sem.at[5])
    store.start()
    store.wait()


def cross_kernel(kv_a, kv_b, timed, space_hbm, q_hbm, w_hbm, keep, give, w_out, space, q_t, sem):
    w_load = pltpu.make_async_copy(w_hbm, w_out, sem.at[2])
    w_load.start()
    loads = [pltpu.make_async_copy(q_hbm, q_t, sem.at[0]), pltpu.make_async_copy(space_hbm, space, sem.at[1])]
    for load in loads:
        load.start()
    both = [ref[...].astype(F32) for ref in (kv_a, kv_b)]
    loads[0].wait()
    query = q_t[...].astype(F32)
    heads = []
    for head in range(2):
        at = head * HD
        sides = [(kv[at : at + HD], kv[PAIR + at : PAIR + at + HD]) for kv in both]
        heads.append(attend(query[at : at + HD], sides))
    loads[1].wait()
    mixed = jnp.concatenate([space[...].astype(F32)] + heads, 0).T
    late = timed[...].astype(F32)
    late = [late[:, i * 8 : i * 8 + 8].reshape(HALF, PAIR) for i in range(2)]
    swap = lax.axis_index("core") == 1
    keep[...] = jnp.concatenate([mixed[:HALF], jnp.where(swap, late[1], late[0])], 1).astype(BF16)
    give[...] = jnp.concatenate([mixed[HALF:], jnp.where(swap, late[0], late[1])], 1).astype(BF16)
    w_load.wait()


def out_kernel(tokens, own, arrived, w_own, w_other, embed_hbm, out, cam_embed, sem):
    load = pltpu.make_async_copy(embed_hbm, cam_embed, sem)
    load.start()
    swap = lax.axis_index("core") == 1
    mine, theirs = own[...].astype(F32), arrived[...].astype(F32)
    first = jnp.where(swap, theirs, mine)
    second = jnp.where(swap, mine, theirs)
    parts = []
    for start, end in ((0, 2 * PAIR), (2 * PAIR, 3 * PAIR), (3 * PAIR, 4 * PAIR)):
        parts += [first[:, start:end], second[:, start:end]]
    mixed = jnp.concatenate(parts, 1).astype(BF16)
    one, two = mm_t(mixed, w_own[...]), mm_t(mixed, w_other[...])
    update = jnp.concatenate([jnp.where(swap, two, one), jnp.where(swap, one, two)], 1)
    load.wait()
    out[...] = (tokens[...].astype(F32) + own_embed(cam_embed) + update).astype(BF16)


def call(kernel, out_shapes, args, scratch=(), flops=0, anys=0, room=VMEM_LIMIT):
    vmem = pl.BlockSpec(memory_space=pltpu.VMEM)
    hbm = pl.BlockSpec(memory_space=pltpu.HBM)
    specs = []
    for i in range(len(args)):
        specs.append(hbm if i >= len(args) - anys else vmem)

    def place(out):
        return pl.BlockSpec(memory_space=pl.ANY) if hasattr(out, "memory_space") else vmem

    single = not isinstance(out_shapes, tuple)
    return pl.pallas_call(
        kernel,
        out_shape=out_shapes,
        in_specs=specs,
        out_specs=place(out_shapes) if single else tuple(place(out) for out in out_shapes),
        scratch_shapes=list(scratch),
        compiler_params=pltpu.CompilerParams(vmem_limit_bytes=room),
        cost_estimate=pl.CostEstimate(flops=flops, bytes_accessed=1, transcendentals=0),
    )(*args)


def shape(*dims):
    return jax.ShapeDtypeStruct(dims, BF16)


def far(*dims):
    return pltpu.HBM(dims, BF16)


def near(*dims):
    return pltpu.VMEM(dims, BF16)


def keep_near(array):
    return pltpu.with_memory_space_constraint(array, pltpu.VMEM)


def stay(array):
    return pltpu.with_memory_space_constraint(array, pltpu.HBM)


def local(frames_in, cam_embed, norm_gain, q_gain, k_gain, w_qkv, w_out):
    tokens = frames_in[0]
    core = lax.axis_index("core")
    gain = norm_gain[None]
    both = jnp.stack([q_gain.reshape(HEADS, HD), k_gain.reshape(HEADS, HD)], 1)

    def gains_of(head, count):
        return lax.dynamic_slice_in_dim(both, head, count, 0)

    pair_gains = jnp.stack([gains_of(8 + 2 * core, 2), gains_of(12 + 2 * core, 2)])
    pair_gains = pair_gains.transpose(0, 2, 1, 3).reshape(2, 2 * PAIR)
    space_gains = gains_of(4 * core, 4).reshape(4, PAIR)
    gains = jnp.concatenate([pair_gains, jnp.pad(space_gains, ((0, 2), (0, PAIR)))], 0)

    pieces = call(
        pack_kernel,
        far(64, PIECE, 128),
        (w_qkv, w_out, tokens),
        [
            pltpu.VMEM((18, 3 * D), BF16),
            pltpu.VMEM((18, D), BF16),
            pltpu.VMEM((HALF, D), BF16),
            pltpu.VMEM((16, 44, 128), F32),
            pltpu.VMEM((64, PIECE, 128), BF16),
            pltpu.SemaphoreType.DMA((4,)),
        ],
        0,
        3,
        58 * 1024 * 1024,
    )
    got = lax.all_to_all(pieces, SLAB, 0, 0, tiled=True)
    other = swap_core(tokens)
    normed = keep_near(call(norm_kernel, shape(ROWS, D), (tokens, other, cam_embed, gain), (), 8 * 10**9))
    own_block, block, time_own = call(
        unpack_kernel,
        (near(QUAD, D), far(QUAD, D), far(HALF, D)),
        (after(got, normed, gains),),
        [
            pltpu.VMEM((QUAD, D), BF16),
            pltpu.VMEM((HALF, D), BF16),
            pltpu.VMEM((3, D, 128), F32),
            pltpu.SemaphoreType.DMA((3,)),
        ],
    )
    blocks = [keep_near(own_block)]
    for way in (X_NEXT, Y_NEXT, X_LAST, Z_NEXT, Y_LAST, None, Z_LAST):
        if way is None:
            blocks.append(lax.ppermute(blocks[1], EVERY, X_NEXT))
        else:
            blocks.append(lax.ppermute(block, EVERY, way))
    blocks = tuple(blocks)
    time_other = swap_core(time_own)
    time_normed = keep_near(call(norm_kernel, shape(ROWS, D), (time_own, time_other, cam_embed, gain), (), 8 * 10**9))
    q_t, kv_t, w_own, early, late = call(
        cross_project_kernel,
        (far(PAIR, ROWS), shape(2 * PAIR, ROWS), near(4 * PAIR, D), near(2, QUAD, D), far(4, QUAD, D)),
        (gains, normed) + blocks,
        [pltpu.VMEM((PAIR, ROWS), BF16), pltpu.VMEM((2, QUAD, D), BF16), pltpu.SemaphoreType.DMA((13,))],
        0,
        8,
    )
    kv_a = lax.ppermute(kv_t, EVERY, ACROSS)
    timed = call(time_kernel, shape(32, 16, PAIR), (gains, after(time_normed, kv_t), keep_near(early)))
    kv_b = lax.ppermute(after(kv_a, timed), EVERY, ALONG)
    space = call(
        space_kernel,
        far(2 * PAIR, ROWS),
        (gains, stay(after(normed, timed)), stay(late)),
        [
            pltpu.VMEM((ROWS, D), BF16),
            pltpu.VMEM((2 * PAIR, ROWS), BF16),
            pltpu.VMEM((4, QUAD, D), BF16),
            pltpu.SemaphoreType.DMA((6,)),
        ],
        16 * 10**9,
        2,
    )
    returned = lax.all_to_all(timed, CHIP, 0, 0, tiled=True)
    w_other = swap_core(w_own)
    keep, give, w_other = call(
        cross_kernel,
        (shape(HALF, 4 * PAIR), shape(HALF, 4 * PAIR), near(4 * PAIR, D)),
        (kv_a, kv_b, returned, stay(space), stay(q_t), w_other),
        [pltpu.VMEM((2 * PAIR, ROWS), BF16), pltpu.VMEM((PAIR, ROWS), BF16), pltpu.SemaphoreType.DMA((3,))],
        0,
        3,
    )
    arrived = swap_core(give)
    return call(
        out_kernel,
        shape(HALF, D),
        (tokens, keep, arrived, w_own, keep_near(w_other), stay(cam_embed)),
        [pltpu.VMEM((8, D), F32), pltpu.SemaphoreType.DMA],
        0,
        1,
    )[None]


def solution(mesh):
    fine = Mesh(mesh.devices.reshape(4, 2, 4, 8, 2), EVERY)
    placed = (P(CAM, SLAB, None), P(), P(), P(), P(), P(SLAB, None), P(SLAB, None))
    return jax.shard_map(local, mesh=fine, in_specs=placed, out_specs=P(CAM, SLAB, None), check_vma=False)
```

```python
import jax
import jax.numpy as jnp
from jax import lax
from jax.experimental import pallas as pl
from jax.experimental.pallas import tpu as pltpu
from jax.sharding import Mesh
from jax.sharding import PartitionSpec as P

HEADS = 16
HD = 72
D = HEADS * HD
PAIR = 2 * HD
QUAD = 4 * HD
HALF = 256
ROWS = 2 * HALF
PIECE = 80
LATE = (6, 7, 2, 3)
CAM = ("x", "yh")
CHIP = ("yl", "z")
SLAB = ("yl", "z", "core")
EVERY = ("x", "yh", "yl", "z", "core")
SCALE = 1.4426950408889634 / HD**0.5
F32 = jnp.float32
BF16 = jnp.bfloat16
VMEM_LIMIT = 18 * 1024 * 1024


def route(move):
    pairs = []
    for x in range(4):
        for y in range(8):
            for z in range(8):
                for core in range(2):
                    a, b, c = move(x, y, z, core)
                    source = ((x * 8 + y) * 8 + z) * 2 + core
                    pairs.append((source, ((a % 4 * 8 + b % 8) * 8 + c % 8) * 2 + core))
    return pairs


def towards(core):
    return 1 if core else -1


TURNS = (0, 2, 1, 6, 3, 7, 4, 5)


def bring(offset):
    a, b, c = offset
    return route(lambda x, y, z, core: (x + a * towards(core), y + b * towards(core), z + c * towards(core)))


X_NEXT, X_LAST = bring((1, 0, 0)), bring((-1, 0, 0))
Y_NEXT, Y_LAST = bring((0, 1, 0)), bring((0, -1, 0))
Z_NEXT, Z_LAST = bring((0, 0, 1)), bring((0, 0, -1))
ACROSS = route(lambda x, y, z, core: (x, y + 4, z))
ALONG = route(lambda x, y, z, core: (x + (1 if y < 4 else -1), y, z))


def swap_core(block):
    return lax.ppermute(block, "core", [(0, 1), (1, 0)])


def mm(a, b):
    return jnp.dot(a, b, preferred_element_type=F32)


def mm_t(a, b):
    return lax.dot_general(a, b, (((1,), (1,)), ((), ())), preferred_element_type=F32)


def position():
    return [lax.axis_index(axis) for axis in EVERY]


def after(value, *others):
    return lax.optimization_barrier((value,) + others)[0]


def pack_kernel(w_qkv_hbm, w_out_hbm, tokens_hbm, out, w_qkv, w_out, tokens, pieces, staged, sem):
    loads = [
        pltpu.make_async_copy(w_qkv_hbm, w_qkv, sem.at[0]),
        pltpu.make_async_copy(w_out_hbm, w_out, sem.at[1]),
        pltpu.make_async_copy(tokens_hbm, tokens, sem.at[2]),
    ]
    for load in loads:
        load.start()
    for load in loads[:2]:
        load.wait()

    def columns(kind, head):
        start = kind * D + head * HD
        return w_qkv[:, start : start + HD].astype(F32)

    for who in range(2):
        a, b, c = 8 + 2 * who, 12 + 2 * who, 4 * who
        content = (
            ((0, a), (0, a + 1)),
            ((0, b), (0, b + 1)),
            ((2, c + 2), (0, c + 3)),
            ((1, c + 3), (2, c + 3)),
            ((1, a), (1, a + 1), (2, a), (2, a + 1)),
            ((1, b), (1, b + 1), (2, b), (2, b + 1)),
            ((0, c), (1, c), (2, c), (0, c + 1)),
            ((1, c + 1), (2, c + 1), (0, c + 2), (1, c + 2)),
        )
        for colour in range(8):
            parts = [columns(*one) for one in content[colour]]
            if colour < 4:
                start = (who * 4 + colour) * PAIR
                parts = [w_out[:, start : start + PAIR].astype(F32)] + parts
            whole = jnp.concatenate(parts, 1)
            place = who * 8 + colour
            pieces[place, :18] = whole[:, :128]
            pieces[place, 18:36] = whole[:, 128:256]
            tail = whole[:, 256:]
            pieces[place, 36:41] = jnp.concatenate([tail[:5], tail[5:10], tail[9:14], tail[13:18]], 1)
            pieces[place, 41:] = jnp.zeros((3, 128), F32)
    x, yh = position()[:2]
    base = 2 * x + 4 * yh
    loads[2].wait()
    stores = []
    for dest in range(64):
        colour = (base + dest // 16 + 3 * (dest // 2 % 8)) % 8
        block = tokens[dest // 2 * 8 : dest // 2 * 8 + 8].astype(F32)
        block = block[dest % 2 * 4 : dest % 2 * 4 + 4]
        rows = [block[:, tile * 128 : tile * 128 + 128] for tile in range(9)]
        rows = [pieces[dest % 2 * 8 + colour]] + rows
        staged[dest] = jnp.concatenate(rows, 0).astype(BF16)
        stores.append(pltpu.make_async_copy(staged.at[dest], out.at[dest], sem.at[3]))
        stores[-1].start()
    for store in stores:
        store.wait()


def unpack_kernel(got, own_out, block_out, tokens_out, block, tokens, wide, sem):
    for source in range(64):
        rows = got[source].astype(F32)
        at = source * 18
        wide[0, at : at + 18] = rows[:18]
        wide[1, at : at + 18] = rows[18:36]
        wide[2, at : at + 5, :32] = rows[36:41, :32]
        wide[2, at + 5 : at + 10, :32] = rows[36:41, 32:64]
        wide[2, at + 10 : at + 14, :32] = rows[37:41, 64:96]
        wide[2, at + 14 : at + 18, :32] = rows[37:41, 96:]
    block[:128] = wide[0].T.astype(BF16)
    block[128:256] = wide[1].T.astype(BF16)
    block[256:] = wide[2].T[:32].astype(BF16)
    stores = [
        pltpu.make_async_copy(block, block_out, sem.at[0]),
        pltpu.make_async_copy(block, own_out, sem.at[1]),
        pltpu.make_async_copy(tokens, tokens_out, sem.at[2]),
    ]
    for store in stores[:2]:
        store.start()
    for source in range(0, 64, 2):
        pair = [got[source + i].astype(F32) for i in range(2)]
        tiles = []
        for tile in range(9):
            start = 44 + tile * 4
            tiles.append(jnp.concatenate([one[start : start + 4] for one in pair], 0))
        tokens[source * 4 : source * 4 + 8] = jnp.concatenate(tiles, 1).astype(BF16)
    stores[2].start()
    for store in stores:
        store.wait()


def own_embed(cam_embed):
    return cam_embed[pl.ds(lax.axis_index("x") * 2 + lax.axis_index("yh"), 1)]


def normalise(ref, embed, gain):
    hidden = ref[...].astype(F32) + embed
    centred = hidden - jnp.mean(hidden, -1, keepdims=True)
    variance = jnp.mean(centred * centred, -1, keepdims=True)
    return (centred * lax.rsqrt(variance + 1e-06) * gain[...]).astype(BF16)


def norm_kernel(own, other, cam_embed, gain, out):
    for i, ref in enumerate((own, other)):
        out[i * HALF : (i + 1) * HALF] = normalise(ref, own_embed(cam_embed), gain)


def start_fetch(blocks, colour, slot, sem):
    x, yh, yl, z, core = position()
    ahead = colour - (2 * x + 4 * yh + yl + 3 * z) + 64
    turn = lax.rem(jnp.where(core == 0, ahead, 128 - ahead), 8)
    for block, own in zip(blocks, TURNS):
        @pl.when(turn == own)
        def _(block=block):
            pltpu.make_async_copy(block, slot, sem).start()


def wait_fetch(blocks, slot, sem):
    pltpu.make_async_copy(blocks[0], slot, sem).wait()


def head_norm(part, gain):
    shaped = part.reshape(part.shape[0] // HD, HD, part.shape[1])
    mean_sq = jnp.mean(shaped * shaped, 1, keepdims=True)
    return (shaped * lax.rsqrt(mean_sq + 1e-06)).reshape(part.shape) * gain


def attend(q_t, sides, mask=None):
    total = None
    for k_t, v_t in sides:
        scores = mm(k_t.T.astype(BF16), q_t.astype(BF16))
        expd = jnp.exp2(scores * SCALE)
        if mask is not None:
            expd = jnp.where(mask, expd, 0.0)
        wide = jnp.concatenate([v_t, jnp.ones((8, v_t.shape[1]), F32)], 0).astype(BF16)
        part = mm(wide, expd.astype(BF16))
        total = part if total is None else total + part
    return total[:HD] / total[HD : HD + 1]


def project_pair(normed, w_q, w_kv, gain):
    q = head_norm(mm_t(w_q, normed[...]), gain[:PAIR])
    kv = mm_t(w_kv, normed[...])
    return q, head_norm(kv[:PAIR], gain[PAIR:]), kv[PAIR:]


def cross_project_kernel(gains, normed, *refs):
    blocks, (q_out, kv_t, q_t, weight, sem) = refs[:8], refs[8:]
    for slot, colour in enumerate((0, 4)):
        start_fetch(blocks, colour, weight.at[slot], sem.at[slot])
    for slot in range(2):
        wait_fetch(blocks, weight.at[slot], sem.at[slot])
    q, k, v = project_pair(normed, weight[0, PAIR:], weight[1], gains[...].T[:, :1])
    q_t[...] = q.astype(BF16)
    store = pltpu.make_async_copy(q_t, q_out, sem.at[2])
    store.start()
    kv_t[...] = jnp.concatenate([k, v], 0).astype(BF16)
    store.wait()


def time_kernel(gains, normed, *refs):
    blocks, (out, w_out, late, weight, sem) = refs[:8], refs[8:]
    for slot, colour in enumerate((1, 5)):
        start_fetch(blocks, colour, weight.at[slot], sem.at[slot])
    for slot in range(2):
        wait_fetch(blocks, weight.at[slot], sem.at[slot])
    for place, colour in enumerate(LATE):
        start_fetch(blocks, colour, late.at[place], sem.at[2 + place])
    parts = [block.at[pl.ds(0, PAIR)] for block in blocks]
    thirds = [w_out.at[pl.ds(colour * PAIR, PAIR)] for colour in range(4)]
    for colour in range(4):
        start_fetch(parts, colour, thirds[colour], sem.at[6 + colour])
    q, k, v = project_pair(normed, weight[0, PAIR:], weight[1], gains[...].T[:, 1:2])
    row = lax.broadcasted_iota(jnp.int32, (HALF, HALF), 0) % 8
    col = lax.broadcasted_iota(jnp.int32, (HALF, HALF), 1) % 8
    sets = []
    for i in range(2):
        part = slice(i * HALF, (i + 1) * HALF)
        heads = []
        for head in range(2):
            at = head * HD
            side = (k[at : at + HD, part], v[at : at + HD, part])
            heads.append(attend(q[at : at + HD, part], [side], row == col))
        sets.append(jnp.concatenate(heads, 0).T.reshape(64, 4, PAIR))
    swap = lax.axis_index("core") == 1
    one = jnp.where(swap, sets[1], sets[0])
    two = jnp.where(swap, sets[0], sets[1])
    out[...] = jnp.concatenate([one, two], 1).reshape(32, 16, PAIR).astype(BF16)
    for place in range(4):
        wait_fetch(blocks, late.at[place], sem.at[2 + place])
    for colour in range(4):
        wait_fetch(parts, thirds[colour], sem.at[6 + colour])


def space_kernel(gains, normed_hbm, weight_hbm, out, normed, result, weight, sem):
    loads = [pltpu.make_async_copy(weight_hbm.at[slot], weight.at[slot], sem.at[slot]) for slot in range(4)]
    loads.insert(0, pltpu.make_async_copy(normed_hbm, normed, sem.at[4]))
    for load in loads:
        load.start()
    columns = gains[...].T[:PAIR]
    loads[0].wait()
    rows = []
    for slot in range(4):
        loads[1 + slot].wait()
        projected = mm_t(weight[slot, (PAIR if slot > 1 else 0) :], normed[...])
        rows += [projected[at : at + HD] for at in range(0, projected.shape[0], HD)]
    heads = []
    for head in range(4):
        q, k, v = rows[3 * head : 3 * head + 3]
        gain = columns[:, 2 + head : 3 + head]
        q, k = head_norm(q, gain[:HD]), head_norm(k, gain[HD:])
        heads.append(attend(q, [(k, v)]))
    result[...] = jnp.concatenate(heads, 0).astype(BF16)
    store = pltpu.make_async_copy(result, out, sem.at[5])
    store.start()
    store.wait()


def cross_kernel(kv_a, kv_b, timed, space_hbm, q_hbm, w_hbm, keep, give, w_out, space, q_t, sem):
    w_load = pltpu.make_async_copy(w_hbm, w_out, sem.at[2])
    w_load.start()
    loads = [pltpu.make_async_copy(q_hbm, q_t, sem.at[0]), pltpu.make_async_copy(space_hbm, space, sem.at[1])]
    for load in loads:
        load.start()
    both = [ref[...].astype(F32) for ref in (kv_a, kv_b)]
    loads[0].wait()
    query = q_t[...].astype(F32)
    heads = []
    for head in range(2):
        at = head * HD
        sides = [(kv[at : at + HD], kv[PAIR + at : PAIR + at + HD]) for kv in both]
        heads.append(attend(query[at : at + HD], sides))
    loads[1].wait()
    mixed = jnp.concatenate([space[...].astype(F32)] + heads, 0).T
    late = timed[...].astype(F32)
    late = [late[:, i * 8 : i * 8 + 8].reshape(HALF, PAIR) for i in range(2)]
    swap = lax.axis_index("core") == 1
    keep[...] = jnp.concatenate([mixed[:HALF], jnp.where(swap, late[1], late[0])], 1).astype(BF16)
    give[...] = jnp.concatenate([mixed[HALF:], jnp.where(swap, late[0], late[1])], 1).astype(BF16)
    w_load.wait()


def out_kernel(tokens, own, arrived, w_own, w_other, embed_hbm, out, cam_embed, sem):
    load = pltpu.make_async_copy(embed_hbm, cam_embed, sem)
    load.start()
    swap = lax.axis_index("core") == 1
    mine, theirs = own[...].astype(F32), arrived[...].astype(F32)
    first = jnp.where(swap, theirs, mine)
    second = jnp.where(swap, mine, theirs)
    parts = []
    for start, end in ((0, 2 * PAIR), (2 * PAIR, 3 * PAIR), (3 * PAIR, 4 * PAIR)):
        parts += [first[:, start:end], second[:, start:end]]
    mixed = jnp.concatenate(parts, 1).astype(BF16)
    one, two = mm_t(mixed, w_own[...]), mm_t(mixed, w_other[...])
    update = jnp.concatenate([jnp.where(swap, two, one), jnp.where(swap, one, two)], 1)
    load.wait()
    out[...] = (tokens[...].astype(F32) + own_embed(cam_embed) + update).astype(BF16)


def call(kernel, out_shapes, args, scratch=(), flops=0, anys=0, room=VMEM_LIMIT):
    vmem = pl.BlockSpec(memory_space=pltpu.VMEM)
    hbm = pl.BlockSpec(memory_space=pltpu.HBM)
    specs = []
    for i in range(len(args)):
        specs.append(hbm if i >= len(args) - anys else vmem)

    def place(out):
        return pl.BlockSpec(memory_space=pl.ANY) if hasattr(out, "memory_space") else vmem

    single = not isinstance(out_shapes, tuple)
    return pl.pallas_call(
        kernel,
        out_shape=out_shapes,
        in_specs=specs,
        out_specs=place(out_shapes) if single else tuple(place(out) for out in out_shapes),
        scratch_shapes=list(scratch),
        compiler_params=pltpu.CompilerParams(vmem_limit_bytes=room),
        cost_estimate=pl.CostEstimate(flops=flops, bytes_accessed=1, transcendentals=0),
    )(*args)


def shape(*dims):
    return jax.ShapeDtypeStruct(dims, BF16)


def far(*dims):
    return pltpu.HBM(dims, BF16)


def near(*dims):
    return pltpu.VMEM(dims, BF16)


def keep_near(array):
    return pltpu.with_memory_space_constraint(array, pltpu.VMEM)


def stay(array):
    return pltpu.with_memory_space_constraint(array, pltpu.HBM)


def local(frames_in, cam_embed, norm_gain, q_gain, k_gain, w_qkv, w_out):
    tokens = frames_in[0]
    core = lax.axis_index("core")
    gain = norm_gain[None]
    both = jnp.stack([q_gain.reshape(HEADS, HD), k_gain.reshape(HEADS, HD)], 1)

    def gains_of(head, count):
        return lax.dynamic_slice_in_dim(both, head, count, 0)

    pair_gains = jnp.stack([gains_of(8 + 2 * core, 2), gains_of(12 + 2 * core, 2)])
    pair_gains = pair_gains.transpose(0, 2, 1, 3).reshape(2, 2 * PAIR)
    space_gains = gains_of(4 * core, 4).reshape(4, PAIR)
    gains = jnp.concatenate([pair_gains, jnp.pad(space_gains, ((0, 2), (0, PAIR)))], 0)

    pieces = call(
        pack_kernel,
        far(64, PIECE, 128),
        (w_qkv, w_out, tokens),
        [
            pltpu.VMEM((18, 3 * D), BF16),
            pltpu.VMEM((18, D), BF16),
            pltpu.VMEM((HALF, D), BF16),
            pltpu.VMEM((16, 44, 128), F32),
            pltpu.VMEM((64, PIECE, 128), BF16),
            pltpu.SemaphoreType.DMA((4,)),
        ],
        0,
        3,
        58 * 1024 * 1024,
    )
    got = lax.all_to_all(pieces, SLAB, 0, 0, tiled=True)
    other = swap_core(tokens)
    normed = keep_near(call(norm_kernel, shape(ROWS, D), (tokens, other, cam_embed, gain), (), 8 * 10**9))
    own_block, block, time_own = call(
        unpack_kernel,
        (near(QUAD, D), far(QUAD, D), far(HALF, D)),
        (after(got, normed, gains),),
        [
            pltpu.VMEM((QUAD, D), BF16),
            pltpu.VMEM((HALF, D), BF16),
            pltpu.VMEM((3, D, 128), F32),
            pltpu.SemaphoreType.DMA((3,)),
        ],
    )
    blocks = [keep_near(own_block)]
    for way in (X_NEXT, Y_NEXT, X_LAST, Z_NEXT, Y_LAST, None, Z_LAST):
        if way is None:
            blocks.append(lax.ppermute(blocks[1], EVERY, X_NEXT))
        else:
            blocks.append(lax.ppermute(block, EVERY, way))
    blocks = tuple(blocks)
    time_other = swap_core(time_own)
    time_normed = keep_near(call(norm_kernel, shape(ROWS, D), (time_own, time_other, cam_embed, gain), (), 8 * 10**9))
    q_t, kv_t = call(
        cross_project_kernel,
        (far(PAIR, ROWS), shape(2 * PAIR, ROWS)),
        (gains, normed) + blocks,
        [pltpu.VMEM((PAIR, ROWS), BF16), pltpu.VMEM((2, QUAD, D), BF16), pltpu.SemaphoreType.DMA((3,))],
        0,
        8,
    )
    kv_a = lax.ppermute(kv_t, EVERY, ACROSS)
    timed, w_own, late = call(
        time_kernel,
        (shape(32, 16, PAIR), near(4 * PAIR, D), far(4, QUAD, D)),
        (gains, after(time_normed, kv_t)) + blocks,
        [pltpu.VMEM((2, QUAD, D), BF16), pltpu.SemaphoreType.DMA((10,))],
        0,
        8,
    )
    w_other = swap_core(w_own)
    kv_b = lax.ppermute(after(kv_a, timed), EVERY, ALONG)
    space = call(
        space_kernel,
        far(2 * PAIR, ROWS),
        (gains, stay(after(normed, timed)), stay(late)),
        [
            pltpu.VMEM((ROWS, D), BF16),
            pltpu.VMEM((2 * PAIR, ROWS), BF16),
            pltpu.VMEM((4, QUAD, D), BF16),
            pltpu.SemaphoreType.DMA((6,)),
        ],
        16 * 10**9,
        2,
    )
    returned = lax.all_to_all(timed, CHIP, 0, 0, tiled=True)
    keep, give, w_other = call(
        cross_kernel,
        (shape(HALF, 4 * PAIR), shape(HALF, 4 * PAIR), near(4 * PAIR, D)),
        (kv_a, kv_b, returned, stay(space), stay(q_t), w_other),
        [pltpu.VMEM((2 * PAIR, ROWS), BF16), pltpu.VMEM((PAIR, ROWS), BF16), pltpu.SemaphoreType.DMA((3,))],
        0,
        3,
    )
    arrived = swap_core(give)
    return call(
        out_kernel,
        shape(HALF, D),
        (tokens, keep, arrived, w_own, keep_near(w_other), stay(cam_embed)),
        [pltpu.VMEM((8, D), F32), pltpu.SemaphoreType.DMA],
        0,
        1,
    )[None]


def solution(mesh):
    fine = Mesh(mesh.devices.reshape(4, 2, 4, 8, 2), EVERY)
    placed = (P(CAM, SLAB, None), P(), P(), P(), P(), P(SLAB, None), P(SLAB, None))
    return jax.shard_map(local, mesh=fine, in_specs=placed, out_specs=P(CAM, SLAB, None), check_vma=False)
```

```python
import jax
import jax.numpy as jnp
from jax import lax
from jax.experimental import pallas as pl
from jax.experimental.pallas import tpu as pltpu
from jax.sharding import Mesh
from jax.sharding import PartitionSpec as P

HEADS = 16
HD = 72
D = HEADS * HD
PAIR = 2 * HD
QUAD = 4 * HD
HALF = 256
ROWS = 2 * HALF
PIECE = 80
LATE = (6, 7, 2, 3)
CAM = ("x", "yh")
CHIP = ("yl", "z")
SLAB = ("yl", "z", "core")
EVERY = ("x", "yh", "yl", "z", "core")
SCALE = 1.4426950408889634 / HD**0.5
F32 = jnp.float32
BF16 = jnp.bfloat16
VMEM_LIMIT = 18 * 1024 * 1024


def route(move):
    pairs = []
    for x in range(4):
        for y in range(8):
            for z in range(8):
                for core in range(2):
                    a, b, c = move(x, y, z, core)
                    source = ((x * 8 + y) * 8 + z) * 2 + core
                    pairs.append((source, ((a % 4 * 8 + b % 8) * 8 + c % 8) * 2 + core))
    return pairs


def towards(core):
    return 1 if core else -1


TURNS = (0, 2, 1, 3, 7, 6, 4, 5)


def bring(offset):
    a, b, c = offset
    return route(lambda x, y, z, core: (x + a * towards(core), y + b * towards(core), z + c * towards(core)))


X_NEXT, X_LAST = bring((1, 0, 0)), bring((-1, 0, 0))
Y_NEXT, Y_LAST = bring((0, 1, 0)), bring((0, -1, 0))
Z_NEXT, Z_LAST = bring((0, 0, 1)), bring((0, 0, -1))
ACROSS = route(lambda x, y, z, core: (x, y + 4, z))
ALONG = route(lambda x, y, z, core: (x + (1 if y < 4 else -1), y, z))


def swap_core(block):
    return lax.ppermute(block, "core", [(0, 1), (1, 0)])


def mm(a, b):
    return jnp.dot(a, b, preferred_element_type=F32)


def mm_t(a, b):
    return lax.dot_general(a, b, (((1,), (1,)), ((), ())), preferred_element_type=F32)


def position():
    return [lax.axis_index(axis) for axis in EVERY]


def after(value, *others):
    return lax.optimization_barrier((value,) + others)[0]


def pack_kernel(w_qkv_hbm, w_out_hbm, tokens_hbm, out, w_qkv, w_out, tokens, pieces, staged, sem):
    loads = [
        pltpu.make_async_copy(w_qkv_hbm, w_qkv, sem.at[0]),
        pltpu.make_async_copy(w_out_hbm, w_out, sem.at[1]),
        pltpu.make_async_copy(tokens_hbm, tokens, sem.at[2]),
    ]
    for load in loads:
        load.start()
    for load in loads[:2]:
        load.wait()

    def columns(kind, head):
        start = kind * D + head * HD
        return w_qkv[:, start : start + HD].astype(F32)

    for who in range(2):
        a, b, c = 8 + 2 * who, 12 + 2 * who, 4 * who
        content = (
            ((0, a), (0, a + 1)),
            ((0, b), (0, b + 1)),
            ((2, c + 2), (0, c + 3)),
            ((1, c + 3), (2, c + 3)),
            ((1, a), (1, a + 1), (2, a), (2, a + 1)),
            ((1, b), (1, b + 1), (2, b), (2, b + 1)),
            ((0, c), (1, c), (2, c), (0, c + 1)),
            ((1, c + 1), (2, c + 1), (0, c + 2), (1, c + 2)),
        )
        for colour in range(8):
            parts = [columns(*one) for one in content[colour]]
            if colour < 4:
                start = (who * 4 + colour) * PAIR
                parts = [w_out[:, start : start + PAIR].astype(F32)] + parts
            whole = jnp.concatenate(parts, 1)
            place = who * 8 + colour
            pieces[place, :18] = whole[:, :128]
            pieces[place, 18:36] = whole[:, 128:256]
            tail = whole[:, 256:]
            pieces[place, 36:41] = jnp.concatenate([tail[:5], tail[5:10], tail[9:14], tail[13:18]], 1)
            pieces[place, 41:] = jnp.zeros((3, 128), F32)
    x, yh = position()[:2]
    base = 2 * x + 4 * yh
    loads[2].wait()
    stores = []
    for dest in range(64):
        colour = (base + dest // 16 + 3 * (dest // 2 % 8)) % 8
        block = tokens[dest // 2 * 8 : dest // 2 * 8 + 8].astype(F32)
        block = block[dest % 2 * 4 : dest % 2 * 4 + 4]
        rows = [block[:, tile * 128 : tile * 128 + 128] for tile in range(9)]
        rows = [pieces[dest % 2 * 8 + colour]] + rows
        staged[dest] = jnp.concatenate(rows, 0).astype(BF16)
        stores.append(pltpu.make_async_copy(staged.at[dest], out.at[dest], sem.at[3]))
        stores[-1].start()
    for store in stores:
        store.wait()


def unpack_kernel(got, own_out, block_out, tokens_out, block, tokens, wide, sem):
    for source in range(64):
        rows = got[source].astype(F32)
        at = source * 18
        wide[0, at : at + 18] = rows[:18]
        wide[1, at : at + 18] = rows[18:36]
        wide[2, at : at + 5, :32] = rows[36:41, :32]
        wide[2, at + 5 : at + 10, :32] = rows[36:41, 32:64]
        wide[2, at + 10 : at + 14, :32] = rows[37:41, 64:96]
        wide[2, at + 14 : at + 18, :32] = rows[37:41, 96:]
    block[:128] = wide[0].T.astype(BF16)
    block[128:256] = wide[1].T.astype(BF16)
    block[256:] = wide[2].T[:32].astype(BF16)
    stores = [
        pltpu.make_async_copy(block, block_out, sem.at[0]),
        pltpu.make_async_copy(block, own_out, sem.at[1]),
        pltpu.make_async_copy(tokens, tokens_out, sem.at[2]),
    ]
    for store in stores[:2]:
        store.start()
    for source in range(0, 64, 2):
        pair = [got[source + i].astype(F32) for i in range(2)]
        tiles = []
        for tile in range(9):
            start = 44 + tile * 4
            tiles.append(jnp.concatenate([one[start : start + 4] for one in pair], 0))
        tokens[source * 4 : source * 4 + 8] = jnp.concatenate(tiles, 1).astype(BF16)
    stores[2].start()
    for store in stores:
        store.wait()


def own_embed(cam_embed):
    return cam_embed[pl.ds(lax.axis_index("x") * 2 + lax.axis_index("yh"), 1)]


def normalise(ref, embed, gain):
    hidden = ref[...].astype(F32) + embed
    centred = hidden - jnp.mean(hidden, -1, keepdims=True)
    variance = jnp.mean(centred * centred, -1, keepdims=True)
    return (centred * lax.rsqrt(variance + 1e-06) * gain[...]).astype(BF16)


def norm_kernel(own, other, cam_embed, gain, out):
    for i, ref in enumerate((own, other)):
        out[i * HALF : (i + 1) * HALF] = normalise(ref, own_embed(cam_embed), gain)


def start_fetch(blocks, colour, slot, sem):
    x, yh, yl, z, core = position()
    ahead = colour - (2 * x + 4 * yh + yl + 3 * z) + 64
    turn = lax.rem(jnp.where(core == 0, ahead, 128 - ahead), 8)
    for block, own in zip(blocks, TURNS):
        @pl.when(turn == own)
        def _(block=block):
            pltpu.make_async_copy(block, slot, sem).start()


def wait_fetch(blocks, slot, sem):
    pltpu.make_async_copy(blocks[0], slot, sem).wait()


def head_norm(part, gain):
    shaped = part.reshape(part.shape[0] // HD, HD, part.shape[1])
    mean_sq = jnp.mean(shaped * shaped, 1, keepdims=True)
    return (shaped * lax.rsqrt(mean_sq + 1e-06)).reshape(part.shape) * gain


def attend(q_t, sides, mask=None):
    total = None
    for k_t, v_t in sides:
        scores = mm(k_t.T.astype(BF16), q_t.astype(BF16))
        expd = jnp.exp2(scores * SCALE)
        if mask is not None:
            expd = jnp.where(mask, expd, 0.0)
        wide = jnp.concatenate([v_t, jnp.ones((8, v_t.shape[1]), F32)], 0).astype(BF16)
        part = mm(wide, expd.astype(BF16))
        total = part if total is None else total + part
    return total[:HD] / total[HD : HD + 1]


def project_pair(normed, w_q, w_kv, gain):
    q = head_norm(mm_t(w_q, normed[...]), gain[:PAIR])
    kv = mm_t(w_kv, normed[...])
    return q, head_norm(kv[:PAIR], gain[PAIR:]), kv[PAIR:]


def cross_project_kernel(gains, normed, *refs):
    blocks, (q_out, kv_t, w_out, early, late, q_t, weight, sem) = refs[:8], refs[8:]
    slots = {0: weight.at[0], 4: weight.at[1], 1: early.at[0], 5: early.at[1]}
    slots.update({colour: late.at[place] for place, colour in enumerate(LATE)})
    for colour in (0, 4):
        start_fetch(blocks, colour, slots[colour], sem.at[colour])
    for colour in (0, 4):
        wait_fetch(blocks, slots[colour], sem.at[colour])
    for colour in (1, 5) + LATE:
        start_fetch(blocks, colour, slots[colour], sem.at[colour])
    parts = [block.at[pl.ds(0, PAIR)] for block in blocks]
    thirds = [w_out.at[pl.ds(colour * PAIR, PAIR)] for colour in range(4)]
    for colour in range(4):
        start_fetch(parts, colour, thirds[colour], sem.at[8 + colour])
    q, k, v = project_pair(normed, weight[0, PAIR:], weight[1], gains[...].T[:, :1])
    kv_t[...] = jnp.concatenate([k, v], 0).astype(BF16)
    q_t[...] = q.astype(BF16)
    store = pltpu.make_async_copy(q_t, q_out, sem.at[12])
    store.start()
    for colour in (1, 5) + LATE:
        wait_fetch(blocks, slots[colour], sem.at[colour])
    for colour in range(4):
        wait_fetch(parts, thirds[colour], sem.at[8 + colour])
    store.wait()


def time_kernel(gains, normed, weight, out):
    q, k, v = project_pair(normed, weight[0, PAIR:], weight[1], gains[...].T[:, 1:2])
    row = lax.broadcasted_iota(jnp.int32, (HALF, HALF), 0) % 8
    col = lax.broadcasted_iota(jnp.int32, (HALF, HALF), 1) % 8
    sets = []
    for i in range(2):
        part = slice(i * HALF, (i + 1) * HALF)
        heads = []
        for head in range(2):
            at = head * HD
            side = (k[at : at + HD, part], v[at : at + HD, part])
            heads.append(attend(q[at : at + HD, part], [side], row == col))
        sets.append(jnp.concatenate(heads, 0).T.reshape(64, 4, PAIR))
    swap = lax.axis_index("core") == 1
    one = jnp.where(swap, sets[1], sets[0])
    two = jnp.where(swap, sets[0], sets[1])
    out[...] = jnp.concatenate([one, two], 1).reshape(32, 16, PAIR).astype(BF16)


def space_kernel(gains, normed_hbm, weight_hbm, out, normed, result, weight, sem):
    loads = [pltpu.make_async_copy(weight_hbm.at[slot], weight.at[slot], sem.at[slot]) for slot in range(4)]
    loads.insert(0, pltpu.make_async_copy(normed_hbm, normed, sem.at[4]))
    for load in loads:
        load.start()
    columns = gains[...].T[:PAIR]
    loads[0].wait()
    rows = []
    for slot in range(4):
        loads[1 + slot].wait()
        projected = mm_t(weight[slot, (PAIR if slot > 1 else 0) :], normed[...])
        rows += [projected[at : at + HD] for at in range(0, projected.shape[0], HD)]
    heads = []
    for head in range(4):
        q, k, v = rows[3 * head : 3 * head + 3]
        gain = columns[:, 2 + head : 3 + head]
        q, k = head_norm(q, gain[:HD]), head_norm(k, gain[HD:])
        heads.append(attend(q, [(k, v)]))
    result[...] = jnp.concatenate(heads, 0).astype(BF16)
    store = pltpu.make_async_copy(result, out, sem.at[5])
    store.start()
    store.wait()


def cross_kernel(kv_a, kv_b, timed, space_hbm, q_hbm, w_hbm, keep, give, w_out, space, q_t, sem):
    w_load = pltpu.make_async_copy(w_hbm, w_out, sem.at[2])
    w_load.start()
    loads = [pltpu.make_async_copy(q_hbm, q_t, sem.at[0]), pltpu.make_async_copy(space_hbm, space, sem.at[1])]
    for load in loads:
        load.start()
    both = [ref[...].astype(F32) for ref in (kv_a, kv_b)]
    loads[0].wait()
    query = q_t[...].astype(F32)
    heads = []
    for head in range(2):
        at = head * HD
        sides = [(kv[at : at + HD], kv[PAIR + at : PAIR + at + HD]) for kv in both]
        heads.append(attend(query[at : at + HD], sides))
    loads[1].wait()
    mixed = jnp.concatenate([space[...].astype(F32)] + heads, 0).T
    late = timed[...].astype(F32)
    late = [late[:, i * 8 : i * 8 + 8].reshape(HALF, PAIR) for i in range(2)]
    swap = lax.axis_index("core") == 1
    keep[...] = jnp.concatenate([mixed[:HALF], jnp.where(swap, late[1], late[0])], 1).astype(BF16)
    give[...] = jnp.concatenate([mixed[HALF:], jnp.where(swap, late[0], late[1])], 1).astype(BF16)
    w_load.wait()


def out_kernel(tokens, own, arrived, w_own, w_other, embed_hbm, out, cam_embed, sem):
    load = pltpu.make_async_copy(embed_hbm, cam_embed, sem)
    load.start()
    swap = lax.axis_index("core") == 1
    mine, theirs = own[...].astype(F32), arrived[...].astype(F32)
    first = jnp.where(swap, theirs, mine)
    second = jnp.where(swap, mine, theirs)
    parts = []
    for start, end in ((0, 2 * PAIR), (2 * PAIR, 3 * PAIR), (3 * PAIR, 4 * PAIR)):
        parts += [first[:, start:end], second[:, start:end]]
    mixed = jnp.concatenate(parts, 1).astype(BF16)
    one, two = mm_t(mixed, w_own[...]), mm_t(mixed, w_other[...])
    update = jnp.concatenate([jnp.where(swap, two, one), jnp.where(swap, one, two)], 1)
    load.wait()
    out[...] = (tokens[...].astype(F32) + own_embed(cam_embed) + update).astype(BF16)


def call(kernel, out_shapes, args, scratch=(), flops=0, anys=0, room=VMEM_LIMIT):
    vmem = pl.BlockSpec(memory_space=pltpu.VMEM)
    hbm = pl.BlockSpec(memory_space=pltpu.HBM)
    specs = []
    for i in range(len(args)):
        specs.append(hbm if i >= len(args) - anys else vmem)

    def place(out):
        return pl.BlockSpec(memory_space=pl.ANY) if hasattr(out, "memory_space") else vmem

    single = not isinstance(out_shapes, tuple)
    return pl.pallas_call(
        kernel,
        out_shape=out_shapes,
        in_specs=specs,
        out_specs=place(out_shapes) if single else tuple(place(out) for out in out_shapes),
        scratch_shapes=list(scratch),
        compiler_params=pltpu.CompilerParams(vmem_limit_bytes=room),
        cost_estimate=pl.CostEstimate(flops=flops, bytes_accessed=1, transcendentals=0),
    )(*args)


def shape(*dims):
    return jax.ShapeDtypeStruct(dims, BF16)


def far(*dims):
    return pltpu.HBM(dims, BF16)


def near(*dims):
    return pltpu.VMEM(dims, BF16)


def keep_near(array):
    return pltpu.with_memory_space_constraint(array, pltpu.VMEM)


def stay(array):
    return pltpu.with_memory_space_constraint(array, pltpu.HBM)


def local(frames_in, cam_embed, norm_gain, q_gain, k_gain, w_qkv, w_out):
    tokens = frames_in[0]
    core = lax.axis_index("core")
    gain = norm_gain[None]
    both = jnp.stack([q_gain.reshape(HEADS, HD), k_gain.reshape(HEADS, HD)], 1)

    def gains_of(head, count):
        return lax.dynamic_slice_in_dim(both, head, count, 0)

    pair_gains = jnp.stack([gains_of(8 + 2 * core, 2), gains_of(12 + 2 * core, 2)])
    pair_gains = pair_gains.transpose(0, 2, 1, 3).reshape(2, 2 * PAIR)
    space_gains = gains_of(4 * core, 4).reshape(4, PAIR)
    gains = jnp.concatenate([pair_gains, jnp.pad(space_gains, ((0, 2), (0, PAIR)))], 0)

    pieces = call(
        pack_kernel,
        far(64, PIECE, 128),
        (w_qkv, w_out, tokens),
        [
            pltpu.VMEM((18, 3 * D), BF16),
            pltpu.VMEM((18, D), BF16),
            pltpu.VMEM((HALF, D), BF16),
            pltpu.VMEM((16, 44, 128), F32),
            pltpu.VMEM((64, PIECE, 128), BF16),
            pltpu.SemaphoreType.DMA((4,)),
        ],
        0,
        3,
        58 * 1024 * 1024,
    )
    got = lax.all_to_all(pieces, SLAB, 0, 0, tiled=True)
    other = swap_core(tokens)
    normed = keep_near(call(norm_kernel, shape(ROWS, D), (tokens, other, cam_embed, gain), (), 8 * 10**9))
    own_block, block, time_own = call(
        unpack_kernel,
        (near(QUAD, D), far(QUAD, D), far(HALF, D)),
        (after(got, normed, gains),),
        [
            pltpu.VMEM((QUAD, D), BF16),
            pltpu.VMEM((HALF, D), BF16),
            pltpu.VMEM((3, D, 128), F32),
            pltpu.SemaphoreType.DMA((3,)),
        ],
    )
    blocks = [keep_near(own_block)]
    for way in (X_NEXT, Y_NEXT, Z_NEXT, Y_LAST, X_LAST, None, Z_LAST):
        if way is None:
            blocks.append(lax.ppermute(blocks[1], EVERY, X_NEXT))
        else:
            blocks.append(lax.ppermute(block, EVERY, way))
    blocks = tuple(blocks)
    time_other = swap_core(time_own)
    time_normed = keep_near(call(norm_kernel, shape(ROWS, D), (time_own, time_other, cam_embed, gain), (), 8 * 10**9))
    q_t, kv_t, w_own, early, late = call(
        cross_project_kernel,
        (far(PAIR, ROWS), shape(2 * PAIR, ROWS), near(4 * PAIR, D), near(2, QUAD, D), far(4, QUAD, D)),
        (gains, after(normed, time_normed)) + blocks,
        [pltpu.VMEM((PAIR, ROWS), BF16), pltpu.VMEM((2, QUAD, D), BF16), pltpu.SemaphoreType.DMA((13,))],
        0,
        8,
    )
    kv_a = lax.ppermute(kv_t, EVERY, ACROSS)
    timed = call(time_kernel, shape(32, 16, PAIR), (gains, time_normed, keep_near(early)))
    kv_b = lax.ppermute(after(kv_a, timed), EVERY, ALONG)
    space = call(
        space_kernel,
        far(2 * PAIR, ROWS),
        (gains, stay(after(normed, timed)), stay(late)),
        [
            pltpu.VMEM((ROWS, D), BF16),
            pltpu.VMEM((2 * PAIR, ROWS), BF16),
            pltpu.VMEM((4, QUAD, D), BF16),
            pltpu.SemaphoreType.DMA((6,)),
        ],
        16 * 10**9,
        2,
    )
    returned = lax.all_to_all(timed, CHIP, 0, 0, tiled=True)
    w_other = swap_core(w_own)
    keep, give, w_other = call(
        cross_kernel,
        (shape(HALF, 4 * PAIR), shape(HALF, 4 * PAIR), near(4 * PAIR, D)),
        (kv_a, kv_b, returned, stay(space), stay(q_t), w_other),
        [pltpu.VMEM((2 * PAIR, ROWS), BF16), pltpu.VMEM((PAIR, ROWS), BF16), pltpu.SemaphoreType.DMA((3,))],
        0,
        3,
    )
    arrived = swap_core(give)
    return call(
        out_kernel,
        shape(HALF, D),
        (tokens, keep, arrived, w_own, keep_near(w_other), stay(cam_embed)),
        [pltpu.VMEM((8, D), F32), pltpu.SemaphoreType.DMA],
        0,
        1,
    )[None]


def solution(mesh):
    fine = Mesh(mesh.devices.reshape(4, 2, 4, 8, 2), EVERY)
    placed = (P(CAM, SLAB, None), P(), P(), P(), P(), P(SLAB, None), P(SLAB, None))
    return jax.shard_map(local, mesh=fine, in_specs=placed, out_specs=P(CAM, SLAB, None), check_vma=False)
```
